32 devices in a mesh: dp: 16 (over z, x, core), tensor: 2 (over y).
Axes of the slice: x: 2, y: 2, z: 4, core: 2. Of those that a mesh axis runs over, the one named last changes fastest.
Arguments:
- tokens: bfloat16 [32768, 1024], P(('dp', 'tensor')), may hold values from -6 to 6
- lengths: int32 [16, 4], P('dp'), may hold values from 64 to 1280, as said below
- attn_gain: float32 [1024], replicated, may hold values from 0.1 to 1.9
- w_query: bfloat16 [1024, 1024], P(None, 'tensor'), may hold values from -0.375 to 0.375
- w_kv: bfloat16 [1024, 256], P(None, 'tensor'), may hold values from -0.1875 to 0.1875
- w_rope: bfloat16 [1024, 32], replicated, may hold values from -0.1875 to 0.1875
- w_out: bfloat16 [1024, 1024], P('tensor'), may hold values from -1 to 1
- mlp_gain: float32 [1024], replicated, may hold values from 0.1 to 1.9
- w_gate: bfloat16 [1024, 2816], P(None, 'tensor'), may hold values from -0.1875 to 0.1875
- w_up: bfloat16 [1024, 2816], P(None, 'tensor'), may hold values from -0.1875 to 0.1875
- w_down: bfloat16 [2816, 1024], P('tensor'), may hold values from -0.21875 to 0.21875
- out_grad: bfloat16 [32768, 1024], P(('dp', 'tensor')), may hold values from -6 to 6
Outputs:
- layer_out: bfloat16 [32768, 1024], P(('dp', 'tensor'))
- tokens_grad: bfloat16 [32768, 1024], P(('dp', 'tensor'))
- attn_gain_grad: float32 [1024], replicated
- w_query_grad: float32 [1024, 1024], P(None, 'tensor')
- w_kv_grad: float32 [1024, 256], P(None, 'tensor')
- w_rope_grad: float32 [1024, 32], replicated
- w_out_grad: float32 [1024, 1024], P('tensor')
- mlp_gain_grad: float32 [1024], replicated
- w_gate_grad: float32 [1024, 2816], P(None, 'tensor')
- w_up_grad: float32 [1024, 2816], P(None, 'tensor')
- w_down_grad: float32 [2816, 1024], P('tensor')
The draws below stay inside these ranges and needn't reach their ends.
Inputs may be any that keep to these rules, and one draw needn't show every extreme that they name: `lengths`: each group has one sequence of exactly 1280 tokens at a place drawn from the seed and one of exactly 64; the others have 64 to 256; the rest of the group's slots are padding.
All inputs are finite; a program needn't handle non-finite values.
Results may differ from the reference program's by a relative error of at most 0.02.
Values may be sent and summed in bfloat16 or wider, within the bound.
No kernel may reach another device: no remote copies, remote signals or barrier semaphores. Data moves between devices by JAX's collectives and lax.ppermute only.
A program may use at most 256 MiB of HBM per device.

```python
import jax
import jax.numpy as jnp
from jax import lax

D = 1024
HEADS = 16
GROUPS = 4
HD = 64
FF = 2816
NSEQ = 4
HALF = 32
LONGEST = 1280
SHORT_MOST = 256
SHORT_LEAST = 64
TOKENS = 32768
N_DP = 16


def draw_lengths(key, part):
    key = jax.random.fold_in(key, 7)
    short_key, place_key, least_key = jax.random.split(key, 3)
    shorts = jax.random.randint(short_key, (N_DP, NSEQ - 1), SHORT_LEAST, SHORT_MOST + 1)
    least_place = jax.random.randint(least_key, (N_DP, 1), 0, NSEQ - 1)
    order = jnp.arange(NSEQ - 1, dtype=jnp.int32)[None, :]
    shorts = jnp.where(order == least_place, SHORT_LEAST, shorts).astype(jnp.int32)
    place = jax.random.randint(place_key, (N_DP, 1), 0, NSEQ)
    index = jnp.arange(NSEQ, dtype=jnp.int32)[None, :]
    source = jnp.clip(index - (index > place).astype(jnp.int32), 0, NSEQ - 2)
    picked = jnp.take_along_axis(shorts, jnp.broadcast_to(source, (N_DP, NSEQ)), axis=1)
    return jnp.where(index == place, LONGEST, picked).astype(jnp.int32)


def levels(own_key, shape, cuts, smallest, top_value):
    def one(dim, parts):
        steps = jax.random.uniform(jax.random.fold_in(jax.random.fold_in(own_key, 6), dim), (parts,), jnp.float32, smallest / len(cuts), top_value / len(cuts))
        return jnp.repeat(jnp.exp(steps), shape[dim] // parts).reshape((-1,) + (1,) * (len(shape) - dim - 1))

    loudness = one(*cuts[0])
    for cut in cuts[1:]:
        loudness = loudness * one(*cut)
    return loudness


def normal_values(own_key, dims, deviation, bound, cuts=(), held_as=jnp.bfloat16):
    drawn = deviation * jax.random.normal(own_key, dims, jnp.float32)
    if cuts:
        drawn = drawn * levels(own_key, dims, cuts, -0.22, 0.18)
    return jnp.clip(drawn, -bound, bound).astype(held_as)


def setup_inputs(seed: int = 0) -> dict:
    keys = jax.random.split(jax.random.key(seed), 13)
    tokens = normal_values(keys[0], (TOKENS, D), 1.0, 6.0, ((0, 32),))
    lengths = draw_lengths(jax.random.fold_in(keys[12], 71), 0)
    attn_gain = jnp.clip(1.0 + 0.18 * jax.random.normal(keys[2], (D,), jnp.float32), 0.1, 1.9)
    w_query = normal_values(keys[3], (D, HEADS * HD), (D // 4) ** -0.5, 0.375, ((1, 2),))
    w_kv = normal_values(keys[4], (D, GROUPS * HD), D ** -0.5, 0.1875, ((1, 2),))
    w_rope = normal_values(keys[5], (D, HALF), D ** -0.5, 0.1875)
    w_out = normal_values(keys[6], (HEADS * HD, D), (D // 32) ** -0.5, 1.0, ((0, 2),))
    mlp_gain = jnp.clip(1.0 + 0.18 * jax.random.normal(keys[7], (D,), jnp.float32), 0.1, 1.9)
    w_gate = normal_values(keys[8], (D, FF), D ** -0.5, 0.1875, ((1, 2),))
    w_up = normal_values(keys[9], (D, FF), D ** -0.5, 0.1875, ((1, 2),))
    w_down = normal_values(keys[10], (FF, D), (FF // 4) ** -0.5, 0.21875, ((0, 2),))
    out_grad = normal_values(keys[11], (TOKENS, D), 1.0, 6.0, ((0, 32),))
    return {"tokens": tokens, "lengths": lengths, "attn_gain": attn_gain, "w_query": w_query, "w_kv": w_kv, "w_rope": w_rope, "w_out": w_out, "mlp_gain": mlp_gain, "w_gate": w_gate, "w_up": w_up, "w_down": w_down, "out_grad": out_grad}


eps_norm = 1e-05
masked_score = -1e+30
highest = lax.Precision.HIGHEST

@jax.custom_vjp
def low(v):
    return lax.optimization_barrier(v.astype(jnp.bfloat16)).astype(jnp.float32)

@jax.custom_vjp
def low_back(v):
    return v

def low_keep(v):
    return (low(v), None)

def low_pass(kept, grad):
    return (grad,)

def back_keep(v):
    return (v, None)

def back_low(kept, grad):
    return (low(grad),)
low.defvjp(low_keep, low_pass)
low_back.defvjp(back_keep, back_low)

def layout(lengths_row, slots):
    slot = jnp.arange(slots, dtype=jnp.int32)
    ends = jnp.cumsum(lengths_row).astype(jnp.int32)
    passed = (slot[:, None] >= ends[None, :]).astype(jnp.int32)
    segment = lax.optimization_barrier(jnp.sum(passed, axis=1)).astype(jnp.int32)
    begin = lax.optimization_barrier(jnp.sum(passed * lengths_row[None, :], axis=1)).astype(jnp.int32)
    valid = (segment < lengths_row.shape[0]).astype(jnp.float32)
    return (slot, segment, (slot - begin).astype(jnp.float32), valid)

def angles(position, width):
    half = width // 2
    freq = 10000.0 ** (-jnp.arange(half, dtype=jnp.float32) / half)
    angle = position[:, None] * freq[None, :]
    return (jnp.cos(angle), jnp.sin(angle))

def rotate(values, cosine, sine):
    half = values.shape[-1] // 2
    first = values[..., :half]
    second = values[..., half:]
    return jnp.concatenate([first * cosine - second * sine, first * sine + second * cosine], axis=-1)

def rms_scale(values, gain):
    return values * lax.rsqrt(lax.optimization_barrier(jnp.mean(values * values, axis=-1, keepdims=True)) + eps_norm) * gain

def matmul(left, right):
    return jnp.dot(left, right, precision=highest)

def block_attention(query_block, rows_block, seg_block, key, value, slot, segment):
    scores = jnp.einsum('bgjd,kgd->gjbk', query_block, key, precision=highest) * query_block.shape[-1] ** (-0.5)
    allowed = (seg_block[:, None] == segment[None, :]) & (slot[None, :] <= rows_block[:, None])
    scores = low_back(jnp.where(allowed, scores, masked_score))
    top = lax.optimization_barrier(jnp.max(scores, axis=-1, keepdims=True))
    weights = jnp.exp(scores - top)
    weights = weights / lax.optimization_barrier(jnp.sum(weights, axis=-1, keepdims=True))
    return jnp.einsum('gjbk,kgd->bgjd', low(weights), value, precision=highest)

def group_forward(tokens_group, lengths_row, attn_gain, w_query, w_kv, w_rope, w_out, mlp_gain, w_gate, w_up, w_down):
    slots = tokens_group.shape[0]
    slot, segment, position, valid = layout(lengths_row, slots)
    cosine, sine = angles(position, HALF)
    first_in = low(rms_scale(tokens_group, attn_gain))
    query = low_back(matmul(first_in, w_query)).reshape(slots, GROUPS, HEADS // GROUPS, HD)
    query = low(jnp.concatenate([query[..., :HALF], rotate(query[..., HALF:], cosine[:, None, None, :], sine[:, None, None, :])], axis=-1))
    shared = low(rotate(matmul(first_in, w_rope), cosine, sine))
    tied = low(low_back(matmul(first_in, w_kv))).reshape(slots, GROUPS, HD)
    key = jnp.concatenate([tied[..., :HALF], jnp.broadcast_to(shared[:, None, :], (slots, GROUPS, HALF))], axis=-1)
    block = min(512, slots)
    blocks = slots // block

    def one_block(items):
        return block_attention(items[0], items[1], items[2], key, tied, slot, segment)
    mixed = lax.map(jax.checkpoint(one_block), (query.reshape(blocks, block, GROUPS, HEADS // GROUPS, HD), slot.reshape(blocks, block), segment.reshape(blocks, block)))
    mixed = mixed.reshape(slots, HEADS * HD) * valid[:, None]
    mixed = low_back(low(mixed))
    middle = tokens_group + low_back(matmul(mixed, w_out))
    second_in = low(rms_scale(middle, mlp_gain))
    gate = low_back(matmul(second_in, w_gate))
    upward = low_back(matmul(second_in, w_up))
    hidden = low(jax.nn.silu(gate) * upward)
    return middle + low_back(matmul(hidden, w_down))

def reference(tokens, lengths, attn_gain, w_query, w_kv, w_rope, w_out, mlp_gain, w_gate, w_up, w_down, out_grad):
    params = tuple((weight.astype(jnp.float32) for weight in (attn_gain, w_query, w_kv, w_rope, w_out, mlp_gain, w_gate, w_up, w_down)))
    groups = lengths.shape[0]
    inputs = tokens.astype(jnp.float32).reshape(groups, -1, tokens.shape[1])
    cotangents = out_grad.astype(jnp.float32).reshape(groups, -1, tokens.shape[1])

    def visit(totals, items):
        tokens_group, lengths_row, cot_group = items

        def forward(values, *weights):
            return group_forward(values, lengths_row, *weights)
        result, pullback = jax.vjp(forward, tokens_group, *params)
        grads = pullback(cot_group)
        summed = tuple((total + grad for total, grad in zip(totals, grads[1:])))
        return (summed, (result.astype(jnp.bfloat16), grads[0].astype(jnp.bfloat16)))
    zeros = tuple((jnp.zeros_like(weight) for weight in params))
    totals, (results, backward) = lax.scan(visit, zeros, (inputs, lengths, cotangents))
    return (results.reshape(tokens.shape), backward.reshape(tokens.shape), totals[0], totals[1], totals[2], totals[3], totals[4], totals[5], totals[6], totals[7], totals[8])
```

```python
import functools

import jax
import jax.numpy as jnp
from jax import lax
from jax.experimental import pallas as pl
from jax.experimental.pallas import tpu as pltpu
from jax.sharding import PartitionSpec as P

eps_norm = 1e-05
masked_score = -1e30
f32 = jnp.float32
bf16 = jnp.bfloat16


def dot(a,b): return lax.dot_general(a,b,(((1,),(0,)),((),())),preferred_element_type=f32)
def dot_nt(a,b): return lax.dot_general(a,b,(((1,),(1,)),((),())),preferred_element_type=f32)

def block_loops(bounds, i, step):
    k0,k1,k2,k3 = (bounds[i, n] for n in range(4))
    lax.fori_loop(k0,k1,lambda kb,c: step(kb,True),None)
    lax.fori_loop(k1,k2,lambda kb,c: step(kb,False),None)
    lax.fori_loop(k2,k3,lambda kb,c: step(kb,True),None)

def allowed_tile(start, kb, bk, qpos):
    kk = lax.broadcasted_iota(jnp.int32,(bk,start.shape[1]),0)+kb*bk
    return (kk>=start)&(kk<=qpos)

def fwd_kernel(own0, heads, hd, bk, bounds, start_ref, q_ref, tied_ref, shared_ref, o_ref, lse_ref, ks, acc, ms, ls):
    i = pl.program_id(1)
    half = hd//2
    bq = q_ref.shape[2]
    @pl.when(i==0)
    def _():
        kT = jnp.concatenate([tied_ref[0,:half,:], shared_ref[...]],axis=0)
        ks[...] = kT.T
    acc[...] = jnp.zeros_like(acc)
    ms[...] = jnp.full_like(ms, masked_score)
    ls[...] = jnp.zeros_like(ls)
    start = start_ref[...]
    qpos = own0 + i*bq + lax.broadcasted_iota(jnp.int32,(1,bq),1)
    def step(kb, masked):
        rows = pl.ds(pl.multiple_of(kb*bk,bk),bk)
        kblk = ks[rows,:]
        vT = tied_ref[0,:,rows]
        if masked: ok = allowed_tile(start,kb,bk,qpos)
        mold = [ms[j:j+1,:] for j in range(heads)]
        lold = [ls[j:j+1,:] for j in range(heads)]
        aold = [acc[j*hd:(j+1)*hd,:] for j in range(heads)]
        ss = [dot(kblk, q_ref[0,j*hd:(j+1)*hd,:]) for j in range(heads)]
        if masked: ss = [jnp.where(ok,s,masked_score) for s in ss]
        mnew = [jnp.maximum(m,jnp.max(s,axis=0,keepdims=True)) for m,s in zip(mold,ss)]
        ps = [jnp.exp(s-m) for s,m in zip(ss,mnew)]
        als = [jnp.exp(a-b) for a,b in zip(mold,mnew)]
        lnew = [l*al+jnp.sum(p,axis=0,keepdims=True) for l,al,p in zip(lold,als,ps)]
        anew = [a*al+dot(vT,p.astype(bf16)) for a,al,p in zip(aold,als,ps)]
        for j in range(heads):
            ms[j:j+1,:]=mnew[j]; ls[j:j+1,:]=lnew[j]; acc[j*hd:(j+1)*hd,:]=anew[j]
    block_loops(bounds,i,step)
    live = start < (1<<29)
    for j in range(heads):
        l = ls[j:j+1,:]
        safe = jnp.where(l>0,l,1.0)
        o_ref[0,j*hd:(j+1)*hd,:] = jnp.where(live,acc[j*hd:(j+1)*hd,:]/safe,0.0).astype(bf16)
        lse_ref[0,j:j+1,:] = ms[j:j+1,:]+jnp.log(safe)

def attn_fwd(bounds,start,qT,tied,shared,own0,bq,bk):
    G,W,rows = qT.shape
    hd = tied.shape[1]; heads = W//hd; slots = tied.shape[2]
    grid=(G,rows//bq)
    return pl.pallas_call(
        functools.partial(fwd_kernel,own0,heads,hd,bk),
        grid_spec=pltpu.PrefetchScalarGridSpec(
            num_scalar_prefetch=1, grid=grid,
            in_specs=[
                pl.BlockSpec((1,bq),lambda g,i,b:(0,i)),
                pl.BlockSpec((1,W,bq),lambda g,i,b:(g,0,i)),
                pl.BlockSpec((1,hd,slots),lambda g,i,b:(g,0,0)),
                pl.BlockSpec((hd//2,slots),lambda g,i,b:(0,0)),
            ],
            out_specs=[
                pl.BlockSpec((1,W,bq),lambda g,i,b:(g,0,i)),
                pl.BlockSpec((1,heads,bq),lambda g,i,b:(g,0,i)),
            ],
            scratch_shapes=[pltpu.VMEM((slots,hd),bf16),pltpu.VMEM((W,bq),f32),pltpu.VMEM((8,bq),f32),pltpu.VMEM((8,bq),f32)],
        ),
        out_shape=[jax.ShapeDtypeStruct((G,W,rows),bf16),jax.ShapeDtypeStruct((G,heads,rows),f32)],
        compiler_params=pltpu.CompilerParams(vmem_limit_bytes=48<<20),
        name="attn_fwd",
    )(bounds,start,qT,tied,shared)

def bwd_kernel(own0, heads, hd, bk, scale, bounds, start_ref, q_ref, tied_ref, shared_ref, o_ref, lse_ref, do_ref, cos_ref, sin_ref,
               dq_ref, tg_ref, sg_ref, ks, kTs, vs, dk, dv, dqa, dl):
    g = pl.program_id(0); i = pl.program_id(1)
    half = hd//2; quarter=hd//4
    bq = q_ref.shape[2]
    @pl.when(i==0)
    def _():
        kT = jnp.concatenate([tied_ref[0,:half,:], shared_ref[...]],axis=0)
        kTs[...] = kT
        ks[...] = kT.T
        vs[...] = tied_ref[0].T
        dk[...] = jnp.zeros_like(dk)
        dv[...] = jnp.zeros_like(dv)
    @pl.when((i==0)&(g==0))
    def _():
        sg_ref[...] = jnp.zeros_like(sg_ref)
    dqa[...] = jnp.zeros_like(dqa)
    for j in range(heads):
        prod = do_ref[0,j*hd:(j+1)*hd,:].astype(f32)*o_ref[0,j*hd:(j+1)*hd,:].astype(f32)
        dl[j:j+1,:] = jnp.sum(prod,axis=0,keepdims=True)
    start = start_ref[...]
    qpos = own0 + i*bq + lax.broadcasted_iota(jnp.int32,(1,bq),1)
    def step(kb, masked):
        rows = pl.ds(pl.multiple_of(kb*bk,bk),bk)
        kblk = ks[rows,:]
        vblk = vs[rows,:]
        kT = kTs[:,rows]
        if masked: ok = allowed_tile(start,kb,bk,qpos)
        dvt = dv[:,rows]; dkt = dk[:,rows]
        sls=[slice(j*hd,(j+1)*hd) for j in range(heads)]
        qs=[q_ref[0,sl,:] for sl in sls]; dos=[do_ref[0,sl,:] for sl in sls]
        lses=[lse_ref[0,j:j+1,:] for j in range(heads)]; dls=[dl[j:j+1,:] for j in range(heads)]
        dqs=[dqa[sl,:] for sl in sls]
        new=[]
        for j in range(heads):
            s = dot(kblk, qs[j])
            if masked: s = jnp.where(ok,s,masked_score)
            p = jnp.exp(s-lses[j])
            dp = dot(vblk, dos[j])
            ds = (p*(dp-dls[j])).astype(bf16)
            dvt = dvt + dot_nt(dos[j], p.astype(bf16))
            dkt = dkt + dot_nt(qs[j], ds)
            new.append(dqs[j]+dot(kT,ds))
        for sl,n in zip(sls,new): dqa[sl,:]=n
        dv[:,rows] = dvt
        dk[:,rows] = dkt
    block_loops(bounds,i,step)
    cosv=cos_ref[...]; sinv=sin_ref[...]
    for j in range(heads):
        b0=j*hd
        x = dqa[b0:b0+hd,:]*scale
        a = x[half:half+quarter]; b=x[half+quarter:]
        dq_ref[0,b0:b0+hd,:] = jnp.concatenate([x[:half],a*cosv+b*sinv,b*cosv-a*sinv],axis=0).astype(bf16)
    @pl.when(i==pl.num_programs(1)-1)
    def _():
        tg_ref[0,:half,:] = dv[:half,:]+dk[:half,:]
        tg_ref[0,half:,:] = dv[half:,:]
        sg_ref[...] += dk[half:,:]

def attn_bwd(bounds,start,qT,tied,shared,oT,lse,doT,cosT,sinT,own0,bq,bk):
    G,W,rows = qT.shape
    hd = tied.shape[1]; heads = W//hd; slots = tied.shape[2]
    grid=(G,rows//bq)
    tile=pl.BlockSpec((1,W,bq),lambda g,i,b:(g,0,i))
    ang=pl.BlockSpec((hd//4,bq),lambda g,i,b:(0,i))
    return pl.pallas_call(
        functools.partial(bwd_kernel,own0,heads,hd,bk,hd**-0.5),
        grid_spec=pltpu.PrefetchScalarGridSpec(
            num_scalar_prefetch=1, grid=grid,
            in_specs=[
                pl.BlockSpec((1,bq),lambda g,i,b:(0,i)),
                tile,
                pl.BlockSpec((1,hd,slots),lambda g,i,b:(g,0,0)),
                pl.BlockSpec((hd//2,slots),lambda g,i,b:(0,0)),
                tile,
                pl.BlockSpec((1,heads,bq),lambda g,i,b:(g,0,i)),
                tile, ang, ang,
            ],
            out_specs=[
                tile,
                pl.BlockSpec((1,hd,slots),lambda g,i,b:(g,0,0)),
                pl.BlockSpec((hd//2,slots),lambda g,i,b:(0,0)),
            ],
            scratch_shapes=[pltpu.VMEM((slots,hd),bf16),pltpu.VMEM((hd,slots),bf16),pltpu.VMEM((slots,hd),bf16),
                pltpu.VMEM((hd,slots),f32),pltpu.VMEM((hd,slots),f32),pltpu.VMEM((W,bq),f32),pltpu.VMEM((8,bq),f32)],
        ),
        out_shape=[jax.ShapeDtypeStruct((G,W,rows),bf16),jax.ShapeDtypeStruct((G,hd,slots),f32),jax.ShapeDtypeStruct((hd//2,slots),f32)],
        compiler_params=pltpu.CompilerParams(vmem_limit_bytes=48<<20),
        name="attn_bwd",
    )(bounds,start,qT,tied,shared,oT,lse,doT,cosT,sinT)

def local_layout(lengths_row, t, rows, bq, bk, own0):
    slot = t*rows + jnp.arange(rows,dtype=jnp.int32)
    ends = jnp.cumsum(lengths_row)
    passed = (slot[:,None]>=ends[None,:]).astype(jnp.int32)
    begin = jnp.sum(passed*lengths_row[None,:],axis=1)
    total = ends[-1]
    valid = slot < total
    shift = own0 - t*rows
    start = jnp.where(valid, begin+shift, 1<<30)
    nqb = rows//bq
    first = begin.reshape(nqb,bq)[:,0]+shift
    lastvalid = jnp.max(jnp.where(valid,begin+shift,0).reshape(nqb,bq),axis=1)
    anyvalid = valid.reshape(nqb,bq)[:,0]
    allvalid = valid.reshape(nqb,bq)[:,-1]
    q0 = own0+jnp.arange(nqb,dtype=jnp.int32)*bq
    k0 = first//bk
    k3 = (q0+bq-1)//bk+1
    k1 = jnp.minimum((lastvalid+bk-1)//bk, k3)
    k2 = jnp.maximum((q0+1)//bk, k1)
    k1 = jnp.where(allvalid,k1,k3); k2=jnp.where(allvalid,k2,k3)
    k0 = jnp.where(anyvalid,k0,0); k1=jnp.where(anyvalid,k1,0); k2=jnp.where(anyvalid,k2,0); k3=jnp.where(anyvalid,k3,0)
    bounds = jnp.stack([k0,k1,k2,k3],axis=1).astype(jnp.int32)
    return slot, (slot-begin).astype(f32), valid, start[None,:], bounds


def rms_parts(values):
    factor = lax.rsqrt(jnp.mean(values * values, axis=-1, keepdims=True) + eps_norm)
    return values * factor, factor


def norm_back(grad, normed, factor, gain):
    inner = grad * gain
    return factor * (inner - normed * jnp.mean(inner * normed, axis=-1, keepdims=True))


def mm(a, b, ca, cb):
    return lax.dot_general(a, b, (((ca,), (cb,)), ((), ())), preferred_element_type=f32)


def rot_T(x, cosT, sinT):
    n = x.shape[-2] // 2
    a, b = x[..., :n, :], x[..., n:, :]
    return jnp.concatenate([a * cosT - b * sinT, a * sinT + b * cosT], axis=-2)


def swap(x, axis, bit):
    n = lax.axis_size(axis)
    return lax.ppermute(x, axis, [(i, i ^ bit) for i in range(n)])


def halves(x, bit):
    n = x.shape[0] // 2
    keep = lax.dynamic_slice_in_dim(x, bit * n, n, 0)
    send = lax.dynamic_slice_in_dim(x, (1 - bit) * n, n, 0)
    return keep, send


def joined(mine, other, bit):
    first = bit == 0
    return jnp.concatenate([jnp.where(first, mine, other), jnp.where(first, other, mine)], axis=0)


def fetch_other(w, core):
    n = w.shape[0] // 2
    piece = lax.dynamic_slice_in_dim(w, core * n, n, 0)
    got = swap(piece, "tensor", 1)
    return joined(got, swap(got, "dp", 1), core)


def add(a, b):
    return (a.astype(f32) + b.astype(f32)).astype(bf16)


def reduce_half(own, other, index):
    size = lax.axis_size("dp")
    bit = index & 1
    keep, send = halves(other, bit)
    theirs = add(keep, swap(send, "dp", 1))
    keep, send = halves(own, bit)
    mine = keep.astype(f32) + swap(send, "dp", 1).astype(f32)
    mine = (mine + swap(theirs, "tensor", 1).astype(f32)).astype(bf16)
    split = [1]
    step = 2
    while step < size:
        b = (index // step) & 1
        if mine.shape[0] % 32 == 0 or mine.shape[0] > 64:
            keep, send = halves(mine, b)
            mine = add(keep, swap(send, "dp", step))
            split.append(step)
        else:
            mine = add(mine, swap(mine, "dp", step))
        step *= 2
    for step in reversed(split):
        mine = joined(mine, swap(mine, "dp", step), (index // step) & 1)
    return mine.astype(f32)


def body(tokens, lengths, attn_gain, w_query, w_kv, w_rope, w_out, mlp_gain, w_gate, w_up, w_down, out_grad):
    rows, width = tokens.shape
    shards = lax.axis_size("tensor")
    t = lax.axis_index("tensor")
    index = lax.axis_index("dp")
    core = index & 1
    half = w_rope.shape[1]
    hd = 2 * half
    quarter = half // 2
    kv_own = w_kv.shape[1]
    q_own = w_query.shape[1]
    groups = 2 * kv_own // hd
    per = q_own // kv_own
    own0 = rows
    bq_f, bk_f, bq_b, bk_b = 256, 512, 512, 256

    slot, position, valid, start, bounds_f = local_layout(lengths[0], t, rows, bq_f, bk_f, own0)
    bounds_b = local_layout(lengths[0], t, rows, bq_b, bk_b, own0)[4]
    freq = 10000.0 ** (-jnp.arange(quarter, dtype=f32) / quarter)
    angle = freq[:, None] * position[None, :]
    cosT, sinT = jnp.cos(angle), jnp.sin(angle)

    w_kv_o = fetch_other(w_kv, core)
    w_query_o = fetch_other(w_query, core)
    w_out_o = fetch_other(w_out, core)
    w_gate_o = fetch_other(w_gate, core)
    w_up_o = fetch_other(w_up, core)
    w_down_o = fetch_other(w_down, core)

    inputs = tokens.astype(f32)
    normed_one, factor_one = rms_parts(inputs)
    first_in = (normed_one * attn_gain).astype(bf16)

    shared = rot_T(mm(w_rope, first_in, 0, 1), cosT, sinT).astype(bf16)
    tied = jnp.concatenate([mm(w_kv, first_in, 0, 1), mm(w_kv_o, first_in, 0, 1)], axis=0).astype(bf16)
    sent = jnp.concatenate([tied, shared], axis=0)
    got = lax.ppermute(sent, "tensor", [(i, i + 1) for i in range(shards - 1)])
    tied_all = jnp.concatenate(
        [jnp.concatenate([got[kv_own : 2 * kv_own], got[:kv_own]], axis=0), tied], axis=1
    ).reshape(groups, hd, 2 * rows)
    shared_all = jnp.concatenate([got[2 * kv_own :], shared], axis=1)

    def queries(w):
        raw = mm(w, first_in, 0, 1).reshape(-1, hd, rows)
        turned = jnp.concatenate([raw[:, :half], rot_T(raw[:, half:], cosT, sinT)], axis=1)
        return (turned.astype(bf16) * bf16(hd**-0.5)).reshape(-1, per * hd, rows)

    q = jnp.concatenate([queries(w_query), queries(w_query_o)], axis=0)
    mixed, lse = attn_fwd(bounds_f, start, q, tied_all, shared_all, own0, bq_f, bk_f)
    mixed_t = mixed.reshape(-1, rows)
    w_out_all = jnp.concatenate([w_out, w_out_o], axis=0)
    middle = inputs + mm(mixed_t, w_out_all, 0, 0)
    normed_two, factor_two = rms_parts(middle)
    second_in = (normed_two * mlp_gain).astype(bf16)

    def mlp(wg, wu, wd):
        gate = mm(second_in, wg, 1, 0)
        up = mm(second_in, wu, 1, 0)
        sig = jax.nn.sigmoid(gate)
        hidden = (gate * sig * up).astype(bf16)
        out = mm(hidden, wd, 1, 0)
        hidden_grad = mm(out_grad, wd, 1, 1)
        gate_grad = (hidden_grad * up * sig * (1.0 + gate * (1.0 - sig))).astype(bf16)
        up_grad = (hidden_grad * gate * sig).astype(bf16)
        wd_grad = mm(hidden, out_grad, 0, 0).astype(bf16)
        wg_grad = mm(second_in, gate_grad, 0, 0).astype(bf16)
        wu_grad = mm(second_in, up_grad, 0, 0).astype(bf16)
        second_grad = mm(gate_grad, wg, 1, 1) + mm(up_grad, wu, 1, 1)
        return out, second_grad, (wg_grad, wu_grad, wd_grad)

    out_b, second_b, grads_b = mlp(w_gate_o, w_up_o, w_down_o)
    out_a, second_a, grads_a = mlp(w_gate, w_up, w_down)
    layer_out = (middle + out_a + out_b).astype(bf16)
    second_grad = second_a + second_b
    mlp_gain_part = jnp.sum(second_grad * normed_two, axis=0)
    middle_grad = out_grad.astype(f32) + norm_back(second_grad, normed_two, factor_two, mlp_gain)
    attn_back = middle_grad.astype(bf16)
    w_out_grad = mm(mixed_t, attn_back, 1, 0).astype(bf16)
    mixed_grad = (mm(w_out_all, attn_back, 1, 1).astype(bf16) * valid[None, :].astype(bf16)).reshape(mixed.shape)

    dq, tied_grad, shared_grad = attn_bwd(
        bounds_b, start, q, tied_all, shared_all, mixed, lse, mixed_grad, cosT, sinT, own0, bq_b, bk_b
    )
    tied_grad = tied_grad.reshape(2 * kv_own, 2 * rows)
    back = jnp.concatenate([tied_grad[:, :rows], shared_grad[:, :rows]], axis=0).astype(bf16)
    back = lax.ppermute(back, "tensor", [(i + 1, i) for i in range(shards - 1)]).astype(f32)
    tied_own = tied_grad[:, rows:] + jnp.concatenate([back[kv_own : 2 * kv_own], back[:kv_own]], axis=0)
    shared_own = rot_T(shared_grad[:, rows:] + back[2 * kv_own :], cosT, -sinT)
    grads_in = jnp.concatenate([dq.reshape(-1, rows), tied_own.astype(bf16), shared_own.astype(bf16)], axis=0)
    weights_in = jnp.concatenate([w_query, w_query_o, w_kv, w_kv_o, w_rope], axis=1)
    first_grad = mm(grads_in, weights_in, 0, 1)
    in_grads = mm(first_in, grads_in, 0, 1).astype(bf16)
    attn_gain_part = jnp.sum(first_grad * normed_one, axis=0)
    tokens_grad = (middle_grad + norm_back(first_grad, normed_one, factor_one, attn_gain)).astype(bf16)

    gate_sum = reduce_half(grads_a[0], grads_b[0], index)
    up_sum = reduce_half(grads_a[1], grads_b[1], index)
    down_sum = reduce_half(grads_a[2], grads_b[2], index)
    out_sum = reduce_half(w_out_grad[:q_own], w_out_grad[q_own:], index)
    small = jnp.concatenate(
        [in_grads[:, 2 * (q_own + kv_own) :], attn_gain_part[:, None].astype(bf16), mlp_gain_part[:, None].astype(bf16)],
        axis=1,
    )
    q2 = 2 * q_own
    tail = reduce_half(
        jnp.concatenate([in_grads[:, :q_own], in_grads[:, q2 : q2 + kv_own], small], axis=1),
        jnp.concatenate([in_grads[:, q_own:q2], in_grads[:, q2 + kv_own : q2 + 2 * kv_own], small], axis=1),
        index,
    )
    k0 = q_own + kv_own
    return (
        layer_out,
        tokens_grad,
        tail[:, k0 + half],
        tail[:, :q_own],
        tail[:, q_own:k0],
        tail[:, k0 : k0 + half],
        out_sum,
        tail[:, k0 + half + 1],
        gate_sum,
        up_sum,
        down_sum,
    )


def solution(mesh):
    rows = P(("dp", "tensor"), None)
    columns = P(None, "tensor")
    down = P("tensor", None)
    return jax.shard_map(
        body,
        mesh=mesh,
        in_specs=(rows, P("dp", None), P(), columns, columns, P(), down, P(), columns, columns, down, rows),
        out_specs=(rows, rows, P(), columns, columns, P(), down, P(), columns, columns, down),
        check_vma=False,
    )
```

```python
import functools

import jax
import jax.numpy as jnp
from jax import lax
from jax.experimental import pallas as pl
from jax.experimental.pallas import tpu as pltpu
from jax.sharding import PartitionSpec as P

eps_norm = 1e-05
masked_score = -1e30
f32 = jnp.float32
bf16 = jnp.bfloat16


def dot(a, b):
    return lax.dot_general(a, b, (((1,), (0,)), ((), ())), preferred_element_type=f32)


def dot_nt(a, b):
    return lax.dot_general(a, b, (((1,), (1,)), ((), ())), preferred_element_type=f32)


ANY = pl.BlockSpec(memory_space=pl.ANY)


def vmem(mib):
    return pltpu.CompilerParams(vmem_limit_bytes=mib << 20)


def block_loops(bounds, i, step):
    k0, k1, k2, k3 = (bounds[i, n] for n in range(4))
    lax.fori_loop(k0, k1, lambda kb, c: step(kb, True), None)
    lax.fori_loop(k1, k2, lambda kb, c: step(kb, False), None)
    lax.fori_loop(k2, k3, lambda kb, c: step(kb, True), None)


def allowed_tile(start, kb, bk, qpos):
    kk = lax.broadcasted_iota(jnp.int32, (bk, start.shape[1]), 0) + kb * bk
    return (kk >= start) & (kk <= qpos)


def load_keys(refs, kT, vT):
    got_ref, sent_ref, got_shared, sent_shared = refs
    rows = sent_ref.shape[1]
    half = sent_shared.shape[0]
    for side, (tied, shared) in enumerate(((got_ref, got_shared), (sent_ref, sent_shared))):
        at = slice(side * rows, (side + 1) * rows)
        vT[:, at] = tied[...]
        kT[:half, at] = tied[:half, :]
        kT[half:, at] = shared[...]


def fwd_kernel(heads, bk, deps, bounds, start_ref, q_ref, *refs):
    kv_refs, refs = refs[:4], refs[4 + deps :]
    o_ref, lse_ref, kT, vT, ks, acc, ms, ls = refs
    i = pl.program_id(1)
    hd = kT.shape[0]
    bq = q_ref.shape[2]
    own0 = kT.shape[1] // 2

    @pl.when(i == 0)
    def _():
        load_keys(kv_refs, kT, vT)
        ks[...] = kT[...].T

    acc[...] = jnp.zeros_like(acc)
    ms[...] = jnp.full_like(ms, masked_score)
    ls[...] = jnp.zeros_like(ls)
    start = start_ref[...]
    qpos = own0 + i * bq + lax.broadcasted_iota(jnp.int32, (1, bq), 1)

    def step(kb, masked):
        rows = pl.ds(pl.multiple_of(kb * bk, bk), bk)
        kblk = ks[rows, :]
        vblk = vT[:, rows]
        mold = [ms[j : j + 1, :] for j in range(heads)]
        lold = [ls[j : j + 1, :] for j in range(heads)]
        aold = [acc[j * hd : (j + 1) * hd, :] for j in range(heads)]
        ss = [dot(kblk, q_ref[0, j * hd : (j + 1) * hd, :]) for j in range(heads)]
        if masked:
            ok = allowed_tile(start, kb, bk, qpos)
            ss = [jnp.where(ok, s, masked_score) for s in ss]
        mnew = [jnp.maximum(m, jnp.max(s, axis=0, keepdims=True)) for m, s in zip(mold, ss)]
        ps = [jnp.exp(s - m) for s, m in zip(ss, mnew)]
        als = [jnp.exp(a - b) for a, b in zip(mold, mnew)]
        lnew = [l * al + jnp.sum(p, axis=0, keepdims=True) for l, al, p in zip(lold, als, ps)]
        anew = [a * al + dot(vblk, p.astype(bf16)) for a, al, p in zip(aold, als, ps)]
        for j in range(heads):
            ms[j : j + 1, :] = mnew[j]
            ls[j : j + 1, :] = lnew[j]
            acc[j * hd : (j + 1) * hd, :] = anew[j]

    block_loops(bounds, i, step)
    live = start < (1 << 29)
    for j in range(heads):
        l = ls[j : j + 1, :]
        safe = jnp.where(l > 0, l, 1.0)
        o_ref[0, j * hd : (j + 1) * hd, :] = jnp.where(live, acc[j * hd : (j + 1) * hd, :] / safe, 0.0).astype(bf16)
        lse_ref[0, j : j + 1, :] = ms[j : j + 1, :] + jnp.log(safe)


def kv_specs(hd, rows, slot_sent, slot_got, n_groups):
    half = hd // 2
    shared_at = 2 * n_groups
    return [
        pl.BlockSpec((hd, rows), lambda g, i, b: (slot_got + g, 0)),
        pl.BlockSpec((hd, rows), lambda g, i, b: (slot_sent + g, 0)),
        pl.BlockSpec((half, rows), lambda g, i, b: (shared_at, 0)),
        pl.BlockSpec((half, rows), lambda g, i, b: (shared_at, 0)),
    ]


def attn_fwd(bounds, start, q, sent, got, hd, slots, bq, bk, deps=()):
    groups, width, rows = q.shape
    heads = width // hd
    n_groups = (sent.shape[0] - hd // 2) // hd
    tile = pl.BlockSpec((1, width, bq), lambda g, i, b: (g, 0, i))
    return pl.pallas_call(
        functools.partial(fwd_kernel, heads, bk, len(deps)),
        grid_spec=pltpu.PrefetchScalarGridSpec(
            num_scalar_prefetch=1,
            grid=(groups, rows // bq),
            in_specs=[pl.BlockSpec((1, bq), lambda g, i, b: (0, i)), tile]
            + kv_specs(hd, rows, *slots, n_groups)
            + [ANY] * len(deps),
            out_specs=[tile, pl.BlockSpec((1, heads, bq), lambda g, i, b: (g, 0, i))],
            scratch_shapes=[
                pltpu.VMEM((hd, 2 * rows), bf16),
                pltpu.VMEM((hd, 2 * rows), bf16),
                pltpu.VMEM((2 * rows, hd), bf16),
                pltpu.VMEM((width, bq), f32),
                pltpu.VMEM((8, bq), f32),
                pltpu.VMEM((8, bq), f32),
            ],
        ),
        out_shape=[jax.ShapeDtypeStruct((groups, width, rows), bf16), jax.ShapeDtypeStruct((groups, heads, rows), f32)],
        compiler_params=vmem(48),
        cost_estimate=pl.CostEstimate(
            flops=48 * groups * width * rows * rows, bytes_accessed=4 * groups * width * rows, transcendentals=0
        ),
        name="attn_fwd",
    )(bounds, start, q, got, sent, got, sent, *deps)


def bwd_kernel(heads, bk, scale, deps, bounds, start_ref, q_ref, o_ref, lse_ref, do_ref, cos_ref, sin_ref, *refs):
    kv_refs, refs = refs[:4], refs[4 + deps :]
    dq_ref, tg_ref, sg_ref, kT, vT, ks, vs, dk, dv, dqa, dl = refs
    g = pl.program_id(0)
    i = pl.program_id(1)
    hd = kT.shape[0]
    half = hd // 2
    quarter = hd // 4
    bq = q_ref.shape[2]
    own0 = kT.shape[1] // 2

    @pl.when(i == 0)
    def _():
        load_keys(kv_refs, kT, vT)
        ks[...] = kT[...].T
        vs[...] = vT[...].T
        dk[...] = jnp.zeros_like(dk)
        dv[...] = jnp.zeros_like(dv)

    @pl.when((i == 0) & (g == 0))
    def _():
        sg_ref[...] = jnp.zeros_like(sg_ref)

    dqa[...] = jnp.zeros_like(dqa)
    sls = [slice(j * hd, (j + 1) * hd) for j in range(heads)]
    for j, sl in enumerate(sls):
        prod = do_ref[0, sl, :].astype(f32) * o_ref[0, sl, :].astype(f32)
        dl[j : j + 1, :] = jnp.sum(prod, axis=0, keepdims=True)
    start = start_ref[...]
    qpos = own0 + i * bq + lax.broadcasted_iota(jnp.int32, (1, bq), 1)

    def step(kb, masked):
        rows = pl.ds(pl.multiple_of(kb * bk, bk), bk)
        kblk = ks[rows, :]
        vblk = vs[rows, :]
        kTb = kT[:, rows]
        if masked:
            ok = allowed_tile(start, kb, bk, qpos)
        dvt = dv[:, rows]
        dkt = dk[:, rows]
        qs = [q_ref[0, sl, :] for sl in sls]
        dos = [do_ref[0, sl, :] for sl in sls]
        lses = [lse_ref[0, j : j + 1, :] for j in range(heads)]
        dls = [dl[j : j + 1, :] for j in range(heads)]
        dqs = [dqa[sl, :] for sl in sls]
        new = []
        for j in range(heads):
            s = dot(kblk, qs[j])
            if masked:
                s = jnp.where(ok, s, masked_score)
            p = jnp.exp(s - lses[j])
            dp = dot(vblk, dos[j])
            ds = (p * (dp - dls[j])).astype(bf16)
            dvt = dvt + dot_nt(dos[j], p.astype(bf16))
            dkt = dkt + dot_nt(qs[j], ds)
            new.append(dqs[j] + dot(kTb, ds))
        for sl, n in zip(sls, new):
            dqa[sl, :] = n
        dv[:, rows] = dvt
        dk[:, rows] = dkt

    block_loops(bounds, i, step)
    cosv = cos_ref[...]
    sinv = sin_ref[...]
    for sl in sls:
        x = dqa[sl, :] * scale
        a, b = x[half : half + quarter], x[half + quarter :]
        turned = jnp.concatenate([x[:half], a * cosv + b * sinv, b * cosv - a * sinv], axis=0)
        dq_ref[0, sl, :] = turned.astype(bf16)

    @pl.when(i == pl.num_programs(1) - 1)
    def _():
        tg_ref[0, :half, :] = dv[:half, :] + dk[:half, :]
        tg_ref[0, half:, :] = dv[half:, :]
        sg_ref[...] += dk[half:, :]


def attn_bwd(bounds, start, q, sent, got, o, lse, do, cosT, sinT, hd, slots, first, groups, bq, bk, deps=()):
    _, width, rows = q.shape
    heads = width // hd
    n_groups = (sent.shape[0] - hd // 2) // hd
    tile = pl.BlockSpec((1, width, bq), lambda g, i, b: (first + g, 0, i))
    angle = pl.BlockSpec((hd // 4, bq), lambda g, i, b: (0, i))
    return pl.pallas_call(
        functools.partial(bwd_kernel, heads, bk, hd**-0.5, len(deps)),
        grid_spec=pltpu.PrefetchScalarGridSpec(
            num_scalar_prefetch=1,
            grid=(groups, rows // bq),
            in_specs=[
                pl.BlockSpec((1, bq), lambda g, i, b: (0, i)),
                tile,
                tile,
                pl.BlockSpec((1, heads, bq), lambda g, i, b: (first + g, 0, i)),
                tile,
                angle,
                angle,
            ]
            + kv_specs(hd, rows, slots[0] + first, slots[1] + first, n_groups)
            + [ANY] * len(deps),
            out_specs=[
                pl.BlockSpec((1, width, bq), lambda g, i, b: (g, 0, i)),
                pl.BlockSpec((1, hd, 2 * rows), lambda g, i, b: (g, 0, 0)),
                pl.BlockSpec((hd // 2, 2 * rows), lambda g, i, b: (0, 0)),
            ],
            scratch_shapes=[
                pltpu.VMEM((hd, 2 * rows), bf16),
                pltpu.VMEM((hd, 2 * rows), bf16),
                pltpu.VMEM((2 * rows, hd), bf16),
                pltpu.VMEM((2 * rows, hd), bf16),
                pltpu.VMEM((hd, 2 * rows), f32),
                pltpu.VMEM((hd, 2 * rows), f32),
                pltpu.VMEM((width, bq), f32),
                pltpu.VMEM((8, bq), f32),
            ],
        ),
        out_shape=[
            jax.ShapeDtypeStruct((groups, width, rows), bf16),
            jax.ShapeDtypeStruct((groups, hd, 2 * rows), f32),
            jax.ShapeDtypeStruct((hd // 2, 2 * rows), f32),
        ],
        compiler_params=vmem(48),
        cost_estimate=pl.CostEstimate(
            flops=90 * groups * width * rows * rows, bytes_accessed=8 * groups * width * rows, transcendentals=0
        ),
        name="attn_bwd",
    )(bounds, start, q, o, lse, do, cosT, sinT, got, sent, got, sent, *deps)


def local_layout(lengths_row, t, rows, bq, bk, own0):
    slot = t * rows + jnp.arange(rows, dtype=jnp.int32)
    ends = jnp.cumsum(lengths_row)
    passed = (slot[:, None] >= ends[None, :]).astype(jnp.int32)
    begin = jnp.sum(passed * lengths_row[None, :], axis=1)
    valid = slot < ends[-1]
    shift = own0 - t * rows
    start = jnp.where(valid, begin + shift, 1 << 30)
    nqb = rows // bq
    first = begin.reshape(nqb, bq)[:, 0] + shift
    last_start = jnp.max(jnp.where(valid, begin + shift, 0).reshape(nqb, bq), axis=1)
    any_valid = valid.reshape(nqb, bq)[:, 0]
    all_valid = valid.reshape(nqb, bq)[:, -1]
    q0 = own0 + jnp.arange(nqb, dtype=jnp.int32) * bq
    k0 = first // bk
    last = jnp.minimum(q0 + bq - 1, ends[-1] + shift - 1)
    k3 = last // bk + 1
    k1 = jnp.minimum((last_start + bk - 1) // bk, k3)
    k2 = jnp.minimum(jnp.maximum((q0 + 1) // bk, k1), k3)
    k1 = jnp.where(all_valid, k1, k3)
    k2 = jnp.where(all_valid, k2, k3)
    bounds = jnp.where(any_valid[:, None], jnp.stack([k0, k1, k2, k3], axis=1), 0).astype(jnp.int32)
    return slot, (slot - begin).astype(f32), valid, start[None, :], bounds


def turned_rows(x, cosv, sinv, n):
    a, b = x[:n], x[n:]
    return jnp.concatenate([a * cosv - b * sinv, a * sinv + b * cosv], axis=0)


def put_queries(raw, cosv, sinv, hd, out):
    half, quarter = hd // 2, hd // 4
    scale = hd**-0.5
    width = out.shape[1]
    for h in range(raw.shape[0] // hd):
        x = raw[h * hd : (h + 1) * hd]
        y = jnp.concatenate([x[:half], turned_rows(x[half:], cosv, sinv, quarter)], axis=0).astype(bf16)
        at = h * hd
        out[at // width, at % width : at % width + hd, :] = (y.astype(f32) * scale).astype(bf16)


def pre_kernel(hd, x_ref, gain_ref, wkv_ref, wr_ref, wq_ref, cos_ref, sin_ref, fin, tied, shared, q, wkvT, wrT, wqT):
    @pl.when(pl.program_id(0) == 0)
    def _():
        wkvT[...] = wkv_ref[...].T
        wrT[...] = wr_ref[...].T
        wqT[...] = wq_ref[...].T

    x = x_ref[...].astype(f32)
    normed = x * lax.rsqrt(jnp.mean(x * x, axis=-1, keepdims=True) + eps_norm)
    f = (normed * gain_ref[...]).astype(bf16)
    fin[...] = f
    cosv, sinv = cos_ref[...], sin_ref[...]
    tied[...] = dot_nt(wkvT[...], f).astype(bf16)
    shared[...] = turned_rows(dot_nt(wrT[...], f), cosv, sinv, hd // 4).astype(bf16)
    put_queries(dot_nt(wqT[...], f), cosv, sinv, hd, q)


def pre_call(x, gain, w_kv, w_rope, w_query, cosT, sinT, hd, per, bt=256):
    rows, width = x.shape
    kv, half, qn = w_kv.shape[1], w_rope.shape[1], w_query.shape[1]
    groups = kv // hd
    full = lambda a: pl.BlockSpec(a.shape, lambda i: (0, 0), pipeline_mode=pl.Buffered(1))
    return pl.pallas_call(
        functools.partial(pre_kernel, hd),
        grid=(rows // bt,),
        in_specs=[
            pl.BlockSpec((bt, width), lambda i: (i, 0)),
            pl.BlockSpec((1, width), lambda i: (0, 0)),
            full(w_kv),
            full(w_rope),
            full(w_query),
            pl.BlockSpec((hd // 4, bt), lambda i: (0, i)),
            pl.BlockSpec((hd // 4, bt), lambda i: (0, i)),
        ],
        out_specs=[
            pl.BlockSpec((bt, width), lambda i: (i, 0)),
            pl.BlockSpec((kv, bt), lambda i: (0, i)),
            pl.BlockSpec((half, bt), lambda i: (0, i)),
            pl.BlockSpec((groups, per * hd, bt), lambda i: (0, 0, i)),
        ],
        out_shape=[
            jax.ShapeDtypeStruct((rows, width), bf16),
            jax.ShapeDtypeStruct((kv, rows), bf16),
            jax.ShapeDtypeStruct((half, rows), bf16),
            jax.ShapeDtypeStruct((groups, per * hd, rows), bf16),
        ],
        scratch_shapes=[pltpu.VMEM((kv, width), bf16), pltpu.VMEM((half, width), bf16), pltpu.VMEM((qn, width), bf16)],
        compiler_params=vmem(32),
        cost_estimate=pl.CostEstimate(flops=4 * rows * width * (qn + kv + half), bytes_accessed=8 * rows * width, transcendentals=0),
        name="first_projections",
    )(x, gain[None, :], w_kv, w_rope, w_query, cosT, sinT)


def kv_kernel(place, f_ref, mine, other, tied_a, shared, sent, w_ref):
    n = mine.shape[0]
    core = place[0]
    w_ref[pl.ds(pl.multiple_of(core * n, n), n), :] = mine[...]
    w_ref[pl.ds(pl.multiple_of((1 - core) * n, n), n), :] = other[...]
    kv = tied_a.shape[0]
    sent[:kv, :] = tied_a[...]
    sent[kv : 2 * kv, :] = dot_nt(w_ref[...].T, f_ref[...]).astype(bf16)
    sent[2 * kv :, :] = shared[...]


def kv_call(place, f, mine, other, tied_a, shared):
    kv, rows = tied_a.shape
    total = 2 * kv + shared.shape[0]
    width = f.shape[1]
    full = lambda a: pl.BlockSpec(a, lambda i, p: (0, 0))
    return pl.pallas_call(
        kv_kernel,
        grid_spec=pltpu.PrefetchScalarGridSpec(
            num_scalar_prefetch=1,
            grid=(1,),
            in_specs=[full(f.shape), full(mine.shape), full(other.shape), full(tied_a.shape), full(shared.shape)],
            out_specs=[full((total, rows)), full((width, kv))],
        ),
        out_shape=[jax.ShapeDtypeStruct((total, rows), bf16), jax.ShapeDtypeStruct((width, kv), bf16)],
        compiler_params=vmem(32),
        cost_estimate=pl.CostEstimate(flops=4 * rows * width * kv, bytes_accessed=2 * rows * width, transcendentals=0),
        name="other_keys",
    )(place, f, mine, other, tied_a, shared)


def query_kernel(hd, place, f_ref, mine, other, cos_ref, sin_ref, q, w_ref, wT):
    @pl.when(pl.program_id(0) == 0)
    def _():
        n = mine.shape[0]
        core = place[0]
        w_ref[pl.ds(pl.multiple_of(core * n, n), n), :] = mine[...]
        w_ref[pl.ds(pl.multiple_of((1 - core) * n, n), n), :] = other[...]
        wT[...] = w_ref[...].T

    put_queries(dot_nt(wT[...], f_ref[...]), cos_ref[...], sin_ref[...], hd, q)


def query_call(place, f, mine, other, cosT, sinT, hd, groups, per, bt=256):
    rows, width = f.shape
    qn = mine.shape[1]
    full = lambda a: pl.BlockSpec(a, lambda i, p: (0, 0))
    return pl.pallas_call(
        functools.partial(query_kernel, hd),
        grid_spec=pltpu.PrefetchScalarGridSpec(
            num_scalar_prefetch=1,
            grid=(rows // bt,),
            in_specs=[
                pl.BlockSpec((bt, width), lambda i, p: (i, 0)),
                full(mine.shape),
                full(other.shape),
                pl.BlockSpec((hd // 4, bt), lambda i, p: (0, i)),
                pl.BlockSpec((hd // 4, bt), lambda i, p: (0, i)),
            ],
            out_specs=[pl.BlockSpec((groups, per * hd, bt), lambda i, p: (0, 0, i)), full((width, qn))],
            scratch_shapes=[pltpu.VMEM((qn, width), bf16)],
        ),
        out_shape=[jax.ShapeDtypeStruct((groups, per * hd, rows), bf16), jax.ShapeDtypeStruct((width, qn), bf16)],
        compiler_params=vmem(32),
        cost_estimate=pl.CostEstimate(flops=4 * rows * width * qn, bytes_accessed=4 * rows * width, transcendentals=0),
        name="other_queries",
    )(place, f, mine, other, cosT, sinT)


def mlp_kernel(first, pieces, edge, deps, place, *refs):
    s_ref, c_ref = refs[:2]
    refs = refs[2:]
    if not first:
        sT, cT = refs[:2]; refs = refs[2:]
    if pieces:
        gs, us, dn, refs = refs[:2], refs[2:4], refs[4:6], refs[6:]
    else:
        wg_ref, wu_ref, wd_ref = refs[:3]; refs = refs[3:]
    refs = refs[deps:]
    hid, gg, ug, keep, send = refs[:5]
    refs = refs[5:]
    if first:
        sT, cT = refs[:2]; refs = refs[2:]
    if pieces:
        wg_ref, wu_ref, wd_ref = refs[:3]
    i = pl.program_id(0)
    core = place[0]
    if first:
        @pl.when(i==0)
        def _():
            sT[...] = s_ref[...].T
            cT[...] = c_ref[...].T
    if pieces:
        n4 = gs[0].shape[0]
        for k in range(2):
            at = pl.multiple_of(place[1+k]*n4, n4)
            wg_ref[pl.ds(at,n4),:] = gs[k][...]
            wu_ref[pl.ds(at,n4),:] = us[k][...]
            wd_ref[:,pl.ds(at,n4)] = dn[k][...]
    rows = s_ref.shape[0]
    width = s_ref.shape[1]
    def tile(n):
        step = rows//4
        for r in range(4):
            rs = slice(r*step,(r+1)*step)
            gate = dot(s_ref[rs,:], wg_ref[:,:n]); up = dot(s_ref[rs,:], wu_ref[:,:n])
            hg = dot_nt(c_ref[rs,:], wd_ref[:n,:])
            sig = 1.0/(1.0+jnp.exp(-gate))
            act = gate*sig
            hid[rs,:n] = (act*up).astype(bf16)
            gg[rs,:n] = (hg*up*(sig+act*(1.0-sig))).astype(bf16)
            ug[rs,:n] = (hg*act).astype(bf16)
        h = hid[:,:n]; g_ = gg[:,:n]; u_ = ug[:,:n]
        hw = width//2
        for ref, side in ((keep,core),(send,1-core)):
            at = pl.ds(pl.multiple_of(side*hw,hw),hw)
            ref[0,:,:n] = dot(sT[at,:],g_).astype(bf16)
            ref[1,:,:n] = dot(sT[at,:],u_).astype(bf16)
            ref[2,:,:n] = dot(cT[at,:],h).astype(bf16)
    bn = wg_ref.shape[1]
    if edge == bn:
        tile(bn)
    else:
        last = pl.num_programs(0)-1
        pl.when(i<last)(lambda: tile(bn))
        pl.when(i==last)(lambda: tile(edge))

def mlp_call(place, s, c, turned, weights, base, cols, bn=256, deps=()):
    rows, width = s.shape
    pieces = len(weights)==6
    first = turned is None
    tiles = -(-cols//bn)
    edge = cols-(tiles-1)*bn
    whole = pl.BlockSpec((rows,width),lambda i,p:(0,0),pipeline_mode=pl.Buffered(1))
    wholeT = pl.BlockSpec((width,rows),lambda i,p:(0,0),pipeline_mode=pl.Buffered(1))
    wholeTo = pl.BlockSpec((width,rows),lambda i,p:(0,0))
    in_specs=[whole,whole]+([] if first else [wholeT,wholeT])
    if pieces:
        n4 = weights[0].shape[0]
        in_specs += [pl.BlockSpec((n4,bn),lambda i,p:(0,base+i))]*4 + [pl.BlockSpec((bn,n4),lambda i,p:(base+i,0))]*2
    else:
        in_specs += [pl.BlockSpec((width,bn),lambda i,p:(0,base+i))]*2 + [pl.BlockSpec((bn,width),lambda i,p:(base+i,0))]
    in_specs += [ANY]*len(deps)
    act = pl.BlockSpec((rows,bn),lambda i,p:(0,i))
    part = pl.BlockSpec((3,width//2,bn),lambda i,p:(0,0,i))
    acts = jax.ShapeDtypeStruct((rows,cols),bf16)
    parts = jax.ShapeDtypeStruct((3,width//2,cols),bf16)
    tsh = jax.ShapeDtypeStruct((width,rows),bf16)
    w_specs = [pl.BlockSpec((width,bn),lambda i,p:(0,i))]*2+[pl.BlockSpec((bn,width),lambda i,p:(i,0))] if pieces else []
    w_shapes = [jax.ShapeDtypeStruct((width,cols),bf16)]*2+[jax.ShapeDtypeStruct((cols,width),bf16)] if pieces else []
    out = pl.pallas_call(
        functools.partial(mlp_kernel,first,pieces,edge,len(deps)),
        grid_spec=pltpu.PrefetchScalarGridSpec(
            num_scalar_prefetch=1, grid=(tiles,), in_specs=in_specs,
            out_specs=[act]*3+[part]*2+([wholeTo]*2 if first else [])+w_specs,
        ),
        out_shape=[acts]*3+[parts]*2+([tsh]*2 if first else [])+w_shapes,
        compiler_params=pltpu.CompilerParams(vmem_limit_bytes=56<<20),
        cost_estimate=pl.CostEstimate(flops=22*rows*width*cols,bytes_accessed=2*(4*rows*width+9*width*cols),transcendentals=rows*cols),
        name="mlp_grads",
    )(place, s, c, *(() if first else turned), *weights, *deps)
    return out


def fold_kernel(counts, sides, deps, bits, *refs):
    n = sum(counts)
    outs = refs[n * sides + deps :]
    for side, out in enumerate(outs):
        at, col = side * n, 0
        for count in counts:
            total = None
            for ref in refs[at : at + count]:
                part = ref[0].astype(f32)
                total = part if total is None else total + part
            width = total.shape[1]
            out[:, col : col + width] = total.astype(out.dtype)
            at, col = at + count, col + width


def fold(groups, bit=None, deps=()):
    groups = [[a if isinstance(a, tuple) else (a[None], 0) for a in g] for g in groups]
    flat = [a for g in groups for a in g]
    rows = flat[0][0].shape[1]
    cols = sum(g[0][0].shape[2] for g in groups)
    sides = 1 if bit is None else 2
    rows_out = rows // sides
    step = rows_out
    while step % 32 == 0 and step * cols > 128 * 1408:
        step //= 2
    blocks = rows_out // step

    def spec(a, k, side):
        shape = (1, step, a.shape[2])
        if sides == 1:
            return pl.BlockSpec(shape, lambda i, b: (k, i, 0))
        if side == 0:
            return pl.BlockSpec(shape, lambda i, b: (k, b[0] * blocks + i, 0))
        return pl.BlockSpec(shape, lambda i, b: (k, (1 - b[0]) * blocks + i, 0))

    out = jax.ShapeDtypeStruct((rows_out, cols), bf16)
    scalars = jnp.reshape(jnp.int32(0) if bit is None else bit, (1,)).astype(jnp.int32)
    result = pl.pallas_call(
        functools.partial(fold_kernel, [len(g) for g in groups], sides, len(deps)),
        grid_spec=pltpu.PrefetchScalarGridSpec(
            num_scalar_prefetch=1,
            grid=(blocks,),
            in_specs=[spec(a, k, side) for side in range(sides) for a, k in flat] + [ANY] * len(deps),
            out_specs=[pl.BlockSpec((step, cols), lambda i, b: (i, 0))] * sides,
        ),
        out_shape=[out] * sides,
        compiler_params=vmem(32),
        cost_estimate=pl.CostEstimate(
            flops=3 * rows * cols, bytes_accessed=8 * rows * cols, transcendentals=0
        ),
        name="fold",
    )(scalars, *[a for _ in range(sides) for a, _ in flat], *deps)
    return result if sides == 2 else result[0]


def take_kernel(deps, place, *refs):
    refs[-1][...] = refs[0][...]


def take(w, at, axis, parts, deps=()):
    shape = list(w.shape)
    shape[axis] //= parts
    block = tuple(shape)
    where = (lambda i, p: (p[0], 0)) if axis == 0 else (lambda i, p: (0, p[0]))
    return pl.pallas_call(
        functools.partial(take_kernel, len(deps)),
        grid_spec=pltpu.PrefetchScalarGridSpec(
            num_scalar_prefetch=1,
            grid=(1,),
            in_specs=[pl.BlockSpec(block, where)] + [pl.BlockSpec(memory_space=pl.ANY)] * len(deps),
            out_specs=pl.BlockSpec(block, lambda i, p: (0, 0)),
        ),
        out_shape=jax.ShapeDtypeStruct(block, w.dtype),
        compiler_params=vmem(32),
        cost_estimate=pl.CostEstimate(flops=0, bytes_accessed=4 * block[0] * block[1], transcendentals=0),
        name="take",
    )(jnp.reshape(at, (1,)).astype(jnp.int32), w, *deps)


def hold(x, dep):
    return pl.pallas_call(
        lambda a, b, c: None,
        in_specs=[ANY, ANY],
        out_specs=ANY,
        out_shape=jax.ShapeDtypeStruct(x.shape, x.dtype),
        input_output_aliases={0: 0},
        name="hold",
    )(x, dep)


def gather_kernel(turn, n, deps, order, *refs):
    pieces, refs = refs[:n], refs[n + deps :]
    out = refs[0]
    rows = pieces[0].shape[0]
    held = refs[1] if turn else out
    for k, piece in enumerate(pieces):
        at = pl.ds(pl.multiple_of(order[k] * rows, rows), rows)
        held[at, :] = piece[...].astype(held.dtype)
    if turn:
        out[...] = held[...].T.astype(f32)


def gathered(pieces, order, turn, deps=(), start=0, cols=None):
    n = len(pieces)
    rows = pieces[0].shape[0]
    cols = cols or pieces[0].shape[1]
    wide = 128 if turn or cols % 256 or start % 256 else 256
    base = start // wide
    total = n * rows
    return pl.pallas_call(
        functools.partial(gather_kernel, turn, n, len(deps)),
        grid_spec=pltpu.PrefetchScalarGridSpec(
            num_scalar_prefetch=1,
            grid=(cols // wide,),
            in_specs=[pl.BlockSpec((rows, wide), lambda i, o: (0, base + i))] * n + [ANY] * len(deps),
            out_specs=pl.BlockSpec((wide, total), lambda i, o: (i, 0))
            if turn
            else pl.BlockSpec((total, wide), lambda i, o: (0, i)),
            scratch_shapes=[pltpu.VMEM((total, wide), bf16)] if turn else [],
        ),
        out_shape=jax.ShapeDtypeStruct((cols, total) if turn else (total, cols), f32),
        compiler_params=vmem(32),
        cost_estimate=pl.CostEstimate(flops=0, bytes_accessed=6 * total * cols, transcendentals=0),
        name="gathered",
    )(order, *pieces, *deps)


def gather_small_kernel(n, kn, half, deps, order, *refs):
    pieces, refs = refs[:n], refs[n + deps :]
    kv, rope, gains, held = refs
    rows = pieces[0].shape[0]
    for k, piece in enumerate(pieces):
        at = pl.ds(pl.multiple_of(order[k] * rows, rows), rows)
        kv[at, :] = piece[:, :kn].astype(f32)
        held[at, :] = piece[:, kn:].astype(f32)
    rope[...] = held[:, :half]
    gains[...] = held[...].T[half : half + 8, :]


def gathered_small(pieces, order, kn, half, deps=()):
    n = len(pieces)
    rows, cols = pieces[0].shape
    total = n * rows
    full = lambda a: pl.BlockSpec(a, lambda i, o: (0, 0))
    shapes = [(total, kn), (total, half), (8, total)]
    return pl.pallas_call(
        functools.partial(gather_small_kernel, n, kn, half, len(deps)),
        grid_spec=pltpu.PrefetchScalarGridSpec(
            num_scalar_prefetch=1,
            grid=(1,),
            in_specs=[full((rows, cols))] * n + [ANY] * len(deps),
            out_specs=[full(a) for a in shapes],
            scratch_shapes=[pltpu.VMEM((total, 128), f32)],
        ),
        out_shape=[jax.ShapeDtypeStruct(a, f32) for a in shapes],
        compiler_params=vmem(32),
        cost_estimate=pl.CostEstimate(flops=0, bytes_accessed=6 * total * cols, transcendentals=0),
        name="gathered_small",
    )(order, *pieces, *deps)


def wgrad_kernel(n, deps, place, l_ref, *refs):
    right, refs = refs[:n], refs[n + deps :]
    keep, send, lT = refs
    lT[...] = l_ref[...].T
    core = place[0]
    hw = keep.shape[0]
    for out, side in ((send, 1 - core), (keep, core)):
        rows = lT[pl.ds(pl.multiple_of(side * hw, hw), hw), :]
        at = 0
        for r in right:
            k = r.shape[-2]
            out[:, at : at + k] = dot_nt(rows, r[...].reshape(r.shape[-2:])).astype(bf16)
            at += k


def wgrad(place, left, right, deps=()):
    rows, width = left.shape
    right = [r if isinstance(r, tuple) else (r[None], 0) for r in right]
    cols = sum(r.shape[1] for r, _ in right)
    full = lambda a: pl.BlockSpec(a, lambda i, p: (0, 0))
    part = jax.ShapeDtypeStruct((width // 2, cols), bf16)

    def spec(r, k):
        return pl.BlockSpec((1, *r.shape[1:]), lambda i, p: (k, 0, 0))

    return pl.pallas_call(
        functools.partial(wgrad_kernel, len(right), len(deps)),
        grid_spec=pltpu.PrefetchScalarGridSpec(
            num_scalar_prefetch=1,
            grid=(1,),
            in_specs=[full(left.shape)] + [spec(r, k) for r, k in right] + [ANY] * len(deps),
            out_specs=[full(part.shape)] * 2,
            scratch_shapes=[pltpu.VMEM((width, rows), bf16)],
        ),
        out_shape=[part] * 2,
        compiler_params=vmem(48),
        cost_estimate=pl.CostEstimate(flops=4 * rows * width * cols, bytes_accessed=4 * rows * width, transcendentals=0),
        name="weight_grads",
    )(place, left, *[r for r, _ in right], *deps)


def back_kernel(n, *refs):
    tgs, sgs, out = refs[:n], refs[n : 2 * n], refs[2 * n]
    hd = tgs[0].shape[1]
    for k, tg in enumerate(tgs):
        out[k * hd : (k + 1) * hd, :] = tg[0].astype(bf16)
    total = sgs[0][...]
    for s in sgs[1:]:
        total = total + s[...]
    out[n * hd :, :] = total.astype(bf16)


def back_call(tgs, sgs):
    n = len(tgs)
    _, hd, two = tgs[0].shape
    rows = two // 2
    return pl.pallas_call(
        functools.partial(back_kernel, n),
        grid=(1,),
        in_specs=[pl.BlockSpec((1, hd, rows), lambda i: (0, 0, 0))] * n
        + [pl.BlockSpec((hd // 2, rows), lambda i: (0, 0))] * n,
        out_specs=pl.BlockSpec((n * hd + hd // 2, rows), lambda i: (0, 0)),
        out_shape=jax.ShapeDtypeStruct((n * hd + hd // 2, rows), bf16),
        compiler_params=vmem(32),
        cost_estimate=pl.CostEstimate(flops=0, bytes_accessed=6 * n * hd * rows, transcendentals=0),
        name="partner_key_grads",
    )(*tgs, *sgs)


def own_kernel(n, deps, *refs):
    tgs, sgs, back, cos_ref, sin_ref = refs[:n], refs[n : 2 * n], refs[2 * n], refs[2 * n + 1], refs[2 * n + 2]
    out = refs[2 * n + 3 + deps]
    hd = tgs[0].shape[1]
    for k, tg in enumerate(tgs):
        other = (k + n // 2) % n
        mine = back[other * hd : (other + 1) * hd, :].astype(f32)
        out[k * hd : (k + 1) * hd, :] = (tg[0] + mine).astype(bf16)
    total = back[n * hd :, :].astype(f32)
    for s in sgs:
        total = total + s[...]
    out[n * hd :, :] = turned_rows(total, cos_ref[...], -sin_ref[...], hd // 4).astype(bf16)


def own_call(tgs, sgs, back, cosT, sinT, deps=()):
    n = len(tgs)
    _, hd, two = tgs[0].shape
    rows = two // 2
    full = lambda a: pl.BlockSpec(a.shape, lambda i: (0, 0))
    return pl.pallas_call(
        functools.partial(own_kernel, n, len(deps)),
        grid=(1,),
        in_specs=[pl.BlockSpec((1, hd, rows), lambda i: (0, 0, 1))] * n
        + [pl.BlockSpec((hd // 2, rows), lambda i: (0, 1))] * n
        + [full(back), full(cosT), full(sinT)]
        + [ANY] * len(deps),
        out_specs=full(back),
        out_shape=jax.ShapeDtypeStruct(back.shape, bf16),
        compiler_params=vmem(32),
        cost_estimate=pl.CostEstimate(flops=0, bytes_accessed=8 * n * hd * rows, transcendentals=0),
        name="own_key_grads",
    )(*tgs, *sgs, back, cosT, sinT, *deps)


def post_kernel(nq, deps, x_ref, mg_ref, gain_ref, kv_ref, wqa, wqb, wka, wkb, wr, *refs):
    dqs, refs = refs[:nq], refs[nq + deps :]
    out, gain_out = refs
    kn = wka.shape[1]
    hn = wqa.shape[1]
    g = [r[0] for r in dqs]
    qa = jnp.concatenate(g[: nq // 2], axis=0).T
    qb = jnp.concatenate(g[nq // 2 :], axis=0).T
    kv = kv_ref[...]
    first = dot_nt(qa, wqa[...]) + dot_nt(qb, wqb[...])
    first = first + dot_nt(kv[:kn].T, wka[...]) + dot_nt(kv[kn : 2 * kn].T, wkb[...])
    first = first + dot_nt(kv[2 * kn :].T, wr[...])
    x = x_ref[...].astype(f32)
    factor = lax.rsqrt(jnp.mean(x * x, axis=-1, keepdims=True) + eps_norm)
    normed = x * factor
    inner = first * gain_ref[...]
    back = factor * (inner - normed * jnp.mean(inner * normed, axis=-1, keepdims=True))
    out[...] = (mg_ref[...] + back).astype(bf16)

    @pl.when(pl.program_id(0) == 0)
    def _():
        gain_out[...] = jnp.zeros_like(gain_out)

    gain_out[...] += jnp.sum(first * normed, axis=0, keepdims=True)


def post_call(x, middle_grad, gain, kv, weights, dqs, deps=(), bt=256):
    rows, width = x.shape
    full = lambda a: pl.BlockSpec(a.shape, lambda i: (0, 0), pipeline_mode=pl.Buffered(1))
    row = pl.BlockSpec((bt, width), lambda i: (i, 0))
    one = pl.BlockSpec((1, width), lambda i: (0, 0))
    return pl.pallas_call(
        functools.partial(post_kernel, len(dqs), len(deps)),
        grid=(rows // bt,),
        in_specs=[row, row, one, pl.BlockSpec((kv.shape[0], bt), lambda i: (0, i))]
        + [full(w) for w in weights]
        + [pl.BlockSpec((1, d.shape[1], bt), lambda i: (0, 0, i)) for d in dqs]
        + [ANY] * len(deps),
        out_specs=[row, one],
        out_shape=[jax.ShapeDtypeStruct((rows, width), bf16), jax.ShapeDtypeStruct((1, width), f32)],
        compiler_params=vmem(40),
        cost_estimate=pl.CostEstimate(flops=5 * rows * width * width, bytes_accessed=16 * rows * width, transcendentals=0),
        name="token_grads",
    )(x, middle_grad, gain[None, :], kv, *weights, *dqs, *deps)


def small_kernel(kn, half, place, f_ref, kv_ref, gain_a, gain_b, keep_a, send_a, keep_b, send_b, lT, rows_s, rows_g):
    lT[...] = f_ref[...].T
    rows_s[...] = jnp.zeros_like(rows_s)
    rows_s[:half, :] = kv_ref[2 * kn :, :]
    rows_g[...] = jnp.zeros_like(rows_g)
    rows_g[half : half + 1, :] = gain_a[...]
    rows_g[half + 1 : half + 2, :] = gain_b[...]
    gains = rows_g[...].T
    rows_g_ref = rows_g
    core = place[0]
    hw = keep_a.shape[0]
    rope = dot_nt(lT[...], rows_s[...]) + gains
    lT_rows = [lT[:hw, :], lT[hw:, :]]
    first = core == 0
    for (a, b), side in (((send_a, send_b), 1), ((keep_a, keep_b), 0)):
        low = jnp.logical_xor(first, side == 1)
        rows = jnp.where(low, lT_rows[0], lT_rows[1])
        small = jnp.where(low, rope[:hw], rope[hw:]).astype(bf16)
        a[:, :kn] = dot_nt(rows, kv_ref[:kn, :]).astype(bf16)
        a[:, kn:] = small
        b[:, :kn] = dot_nt(rows, kv_ref[kn : 2 * kn, :]).astype(bf16)
        b[:, kn:] = small


def small_call(place, f, kv, gain_a, gain_b, kn, half):
    rows, width = f.shape
    full = lambda a: pl.BlockSpec(a, lambda i, p: (0, 0))
    part = jax.ShapeDtypeStruct((width // 2, kn + 128), bf16)
    return pl.pallas_call(
        functools.partial(small_kernel, kn, half),
        grid_spec=pltpu.PrefetchScalarGridSpec(
            num_scalar_prefetch=1,
            grid=(1,),
            in_specs=[full(f.shape), full(kv.shape), full((1, width)), full((1, width))],
            out_specs=[full(part.shape)] * 4,
            scratch_shapes=[pltpu.VMEM((width, rows), bf16), pltpu.VMEM((128, rows), bf16), pltpu.VMEM((128, width), f32)],
        ),
        out_shape=[part] * 4,
        compiler_params=vmem(48),
        cost_estimate=pl.CostEstimate(flops=2 * rows * width * 512, bytes_accessed=3 * rows * width, transcendentals=0),
        name="small_grads",
    )(place, f, kv, gain_a, gain_b)


def rms_parts(values):
    factor = lax.rsqrt(jnp.mean(values * values, axis=-1, keepdims=True) + eps_norm)
    return values * factor, factor


def norm_back(grad, normed, factor, gain):
    inner = grad * gain
    return factor * (inner - normed * jnp.mean(inner * normed, axis=-1, keepdims=True))


def mm(a, b, ca, cb):
    return lax.dot_general(a, b, (((ca,), (cb,)), ((), ())), preferred_element_type=f32)


def swap(x, axis, bit):
    n = lax.axis_size(axis)
    return lax.ppermute(x, axis, [(i, i ^ bit) for i in range(n)])


def joined(mine, other, bit):
    first = bit == 0
    return jnp.concatenate([jnp.where(first, mine, other), jnp.where(first, other, mine)], axis=0)


class Order:
    def __init__(self, first):
        self.last = first

    def after(self, out):
        self.last = out[0] if isinstance(out, (tuple, list)) else out
        return out

    def fold(self, groups, bit=None):
        return self.after(fold(groups, bit, (self.last,)))


def spread(piece, steps):
    pieces = [piece]
    for step in steps:
        pieces = pieces + [swap(p, "dp", step) for p in pieces]
    return pieces


def piece_order(bits):
    order = [jnp.int32(0)]
    for bit in bits:
        order = [2 * o + b for o in order for b in (bit, 1 - bit)]
    return jnp.stack(order).astype(jnp.int32)


class Sum:
    def __init__(self, run, bits):
        self.run, self.bits, self.steps = run, bits, [1]

    def x(self, groups):
        self.keep, send = self.run.fold(groups, self.bits[1])
        self.got = swap(send, "dp", 2)
        self.steps = [2, 1]

    def z(self):
        self.keep, send = self.run.fold([[self.keep, self.got]], self.bits[2])
        self.got = swap(send, "dp", 4)
        self.steps = [4, 2, 1]

    def line(self, step=8):
        self.keep = self.run.fold([[self.keep, self.got]])
        self.got = swap(self.keep, "dp", step)

    def end(self):
        step = 16
        while step < lax.axis_size("dp"):
            self.line(step)
            step *= 2
        self.keep = self.run.fold([[self.keep, self.got]])
        self.pieces = spread(self.keep, self.steps)
        self.order = piece_order(self.bits[: len(self.steps)])


def body(tokens, lengths, attn_gain, w_query, w_kv, w_rope, w_out, mlp_gain, w_gate, w_up, w_down, out_grad):
    rows, width = tokens.shape
    shards = lax.axis_size("tensor")
    t = lax.axis_index("tensor")
    index = lax.axis_index("dp")
    bits = (index & 1, (index >> 1) & 1, (index >> 2) & 1)
    core = bits[0]
    half = w_rope.shape[1]
    hd = 2 * half
    kv_own = w_kv.shape[1]
    q_own = w_query.shape[1]
    groups = kv_own // hd
    per = q_own // kv_own
    ff = w_gate.shape[1]
    own0 = rows
    bq_f, bk_f, bq_b, bk_b = 256, 512, 512, 256
    place = jnp.stack([core, core, 1 - core]).astype(jnp.int32)

    kv_piece = take(w_kv, core, 0, 2)
    kv_got = swap(kv_piece, "tensor", 1)
    q_piece = take(w_query, core, 0, 2, (kv_piece,))
    q_got = swap(q_piece, "tensor", 1)
    gate_piece = take(w_gate, core, 0, 2, (q_piece,))
    gate_got = swap(gate_piece, "tensor", 1)

    slot, position, valid, start, bounds_f = local_layout(lengths[0], t, rows, bq_f, bk_f, own0)
    bounds_b = local_layout(lengths[0], t, rows, bq_b, bk_b, own0)[4]
    quarter = half // 2
    freq = 10000.0 ** (-jnp.arange(quarter, dtype=f32) / quarter)
    angle = freq[:, None] * position[None, :]
    cosT, sinT = jnp.cos(angle), jnp.sin(angle)

    first_in, tied_a, shared, q_a = pre_call(tokens, attn_gain, w_kv, w_rope, w_query, cosT, sinT, hd, per)
    sent, w_kv_o = kv_call(place, first_in, kv_got, swap(kv_got, "dp", 1), tied_a, shared)
    got = lax.ppermute(sent, "tensor", [(i, i + 1) for i in range(shards - 1)])
    up_piece = take(w_up, core, 0, 2, (got,))
    up_got = swap(up_piece, "tensor", 1)
    out_piece = take(w_out, core, 0, 2, (up_piece,))
    out_got = swap(out_piece, "tensor", 1)
    down_piece = take(w_down, core, 1, 2, (out_piece,))
    down_got = swap(down_piece, "tensor", 1)

    def both(p):
        return p, swap(p, "dp", 1)

    at_a, at_b = (0, groups), (groups, 0)
    mixed_a, lse_a = attn_fwd(bounds_f, start, q_a, sent, got, hd, at_a, bq_f, bk_f, (down_piece,))
    q_got = hold(q_got, mixed_a)
    q_b, w_query_o = query_call(place, first_in, q_got, swap(q_got, "dp", 1), cosT, sinT, hd, groups, per)
    mixed_b, lse_b = attn_fwd(bounds_f, start, q_b, sent, got, hd, at_b, bq_f, bk_f)
    out_got = hold(out_got, mixed_b)
    w_out_o = joined(out_got, swap(out_got, "dp", 1), core)
    mix_a, mix_b = mixed_a.reshape(-1, rows), mixed_b.reshape(-1, rows)
    inputs = tokens.astype(f32)
    middle = inputs + mm(mix_a, w_out, 0, 0) + mm(mix_b, w_out_o, 0, 0)
    normed_two, factor_two = rms_parts(middle)
    second_in = (normed_two * mlp_gain).astype(bf16)

    hid_a, gg_a, ug_a, keep_a, send_a, in_T, back_T = mlp_call(
        place, second_in, out_grad, None, (w_gate, w_up, w_down), 0, ff
    )
    core_a = swap(send_a, "dp", 1)
    gates, ups, downs = both(hold(gate_got, mixed_b)), both(hold(up_got, mixed_b)), both(hold(down_got, hid_a))
    second_a = mm(hold(gg_a, downs[0]), w_gate, 1, 1) + mm(hold(ug_a, downs[0]), w_up, 1, 1)
    hid_b, gg_b, ug_b, keep_b, send_b, w_gate_o, w_up_o, w_down_o = mlp_call(
        place, second_in, out_grad, (in_T, back_T), (*gates, *ups, *downs), 0, ff, deps=(second_a,)
    )
    core_b = swap(send_b, "dp", 1)
    hid_a = hold(hid_a, hid_b)
    layer_out = (middle + mm(hid_a, w_down, 1, 0) + mm(hid_b, w_down_o, 1, 0)).astype(bf16)
    run = Order(layer_out)
    ysend = [run.fold([[(keep_b, k), (core_b, k)]]) for k in range(3)]
    ygot = [swap(y, "tensor", 1) for y in ysend]
    gg_b, ug_b = hold(gg_b, run.last), hold(ug_b, run.last)
    second_grad = second_a + mm(gg_b, w_gate_o, 1, 1) + mm(ug_b, w_up_o, 1, 1)
    mlp_gain_part = jnp.sum(second_grad * normed_two, axis=0, keepdims=True)
    middle_grad = out_grad.astype(f32) + norm_back(second_grad, normed_two, factor_two, mlp_gain)
    attn_back = middle_grad.astype(bf16)
    live = valid[None, :].astype(bf16)
    mixed_grad_b = (mm(w_out_o, attn_back, 1, 1).astype(bf16) * live).reshape(mixed_b.shape)
    mixed_grad_a = (mm(w_out, attn_back, 1, 1).astype(bf16) * live).reshape(mixed_a.shape)

    def parts(x):
        return [(x, k) for k in range(groups)]

    def back(q, mixed, lse, grad, at, k):
        return run.after(
            attn_bwd(
                bounds_b, start, q, sent, got, mixed, lse, grad, cosT, sinT, hd, at, k, 1, bq_b, bk_b, (run.last,)
            )
        )

    wo_keep_b, wo_send_b = run.after(wgrad(place, attn_back, parts(mixed_b), (run.last,)))
    wo_core_b = swap(wo_send_b, "dp", 1)
    wo_keep_a, wo_send_a = run.after(wgrad(place, attn_back, parts(mixed_a), (run.last,)))
    wo_core_a = swap(wo_send_a, "dp", 1)

    gate_s, up_s, down_s, rest_s, small_s = (Sum(run, bits) for _ in range(5))
    gate_s.x([[(keep_a, 0), (core_a, 0), ygot[0]]])
    dq_b0, tg_b0, sg_b0 = back(q_b, mixed_b, lse_b, mixed_grad_b, at_b, 0)
    wo_got = swap(run.fold([[wo_keep_b, wo_core_b]]), "tensor", 1)
    gate_s.z()
    dq_b1, tg_b1, sg_b1 = back(q_b, mixed_b, lse_b, mixed_grad_b, at_b, 1)
    wq_keep_b, wq_send_b = run.after(wgrad(place, first_in, [(dq_b0, 0), (dq_b1, 0)], (run.last,)))
    wq_core_b = swap(wq_send_b, "dp", 1)
    up_s.x([[(keep_a, 1), (core_a, 1), ygot[1]]])
    gate_s.line()
    dq_a0, tg_a0, sg_a0 = back(q_a, mixed_a, lse_a, mixed_grad_a, at_a, 0)
    wq_got = swap(run.fold([[wq_keep_b, wq_core_b]]), "tensor", 1)
    up_s.z()
    down_s.x([[(keep_a, 2), (core_a, 2), ygot[2]]])
    gate_s.end()
    dq_a1, tg_a1, sg_a1 = back(q_a, mixed_a, lse_a, mixed_grad_a, at_a, 1)
    tgs, sgs = (tg_a0, tg_a1, tg_b0, tg_b1), (sg_a0, sg_a1, sg_b0, sg_b1)
    key_back = run.after(back_call(tgs, sgs))
    key_got = lax.ppermute(key_back, "tensor", [(i + 1, i) for i in range(shards - 1)])
    wq_keep_a, wq_send_a = run.after(wgrad(place, first_in, [(dq_a0, 0), (dq_a1, 0)], (run.last,)))
    wq_core_a = swap(wq_send_a, "dp", 1)
    down_s.z()
    up_s.line()
    rest_s.x([[wo_keep_a, wo_core_a, wo_got], [wq_keep_a, wq_core_a, wq_got]])
    kv_grad = run.after(own_call(tgs, sgs, key_got, cosT, sinT, (run.last,)))
    tokens_grad, attn_gain_part = post_call(
        tokens, middle_grad, attn_gain, kv_grad, (w_query, w_query_o, w_kv, w_kv_o, w_rope),
        (dq_a0, dq_a1, dq_b0, dq_b1), (run.last,),
    )
    run.last = attn_gain_part
    sm_keep_a, sm_send_a, sm_keep_b, sm_send_b = run.after(
        small_call(place, first_in, kv_grad, attn_gain_part, mlp_gain_part, kv_own, half)
    )
    sm_core_b = swap(sm_send_b, "dp", 1)
    sm_core_a = swap(sm_send_a, "dp", 1)
    down_s.line()
    rest_s.z()
    up_s.end()
    sm_got = swap(run.fold([[sm_keep_b, sm_core_b]]), "tensor", 1)
    gate_sum = run.after(gathered(gate_s.pieces, gate_s.order, False, (run.last,)))
    small_s.x([[sm_keep_a, sm_core_a, sm_got]])
    rest_s.line()
    down_s.end()
    small_s.line(4)
    small_s.line()
    rest_s.end()
    up_sum = run.after(gathered(up_s.pieces, up_s.order, False, (run.last,)))
    small_s.end()
    down_sum = run.after(gathered(down_s.pieces, down_s.order, True, (run.last,)))
    out_sum = run.after(gathered(rest_s.pieces, rest_s.order, True, (run.last,), 0, q_own))
    query_sum = run.after(gathered(rest_s.pieces, rest_s.order, False, (run.last,), q_own, q_own))
    kv_sum, rope_sum, gains = gathered_small(small_s.pieces, small_s.order, kv_own, half, (run.last,))
    return (
        layer_out,
        tokens_grad,
        gains[0],
        query_sum,
        kv_sum,
        rope_sum,
        out_sum,
        gains[1],
        gate_sum,
        up_sum,
        down_sum,
    )


def solution(mesh):
    rows = P(("dp", "tensor"), None)
    columns = P(None, "tensor")
    down = P("tensor", None)
    return jax.shard_map(
        body,
        mesh=mesh,
        in_specs=(rows, P("dp", None), P(), columns, columns, P(), down, P(), columns, columns, down, rows),
        out_specs=(rows, rows, P(), columns, columns, P(), down, P(), columns, columns, down),
        check_vma=False,
    )
```

```python
import functools

import jax
import jax.numpy as jnp
from jax import lax
from jax.experimental import pallas as pl
from jax.experimental.pallas import tpu as pltpu
from jax.sharding import PartitionSpec as P

eps_norm = 1e-05
masked_score = -1e30
f32 = jnp.float32
bf16 = jnp.bfloat16


def dot(a, b):
    return lax.dot_general(a, b, (((1,), (0,)), ((), ())), preferred_element_type=f32)


def dot_nt(a, b):
    return lax.dot_general(a, b, (((1,), (1,)), ((), ())), preferred_element_type=f32)


ANY = pl.BlockSpec(memory_space=pl.ANY)


TOKEN = jax.ShapeDtypeStruct((8, 128), f32)


def token_spec():
    return pl.BlockSpec((8, 128), lambda *a: (0, 0))


def mark(token):
    token[...] = jnp.zeros_like(token)


def vmem(mib):
    return pltpu.CompilerParams(vmem_limit_bytes=mib << 20)


def block_loops(bounds, i, step):
    k0, k1, k2, k3 = (bounds[i, n] for n in range(4))
    lax.fori_loop(k0, k1, lambda kb, c: step(kb, True), None)
    lax.fori_loop(k1, k2, lambda kb, c: step(kb, False), None)
    lax.fori_loop(k2, k3, lambda kb, c: step(kb, True), None)


def allowed_tile(start, kb, bk, qpos):
    kk = lax.broadcasted_iota(jnp.int32, (bk, start.shape[1]), 0) + kb * bk
    return (kk >= start) & (kk <= qpos)


def load_keys(own, partner, sent_ref, got_ref, k, kT, vT):
    hd = kT.shape[1]
    half = hd // 2
    rows = sent_ref.shape[1]
    shared = sent_ref.shape[0] - half
    for side, (at, ref) in enumerate(((partner, got_ref), (own, sent_ref))):
        to = slice(side * rows, (side + 1) * rows)
        vT[k, :, to] = ref[at * hd : (at + 1) * hd, :]
        kT[k, :half, to] = ref[at * hd : at * hd + half, :]
        kT[k, half:, to] = ref[shared:, :]


def fwd_kernel(n, heads, bk, deps, bounds, start_ref, qa_ref, qb_ref, sent_ref, got_ref, *refs):
    oa_ref, ob_ref, lsea_ref, lseb_ref, kT, vT, ks, acc, ms, ls = refs[deps:]
    i = pl.program_id(0)
    hd = kT.shape[1]
    bq = qa_ref.shape[2]
    own0 = kT.shape[2] // 2
    width = heads * hd

    @pl.when(i == 0)
    def _():
        for k in range(2 * n):
            load_keys(k, (k + n) % (2 * n), sent_ref, got_ref, k, kT, vT)
            ks[k] = kT[k].T

    acc[...] = jnp.zeros_like(acc)
    ms[...] = jnp.full_like(ms, masked_score)
    ls[...] = jnp.zeros_like(ls)
    start = start_ref[...]
    qpos = own0 + i * bq + lax.broadcasted_iota(jnp.int32, (1, bq), 1)

    def step(kb, masked):
        rows = pl.ds(pl.multiple_of(kb * bk, bk), bk)
        if masked:
            ok = allowed_tile(start, kb, bk, qpos)
        for k in range(2 * n):
            q_ref = qa_ref if k < n else qb_ref
            kblk = ks[k, rows, :]
            vblk = vT[k, :, rows]
            h0 = k * heads
            mold = [ms[h : h + 1, :] for h in range(h0, h0 + heads)]
            lold = [ls[h : h + 1, :] for h in range(h0, h0 + heads)]
            aold = [acc[h * hd : (h + 1) * hd, :] for h in range(h0, h0 + heads)]
            ss = [dot(kblk, q_ref[k % n, j * hd : (j + 1) * hd, :]) for j in range(heads)]
            if masked:
                ss = [jnp.where(ok, s, masked_score) for s in ss]
            mnew = [jnp.maximum(m, jnp.max(s, axis=0, keepdims=True)) for m, s in zip(mold, ss)]
            ps = [jnp.exp(s - m) for s, m in zip(ss, mnew)]
            als = [jnp.exp(a - b) for a, b in zip(mold, mnew)]
            lnew = [l * al + jnp.sum(p, axis=0, keepdims=True) for l, al, p in zip(lold, als, ps)]
            anew = [a * al + dot(vblk, p.astype(bf16)) for a, al, p in zip(aold, als, ps)]
            for j in range(heads):
                h = h0 + j
                ms[h : h + 1, :] = mnew[j]
                ls[h : h + 1, :] = lnew[j]
                acc[h * hd : (h + 1) * hd, :] = anew[j]

    block_loops(bounds, i, step)
    live = start < (1 << 29)
    for h in range(2 * n * heads):
        l = ls[h : h + 1, :]
        safe = jnp.where(l > 0, l, 1.0)
        side, g, j = h // (n * heads), h // heads % n, h % heads
        o_ref, lse_ref = ((oa_ref, lsea_ref), (ob_ref, lseb_ref))[side]
        out = jnp.where(live, acc[h * hd : (h + 1) * hd, :] / safe, 0.0)
        o_ref[g, j * hd : (j + 1) * hd, :] = out.astype(bf16)
        lse_ref[g, j : j + 1, :] = ms[h : h + 1, :] + jnp.log(safe)


def attn_fwd(bounds, start, qa, qb, sent, got, hd, bq, bk, deps=()):
    n, width, rows = qa.shape
    heads = width // hd
    tile = pl.BlockSpec((n, width, bq), lambda i, b: (0, 0, i))
    logs = pl.BlockSpec((n, heads, bq), lambda i, b: (0, 0, i))
    kv = pl.BlockSpec(sent.shape, lambda i, b: (0, 0), pipeline_mode=pl.Buffered(1))
    return pl.pallas_call(
        functools.partial(fwd_kernel, n, heads, bk, len(deps)),
        grid_spec=pltpu.PrefetchScalarGridSpec(
            num_scalar_prefetch=1,
            grid=(rows // bq,),
            in_specs=[pl.BlockSpec((1, bq), lambda i, b: (0, i)), tile, tile, kv, kv] + [ANY] * len(deps),
            out_specs=[tile, tile, logs, logs],
            scratch_shapes=[
                pltpu.VMEM((2 * n, hd, 2 * rows), bf16),
                pltpu.VMEM((2 * n, hd, 2 * rows), bf16),
                pltpu.VMEM((2 * n, 2 * rows, hd), bf16),
                pltpu.VMEM((2 * n * width, bq), f32),
                pltpu.VMEM((2 * n * heads, bq), f32),
                pltpu.VMEM((2 * n * heads, bq), f32),
            ],
        ),
        out_shape=[jax.ShapeDtypeStruct((n, width, rows), bf16)] * 2
        + [jax.ShapeDtypeStruct((n, heads, rows), f32)] * 2,
        compiler_params=vmem(60),
        cost_estimate=pl.CostEstimate(
            flops=96 * n * width * rows * rows, bytes_accessed=8 * n * width * rows, transcendentals=0
        ),
        name="attn_fwd",
    )(bounds, start, qa, qb, sent, got, *deps)


def bwd_kernel(
    n, first, partner, heads, bk, scale, deps, bounds, start_ref, q_ref, o_ref, lse_ref, do_ref, cos_ref, sin_ref,
    sent_ref, got_ref, *refs
):
    dq_ref, tg_ref, sg_ref, token, kT, vT, ks, vs, dk, dv, dqa, dl = refs[deps:]
    mark(token)
    i = pl.program_id(0)
    hd = kT.shape[1]
    half = hd // 2
    quarter = hd // 4
    bq = q_ref.shape[2]
    own0 = kT.shape[2] // 2

    @pl.when(i == 0)
    def _():
        for g in range(n):
            load_keys(first + g, partner + g, sent_ref, got_ref, g, kT, vT)
            ks[g] = kT[g].T
            vs[g] = vT[g].T
        dk[...] = jnp.zeros_like(dk)
        dv[...] = jnp.zeros_like(dv)

    dqa[...] = jnp.zeros_like(dqa)
    sls = [slice(j * hd, (j + 1) * hd) for j in range(heads)]
    for g in range(n):
        for j, sl in enumerate(sls):
            prod = do_ref[g, sl, :].astype(f32) * o_ref[g, sl, :].astype(f32)
            dl[g * heads + j : g * heads + j + 1, :] = jnp.sum(prod, axis=0, keepdims=True)
    start = start_ref[...]
    qpos = own0 + i * bq + lax.broadcasted_iota(jnp.int32, (1, bq), 1)

    def step(kb, masked):
        rows = pl.ds(pl.multiple_of(kb * bk, bk), bk)
        if masked:
            ok = allowed_tile(start, kb, bk, qpos)
        for g in range(n):
            kblk = ks[g, rows, :]
            vblk = vs[g, rows, :]
            kTb = kT[g, :, rows]
            dvt = dv[g, :, rows]
            dkt = dk[g, :, rows]
            qs = [q_ref[g, sl, :] for sl in sls]
            dos = [do_ref[g, sl, :] for sl in sls]
            lses = [lse_ref[g, j : j + 1, :] for j in range(heads)]
            dls = [dl[g * heads + j : g * heads + j + 1, :] for j in range(heads)]
            dqs = [dqa[g, sl, :] for sl in sls]
            new = []
            for j in range(heads):
                s = dot(kblk, qs[j])
                if masked:
                    s = jnp.where(ok, s, masked_score)
                p = jnp.exp(s - lses[j])
                dp = dot(vblk, dos[j])
                ds = (p * (dp - dls[j])).astype(bf16)
                dvt = dvt + dot_nt(dos[j], p.astype(bf16))
                dkt = dkt + dot_nt(qs[j], ds)
                new.append(dqs[j] + dot(kTb, ds))
            for sl, x in zip(sls, new):
                dqa[g, sl, :] = x
            dv[g, :, rows] = dvt
            dk[g, :, rows] = dkt

    block_loops(bounds, i, step)
    cosv = cos_ref[...]
    sinv = sin_ref[...]
    for g in range(n):
        for sl in sls:
            x = dqa[g, sl, :] * scale
            a, b = x[half : half + quarter], x[half + quarter :]
            turned = jnp.concatenate([x[:half], a * cosv + b * sinv, b * cosv - a * sinv], axis=0)
            dq_ref[g, sl, :] = turned.astype(bf16)

    @pl.when(i == pl.num_programs(0) - 1)
    def _():
        for g in range(n):
            tg_ref[g, :half, :] = dv[g, :half, :] + dk[g, :half, :]
            tg_ref[g, half:, :] = dv[g, half:, :]
        total = dk[0, half:, :]
        for g in range(1, n):
            total = total + dk[g, half:, :]
        sg_ref[...] = total


def attn_bwd(bounds, start, q, sent, got, o, lse, do, cosT, sinT, hd, side, g0, n, bq, bk, deps=()):
    groups, width, rows = q.shape
    first, partner = side * groups + g0, (1 - side) * groups + g0
    heads = width // hd
    tile = pl.BlockSpec((n, width, bq), lambda i, b: (g0 // n, 0, i))
    out = pl.BlockSpec((n, width, bq), lambda i, b: (0, 0, i))
    angle = pl.BlockSpec((hd // 4, bq), lambda i, b: (0, i))
    kv = pl.BlockSpec(sent.shape, lambda i, b: (0, 0), pipeline_mode=pl.Buffered(1))
    return pl.pallas_call(
        functools.partial(bwd_kernel, n, first, partner, heads, bk, hd**-0.5, len(deps)),
        grid_spec=pltpu.PrefetchScalarGridSpec(
            num_scalar_prefetch=1,
            grid=(rows // bq,),
            in_specs=[
                pl.BlockSpec((1, bq), lambda i, b: (0, i)),
                tile,
                tile,
                pl.BlockSpec((n, heads, bq), lambda i, b: (g0 // n, 0, i)),
                tile,
                angle,
                angle,
                kv,
                kv,
            ]
            + [ANY] * len(deps),
            out_specs=[
                out,
                pl.BlockSpec((n, hd, 2 * rows), lambda i, b: (0, 0, 0)),
                pl.BlockSpec((hd // 2, 2 * rows), lambda i, b: (0, 0)),
                token_spec(),
            ],
            scratch_shapes=[
                pltpu.VMEM((n, hd, 2 * rows), bf16),
                pltpu.VMEM((n, hd, 2 * rows), bf16),
                pltpu.VMEM((n, 2 * rows, hd), bf16),
                pltpu.VMEM((n, 2 * rows, hd), bf16),
                pltpu.VMEM((n, hd, 2 * rows), f32),
                pltpu.VMEM((n, hd, 2 * rows), f32),
                pltpu.VMEM((n, width, bq), f32),
                pltpu.VMEM((n * heads, bq), f32),
            ],
        ),
        out_shape=[
            jax.ShapeDtypeStruct((n, width, rows), bf16),
            jax.ShapeDtypeStruct((n, hd, 2 * rows), f32),
            jax.ShapeDtypeStruct((hd // 2, 2 * rows), f32),
            TOKEN,
        ],
        compiler_params=vmem(60),
        cost_estimate=pl.CostEstimate(
            flops=90 * n * width * rows * rows, bytes_accessed=8 * n * width * rows, transcendentals=0
        ),
        name="attn_bwd",
    )(bounds, start, q, o, lse, do, cosT, sinT, sent, got, *deps)


def local_layout(lengths_row, t, rows, bq, bk, own0):
    slot = t * rows + jnp.arange(rows, dtype=jnp.int32)
    ends = jnp.cumsum(lengths_row)
    passed = (slot[:, None] >= ends[None, :]).astype(jnp.int32)
    begin = jnp.sum(passed * lengths_row[None, :], axis=1)
    valid = slot < ends[-1]
    shift = own0 - t * rows
    start = jnp.where(valid, begin + shift, 1 << 30)
    nqb = rows // bq
    first = begin.reshape(nqb, bq)[:, 0] + shift
    last_start = jnp.max(jnp.where(valid, begin + shift, 0).reshape(nqb, bq), axis=1)
    any_valid = valid.reshape(nqb, bq)[:, 0]
    all_valid = valid.reshape(nqb, bq)[:, -1]
    q0 = own0 + jnp.arange(nqb, dtype=jnp.int32) * bq
    k0 = first // bk
    last = jnp.minimum(q0 + bq - 1, ends[-1] + shift - 1)
    k3 = last // bk + 1
    k1 = jnp.minimum((last_start + bk - 1) // bk, k3)
    k2 = jnp.minimum(jnp.maximum((q0 + 1) // bk, k1), k3)
    k1 = jnp.where(all_valid, k1, k3)
    k2 = jnp.where(all_valid, k2, k3)
    bounds = jnp.where(any_valid[:, None], jnp.stack([k0, k1, k2, k3], axis=1), 0).astype(jnp.int32)
    return slot, (slot - begin).astype(f32), valid, start[None, :], bounds


def turned_rows(x, cosv, sinv, n):
    a, b = x[:n], x[n:]
    return jnp.concatenate([a * cosv - b * sinv, a * sinv + b * cosv], axis=0)


def put_queries(raw, cosv, sinv, hd, out):
    half, quarter = hd // 2, hd // 4
    scale = hd**-0.5
    width = out.shape[1]
    for h in range(raw.shape[0] // hd):
        x = raw[h * hd : (h + 1) * hd]
        y = jnp.concatenate([x[:half], turned_rows(x[half:], cosv, sinv, quarter)], axis=0).astype(bf16)
        at = h * hd
        out[at // width, at % width : at % width + hd, :] = (y.astype(f32) * scale).astype(bf16)


def pre_kernel(hd, x_ref, gain_ref, wkv_ref, wr_ref, wq_ref, cos_ref, sin_ref, fin, tied, shared, q, wkvT, wrT, wqT):
    @pl.when(pl.program_id(0) == 0)
    def _():
        wkvT[...] = wkv_ref[...].T
        wrT[...] = wr_ref[...].T
        wqT[...] = wq_ref[...].T

    x = x_ref[...].astype(f32)
    normed = x * lax.rsqrt(jnp.mean(x * x, axis=-1, keepdims=True) + eps_norm)
    f = (normed * gain_ref[...]).astype(bf16)
    fin[...] = f
    cosv, sinv = cos_ref[...], sin_ref[...]
    tied[...] = dot_nt(wkvT[...], f).astype(bf16)
    shared[...] = turned_rows(dot_nt(wrT[...], f), cosv, sinv, hd // 4).astype(bf16)
    put_queries(dot_nt(wqT[...], f), cosv, sinv, hd, q)


def pre_call(x, gain, w_kv, w_rope, w_query, cosT, sinT, hd, per, bt=256):
    rows, width = x.shape
    kv, half, qn = w_kv.shape[1], w_rope.shape[1], w_query.shape[1]
    groups = kv // hd
    full = lambda a: pl.BlockSpec(a.shape, lambda i: (0, 0), pipeline_mode=pl.Buffered(1))
    return pl.pallas_call(
        functools.partial(pre_kernel, hd),
        grid=(rows // bt,),
        in_specs=[
            pl.BlockSpec((bt, width), lambda i: (i, 0)),
            pl.BlockSpec((1, width), lambda i: (0, 0)),
            full(w_kv),
            full(w_rope),
            full(w_query),
            pl.BlockSpec((hd // 4, bt), lambda i: (0, i)),
            pl.BlockSpec((hd // 4, bt), lambda i: (0, i)),
        ],
        out_specs=[
            pl.BlockSpec((bt, width), lambda i: (i, 0)),
            pl.BlockSpec((kv, bt), lambda i: (0, i)),
            pl.BlockSpec((half, bt), lambda i: (0, i)),
            pl.BlockSpec((groups, per * hd, bt), lambda i: (0, 0, i)),
        ],
        out_shape=[
            jax.ShapeDtypeStruct((rows, width), bf16),
            jax.ShapeDtypeStruct((kv, rows), bf16),
            jax.ShapeDtypeStruct((half, rows), bf16),
            jax.ShapeDtypeStruct((groups, per * hd, rows), bf16),
        ],
        scratch_shapes=[pltpu.VMEM((kv, width), bf16), pltpu.VMEM((half, width), bf16), pltpu.VMEM((qn, width), bf16)],
        compiler_params=vmem(32),
        cost_estimate=pl.CostEstimate(flops=4 * rows * width * (qn + kv + half), bytes_accessed=8 * rows * width, transcendentals=0),
        name="first_projections",
    )(x, gain[None, :], w_kv, w_rope, w_query, cosT, sinT)


def kv_kernel(place, f_ref, mine, other, tied_a, shared, sent, w_ref):
    n = mine.shape[0]
    core = place[0]
    w_ref[pl.ds(pl.multiple_of(core * n, n), n), :] = mine[...]
    w_ref[pl.ds(pl.multiple_of((1 - core) * n, n), n), :] = other[...]
    kv = tied_a.shape[0]
    sent[:kv, :] = tied_a[...]
    sent[kv : 2 * kv, :] = dot_nt(w_ref[...].T, f_ref[...]).astype(bf16)
    sent[2 * kv :, :] = shared[...]


def kv_call(place, f, mine, other, tied_a, shared):
    kv, rows = tied_a.shape
    total = 2 * kv + shared.shape[0]
    width = f.shape[1]
    full = lambda a: pl.BlockSpec(a, lambda i, p: (0, 0))
    return pl.pallas_call(
        kv_kernel,
        grid_spec=pltpu.PrefetchScalarGridSpec(
            num_scalar_prefetch=1,
            grid=(1,),
            in_specs=[full(f.shape), full(mine.shape), full(other.shape), full(tied_a.shape), full(shared.shape)],
            out_specs=[full((total, rows)), full((width, kv))],
        ),
        out_shape=[jax.ShapeDtypeStruct((total, rows), bf16), jax.ShapeDtypeStruct((width, kv), bf16)],
        compiler_params=vmem(32),
        cost_estimate=pl.CostEstimate(flops=4 * rows * width * kv, bytes_accessed=2 * rows * width, transcendentals=0),
        name="other_keys",
    )(place, f, mine, other, tied_a, shared)


def query_kernel(hd, place, f_ref, mine, other, cos_ref, sin_ref, q, w_ref, token, wT):
    mark(token)

    @pl.when(pl.program_id(0) == 0)
    def _():
        n = mine.shape[0]
        core = place[0]
        w_ref[pl.ds(pl.multiple_of(core * n, n), n), :] = mine[...]
        w_ref[pl.ds(pl.multiple_of((1 - core) * n, n), n), :] = other[...]
        wT[...] = w_ref[...].T

    put_queries(dot_nt(wT[...], f_ref[...]), cos_ref[...], sin_ref[...], hd, q)


def query_call(place, f, mine, other, cosT, sinT, hd, groups, per, bt=256):
    rows, width = f.shape
    qn = mine.shape[1]
    full = lambda a: pl.BlockSpec(a, lambda i, p: (0, 0))
    return pl.pallas_call(
        functools.partial(query_kernel, hd),
        grid_spec=pltpu.PrefetchScalarGridSpec(
            num_scalar_prefetch=1,
            grid=(rows // bt,),
            in_specs=[
                pl.BlockSpec((bt, width), lambda i, p: (i, 0)),
                full(mine.shape),
                full(other.shape),
                pl.BlockSpec((hd // 4, bt), lambda i, p: (0, i)),
                pl.BlockSpec((hd // 4, bt), lambda i, p: (0, i)),
            ],
            out_specs=[pl.BlockSpec((groups, per * hd, bt), lambda i, p: (0, 0, i)), full((width, qn)), token_spec()],
            scratch_shapes=[pltpu.VMEM((qn, width), bf16)],
        ),
        out_shape=[jax.ShapeDtypeStruct((groups, per * hd, rows), bf16), jax.ShapeDtypeStruct((width, qn), bf16), TOKEN],
        compiler_params=vmem(32),
        cost_estimate=pl.CostEstimate(flops=4 * rows * width * qn, bytes_accessed=4 * rows * width, transcendentals=0),
        name="other_queries",
    )(place, f, mine, other, cosT, sinT)


def mlp_kernel(first, pieces, edge, deps, place, *refs):
    s_ref, c_ref = refs[:2]
    refs = refs[2:]
    if not first:
        sT, cT = refs[:2]; refs = refs[2:]
    if pieces:
        gs, us, dn, refs = refs[:2], refs[2:4], refs[4:6], refs[6:]
    else:
        wg_ref, wu_ref, wd_ref = refs[:3]; refs = refs[3:]
    refs = refs[deps:]
    hid, gg, ug, keep = refs[:4]
    sends, refs = refs[4:7], refs[7:]
    if first:
        sT, cT = refs[:2]; refs = refs[2:]
    if pieces:
        wg_ref, wu_ref, wd_ref = refs[:3]
    token = refs[-1]
    i = pl.program_id(0)
    mark(token)
    core = place[0]
    if first:
        @pl.when(i==0)
        def _():
            sT[...] = s_ref[...].T
            cT[...] = c_ref[...].T
    if pieces:
        n4 = gs[0].shape[0]
        for k in range(2):
            at = pl.multiple_of(place[1+k]*n4, n4)
            wg_ref[pl.ds(at,n4),:] = gs[k][...]
            wu_ref[pl.ds(at,n4),:] = us[k][...]
            wd_ref[:,pl.ds(at,n4)] = dn[k][...]
    rows = s_ref.shape[0]
    width = s_ref.shape[1]
    def tile(n):
        step = rows//4
        for r in range(4):
            rs = slice(r*step,(r+1)*step)
            gate = dot(s_ref[rs,:], wg_ref[:,:n]); up = dot(s_ref[rs,:], wu_ref[:,:n])
            hg = dot_nt(c_ref[rs,:], wd_ref[:n,:])
            sig = 1.0/(1.0+jnp.exp(-gate))
            act = gate*sig
            hid[rs,:n] = (act*up).astype(bf16)
            gg[rs,:n] = (hg*up*(sig+act*(1.0-sig))).astype(bf16)
            ug[rs,:n] = (hg*act).astype(bf16)
        h = hid[:,:n]; g_ = gg[:,:n]; u_ = ug[:,:n]
        hw = width//2
        lo = pl.ds(pl.multiple_of(core*hw,hw),hw)
        away = pl.ds(pl.multiple_of((1-core)*hw,hw),hw)
        for k,(left,right) in enumerate(((sT,g_),(sT,u_),(cT,h))):
            keep[k,:,:n] = dot(left[lo,:],right).astype(bf16)
            sends[k][:,:n] = dot(left[away,:],right).astype(bf16)
    bn = wg_ref.shape[1]
    if edge == bn:
        tile(bn)
    else:
        last = pl.num_programs(0)-1
        pl.when(i<last)(lambda: tile(bn))
        pl.when(i==last)(lambda: tile(edge))

def mlp_call(place, s, c, turned, weights, base, cols, bn=256, deps=()):
    rows, width = s.shape
    pieces = len(weights)==6
    first = turned is None
    tiles = -(-cols//bn)
    edge = cols-(tiles-1)*bn
    whole = pl.BlockSpec((rows,width),lambda i,p:(0,0),pipeline_mode=pl.Buffered(1))
    wholeT = pl.BlockSpec((width,rows),lambda i,p:(0,0),pipeline_mode=pl.Buffered(1))
    wholeTo = pl.BlockSpec((width,rows),lambda i,p:(0,0))
    in_specs=[whole,whole]+([] if first else [wholeT,wholeT])
    if pieces:
        n4 = weights[0].shape[0]
        in_specs += [pl.BlockSpec((n4,bn),lambda i,p:(0,base+i))]*4 + [pl.BlockSpec((bn,n4),lambda i,p:(base+i,0))]*2
    else:
        in_specs += [pl.BlockSpec((width,bn),lambda i,p:(0,base+i))]*2 + [pl.BlockSpec((bn,width),lambda i,p:(base+i,0))]
    in_specs += [ANY]*len(deps)
    act = pl.BlockSpec((rows,bn),lambda i,p:(0,i))
    part = pl.BlockSpec((3,width//2,bn),lambda i,p:(0,0,i))
    one = pl.BlockSpec((width//2,bn),lambda i,p:(0,i))
    ones = jax.ShapeDtypeStruct((width//2,cols),bf16)
    acts = jax.ShapeDtypeStruct((rows,cols),bf16)
    parts = jax.ShapeDtypeStruct((3,width//2,cols),bf16)
    tsh = jax.ShapeDtypeStruct((width,rows),bf16)
    w_specs = [pl.BlockSpec((width,bn),lambda i,p:(0,i))]*2+[pl.BlockSpec((bn,width),lambda i,p:(i,0))] if pieces else []
    w_shapes = [jax.ShapeDtypeStruct((width,cols),bf16)]*2+[jax.ShapeDtypeStruct((cols,width),bf16)] if pieces else []
    out = pl.pallas_call(
        functools.partial(mlp_kernel,first,pieces,edge,len(deps)),
        grid_spec=pltpu.PrefetchScalarGridSpec(
            num_scalar_prefetch=1, grid=(tiles,), in_specs=in_specs,
            out_specs=[act]*3+[part]+[one]*3+([wholeTo]*2 if first else [])+w_specs+[token_spec()],
        ),
        out_shape=[acts]*3+[parts]+[ones]*3+([tsh]*2 if first else [])+w_shapes+[TOKEN],
        compiler_params=pltpu.CompilerParams(vmem_limit_bytes=56<<20),
        cost_estimate=pl.CostEstimate(flops=22*rows*width*cols,bytes_accessed=2*(4*rows*width+9*width*cols),transcendentals=rows*cols),
        name="mlp_grads",
    )(place, s, c, *(() if first else turned), *weights, *deps)
    return out


def fold_kernel(counts, sides, deps, bits, *refs):
    n = sum(counts)
    outs, token = refs[n * sides + deps : -1], refs[-1]
    mark(token)
    for side, out in enumerate(outs):
        at, col = side * n, 0
        for count in counts:
            total = None
            for ref in refs[at : at + count]:
                part = ref[0].astype(f32)
                total = part if total is None else total + part
            width = total.shape[1]
            out[:, col : col + width] = total.astype(out.dtype)
            at, col = at + count, col + width


def fold(groups, bit=None, deps=()):
    groups = [[a if isinstance(a, tuple) else (a[None], 0) for a in g] for g in groups]
    flat = [a for g in groups for a in g]
    rows = flat[0][0].shape[1]
    cols = sum(g[0][0].shape[2] for g in groups)
    sides = 1 if bit is None else 2
    rows_out = rows // sides
    step = rows_out
    while step % 32 == 0 and step * cols > 128 * 1408:
        step //= 2
    blocks = rows_out // step

    def spec(a, k, side):
        shape = (1, step, a.shape[2])
        if sides == 1:
            return pl.BlockSpec(shape, lambda i, b: (k, i, 0))
        if side == 0:
            return pl.BlockSpec(shape, lambda i, b: (k, b[0] * blocks + i, 0))
        return pl.BlockSpec(shape, lambda i, b: (k, (1 - b[0]) * blocks + i, 0))

    out = jax.ShapeDtypeStruct((rows_out, cols), bf16)
    scalars = jnp.reshape(jnp.int32(0) if bit is None else bit, (1,)).astype(jnp.int32)
    result = pl.pallas_call(
        functools.partial(fold_kernel, [len(g) for g in groups], sides, len(deps)),
        grid_spec=pltpu.PrefetchScalarGridSpec(
            num_scalar_prefetch=1,
            grid=(blocks,),
            in_specs=[spec(a, k, side) for side in range(sides) for a, k in flat] + [ANY] * len(deps),
            out_specs=[pl.BlockSpec((step, cols), lambda i, b: (i, 0))] * sides + [token_spec()],
        ),
        out_shape=[out] * sides + [TOKEN],
        compiler_params=vmem(32),
        cost_estimate=pl.CostEstimate(
            flops=3 * rows * cols, bytes_accessed=8 * rows * cols, transcendentals=0
        ),
        name="fold",
    )(scalars, *[a for _ in range(sides) for a, _ in flat], *deps)
    return result


def take_kernel(deps, place, *refs):
    refs[-2][...] = refs[0][...]
    mark(refs[-1])


def take(w, at, axis, parts, deps=()):
    shape = list(w.shape)
    shape[axis] //= parts
    block = tuple(shape)
    where = (lambda i, p: (p[0], 0)) if axis == 0 else (lambda i, p: (0, p[0]))
    return pl.pallas_call(
        functools.partial(take_kernel, len(deps)),
        grid_spec=pltpu.PrefetchScalarGridSpec(
            num_scalar_prefetch=1,
            grid=(1,),
            in_specs=[pl.BlockSpec(block, where)] + [pl.BlockSpec(memory_space=pl.ANY)] * len(deps),
            out_specs=[pl.BlockSpec(block, lambda i, p: (0, 0)), token_spec()],
        ),
        out_shape=[jax.ShapeDtypeStruct(block, w.dtype), TOKEN],
        compiler_params=vmem(32),
        cost_estimate=pl.CostEstimate(flops=0, bytes_accessed=4 * block[0] * block[1], transcendentals=0),
        name="take",
    )(jnp.reshape(at, (1,)).astype(jnp.int32), w, *deps)


def hold(x, dep):
    return pl.pallas_call(
        lambda a, b, c: None,
        in_specs=[ANY, ANY],
        out_specs=ANY,
        out_shape=jax.ShapeDtypeStruct(x.shape, x.dtype),
        input_output_aliases={0: 0},
        name="hold",
    )(x, dep)


def gather_kernel(turn, n, order, *refs):
    out, token = refs[-2:]
    mark(token)
    for k in range(n):

        @pl.when(pl.program_id(0) == k)
        def _():
            piece = refs[k][...]
            out[...] = (piece.T if turn else piece).astype(f32)


def gathered(pieces, order, turn, deps=(), start=0, cols=None):
    n = len(pieces)
    rows = pieces[0].shape[0]
    cols = cols or pieces[0].shape[1]
    base = start // cols
    total = n * rows
    return pl.pallas_call(
        functools.partial(gather_kernel, turn, n),
        grid_spec=pltpu.PrefetchScalarGridSpec(
            num_scalar_prefetch=1,
            grid=(n,),
            in_specs=[pl.BlockSpec((rows, cols), lambda i, o: (0, base), pipeline_mode=pl.Buffered(1))] * n
            + [ANY] * len(deps),
            out_specs=[
                pl.BlockSpec((cols, rows), lambda i, o: (0, o[i])) if turn else pl.BlockSpec((rows, cols), lambda i, o: (o[i], 0)),
                token_spec(),
            ],
        ),
        out_shape=[jax.ShapeDtypeStruct((cols, total) if turn else (total, cols), f32), TOKEN],
        compiler_params=vmem(60),
        cost_estimate=pl.CostEstimate(flops=0, bytes_accessed=6 * total * cols, transcendentals=0),
        name="gathered",
    )(order, *pieces, *deps)


def gather_tiles_kernel(turn, n, order, *refs):
    out = refs[-1] if not turn else refs[-2]
    held = refs[-1]
    rows = refs[0].shape[0]
    for k in range(n):
        at = pl.ds(pl.multiple_of(order[k] * rows, rows), rows)
        held[at, :] = refs[k][...].astype(held.dtype)
    if turn:
        out[...] = held[...].T.astype(f32)


def gathered_tiles(pieces, order, turn, deps, start, cols, wide=256):
    n = len(pieces)
    rows = pieces[0].shape[0]
    base = start // wide
    total = n * rows
    return pl.pallas_call(
        functools.partial(gather_tiles_kernel, turn, n),
        grid_spec=pltpu.PrefetchScalarGridSpec(
            num_scalar_prefetch=1,
            grid=(cols // wide,),
            in_specs=[pl.BlockSpec((rows, wide), lambda i, o: (0, base + i))] * n + [ANY] * len(deps),
            out_specs=pl.BlockSpec((wide, total), lambda i, o: (i, 0))
            if turn
            else pl.BlockSpec((total, wide), lambda i, o: (0, i)),
            scratch_shapes=[pltpu.VMEM((total, wide), bf16)] if turn else [],
        ),
        out_shape=jax.ShapeDtypeStruct((cols, total) if turn else (total, cols), f32),
        compiler_params=vmem(32),
        cost_estimate=pl.CostEstimate(flops=0, bytes_accessed=6 * total * cols, transcendentals=0),
        name="gathered",
    )(order, *pieces, *deps)


def gather_small_kernel(n, kn, half, deps, order, *refs):
    pieces, refs = refs[:n], refs[n + deps :]
    kv, rope, gains, held = refs
    rows = pieces[0].shape[0]
    for k, piece in enumerate(pieces):
        at = pl.ds(pl.multiple_of(order[k] * rows, rows), rows)
        kv[at, :] = piece[:, :kn].astype(f32)
        held[at, :] = piece[:, kn:].astype(f32)
    rope[...] = held[:, :half]
    gains[...] = held[...].T[half : half + 8, :]


def gathered_small(pieces, order, kn, half, deps=(), start=0):
    n = len(pieces)
    rows, cols = pieces[0].shape[0], kn + 128
    base = start // cols
    total = n * rows
    full = lambda a: pl.BlockSpec(a, lambda i, o: (0, 0))
    shapes = [(total, kn), (total, half), (8, total)]
    return pl.pallas_call(
        functools.partial(gather_small_kernel, n, kn, half, len(deps)),
        grid_spec=pltpu.PrefetchScalarGridSpec(
            num_scalar_prefetch=1,
            grid=(1,),
            in_specs=[pl.BlockSpec((rows, cols), lambda i, o: (0, base))] * n + [ANY] * len(deps),
            out_specs=[full(a) for a in shapes],
            scratch_shapes=[pltpu.VMEM((total, 128), f32)],
        ),
        out_shape=[jax.ShapeDtypeStruct(a, f32) for a in shapes],
        compiler_params=vmem(32),
        cost_estimate=pl.CostEstimate(flops=0, bytes_accessed=6 * total * cols, transcendentals=0),
        name="gathered_small",
    )(order, *pieces, *deps)


def wgrad_kernel(n, deps, place, l_ref, *refs):
    right, refs = refs[:n], refs[n + deps :]
    keep, send, token, lT = refs
    mark(token)
    lT[...] = l_ref[...].T
    core = place[0]
    hw = keep.shape[0]
    for out, side in ((send, 1 - core), (keep, core)):
        rows = lT[pl.ds(pl.multiple_of(side * hw, hw), hw), :]
        at = 0
        for r in right:
            k = r.shape[-2]
            out[:, at : at + k] = dot_nt(rows, r[...].reshape(r.shape[-2:])).astype(bf16)
            at += k


def wgrad(place, left, right, deps=()):
    rows, width = left.shape
    right = [r if isinstance(r, tuple) else (r[None], 0) for r in right]
    cols = sum(r.shape[1] for r, _ in right)
    full = lambda a: pl.BlockSpec(a, lambda i, p: (0, 0))
    part = jax.ShapeDtypeStruct((width // 2, cols), bf16)

    def spec(r, k):
        return pl.BlockSpec((1, *r.shape[1:]), lambda i, p: (k, 0, 0))

    return pl.pallas_call(
        functools.partial(wgrad_kernel, len(right), len(deps)),
        grid_spec=pltpu.PrefetchScalarGridSpec(
            num_scalar_prefetch=1,
            grid=(1,),
            in_specs=[full(left.shape)] + [spec(r, k) for r, k in right] + [ANY] * len(deps),
            out_specs=[full(part.shape)] * 2 + [token_spec()],
            scratch_shapes=[pltpu.VMEM((width, rows), bf16)],
        ),
        out_shape=[part] * 2 + [TOKEN],
        compiler_params=vmem(48),
        cost_estimate=pl.CostEstimate(flops=4 * rows * width * cols, bytes_accessed=4 * rows * width, transcendentals=0),
        name="weight_grads",
    )(place, left, *[r for r, _ in right], *deps)


def back_kernel(n, *refs):
    tgs, sgs = refs[:n], refs[n : 2 * n]
    out, token = refs[-2:]
    mark(token)
    per, hd, _ = tgs[0].shape
    for g in range(n * per):
        out[g * hd : (g + 1) * hd, :] = tgs[g // per][g % per].astype(bf16)
    total = sgs[0][...]
    for s in sgs[1:]:
        total = total + s[...]
    out[n * per * hd :, :] = total.astype(bf16)


def back_call(tgs, sgs, deps=()):
    n = len(tgs)
    per, hd, two = tgs[0].shape
    rows = two // 2
    total = n * per * hd + hd // 2
    return pl.pallas_call(
        functools.partial(back_kernel, n),
        grid=(1,),
        in_specs=[pl.BlockSpec((per, hd, rows), lambda i: (0, 0, 0))] * n
        + [pl.BlockSpec((hd // 2, rows), lambda i: (0, 0))] * n
        + [ANY] * len(deps),
        out_specs=[pl.BlockSpec((total, rows), lambda i: (0, 0)), token_spec()],
        out_shape=[jax.ShapeDtypeStruct((total, rows), bf16), TOKEN],
        compiler_params=vmem(32),
        cost_estimate=pl.CostEstimate(flops=0, bytes_accessed=6 * total * rows, transcendentals=0),
        name="partner_key_grads",
    )(*tgs, *sgs, *deps)


def own_kernel(n, *refs):
    tgs, sgs = refs[: 2 * n], refs[2 * n : 4 * n]
    back_a, back_b, cos_ref, sin_ref = refs[4 * n : 4 * n + 4]
    out, token = refs[-2:]
    mark(token)
    per, hd, _ = tgs[0].shape
    kv = n * per * hd
    for k in range(2 * n * per):
        back = (back_a, back_b)[k // (n * per)]
        at = k % (n * per) * hd
        mine = tgs[k // per][k % per]
        out[k * hd : (k + 1) * hd, :] = (mine + back[at : at + hd, :].astype(f32)).astype(bf16)
    total = back_a[kv:, :].astype(f32) + back_b[kv:, :].astype(f32)
    for s in sgs:
        total = total + s[...]
    out[2 * kv :, :] = turned_rows(total, cos_ref[...], -sin_ref[...], hd // 4).astype(bf16)


def own_call(tgs, sgs, backs, cosT, sinT, deps=()):
    n = len(tgs)
    per, hd, two = tgs[0].shape
    rows = two // 2
    total = n * per * hd + hd // 2
    full = lambda a: pl.BlockSpec(a.shape, lambda i: (0, 0))
    return pl.pallas_call(
        functools.partial(own_kernel, n // 2),
        grid=(1,),
        in_specs=[pl.BlockSpec((per, hd, rows), lambda i: (0, 0, 1))] * n
        + [pl.BlockSpec((hd // 2, rows), lambda i: (0, 1))] * n
        + [full(backs[0]), full(backs[1]), full(cosT), full(sinT)]
        + [ANY] * len(deps),
        out_specs=[pl.BlockSpec((total, rows), lambda i: (0, 0)), token_spec()],
        out_shape=[jax.ShapeDtypeStruct((total, rows), bf16), TOKEN],
        compiler_params=vmem(32),
        cost_estimate=pl.CostEstimate(flops=0, bytes_accessed=8 * total * rows, transcendentals=0),
        name="own_key_grads",
    )(*tgs, *sgs, *backs, cosT, sinT, *deps)


def post_kernel(deps, x_ref, mg_ref, gain_ref, kv_ref, wqa, wqb, wka, wkb, wr, *refs):
    dqs = refs[:2]
    out, gain_out = refs[2 + deps :]
    kn = wka.shape[1]
    hn = wqa.shape[1]
    qa = dqs[0][...].reshape(hn, -1).T
    qb = dqs[1][...].reshape(hn, -1).T
    kv = kv_ref[...]
    first = dot_nt(qa, wqa[...]) + dot_nt(qb, wqb[...])
    first = first + dot_nt(kv[:kn].T, wka[...]) + dot_nt(kv[kn : 2 * kn].T, wkb[...])
    first = first + dot_nt(kv[2 * kn :].T, wr[...])
    x = x_ref[...].astype(f32)
    factor = lax.rsqrt(jnp.mean(x * x, axis=-1, keepdims=True) + eps_norm)
    normed = x * factor
    inner = first * gain_ref[...]
    back = factor * (inner - normed * jnp.mean(inner * normed, axis=-1, keepdims=True))
    out[...] = (mg_ref[...] + back).astype(bf16)

    @pl.when(pl.program_id(0) == 0)
    def _():
        gain_out[...] = jnp.zeros_like(gain_out)

    gain_out[...] += jnp.sum(first * normed, axis=0, keepdims=True)


def post_call(x, middle_grad, gain, kv, weights, dqs, deps=(), bt=256):
    rows, width = x.shape
    full = lambda a: pl.BlockSpec(a.shape, lambda i: (0, 0), pipeline_mode=pl.Buffered(1))
    row = pl.BlockSpec((bt, width), lambda i: (i, 0))
    one = pl.BlockSpec((1, width), lambda i: (0, 0))
    return pl.pallas_call(
        functools.partial(post_kernel, len(deps)),
        grid=(rows // bt,),
        in_specs=[row, row, one, pl.BlockSpec((kv.shape[0], bt), lambda i: (0, i))]
        + [full(w) for w in weights]
        + [pl.BlockSpec((*d.shape[:2], bt), lambda i: (0, 0, i)) for d in dqs]
        + [ANY] * len(deps),
        out_specs=[row, one],
        out_shape=[jax.ShapeDtypeStruct((rows, width), bf16), jax.ShapeDtypeStruct((1, width), f32)],
        compiler_params=vmem(40),
        cost_estimate=pl.CostEstimate(flops=5 * rows * width * width, bytes_accessed=16 * rows * width, transcendentals=0),
        name="token_grads",
    )(x, middle_grad, gain[None, :], kv, *weights, *dqs, *deps)


def small_kernel(kn, half, place, f_ref, kv_ref, gain_a, gain_b, keep_a, send_a, keep_b, send_b, token, lT, rows_s, rows_g):
    mark(token)
    lT[...] = f_ref[...].T
    rows_s[...] = jnp.zeros_like(rows_s)
    rows_s[:half, :] = kv_ref[2 * kn :, :]
    rows_g[...] = jnp.zeros_like(rows_g)
    rows_g[half : half + 1, :] = gain_a[...]
    rows_g[half + 1 : half + 2, :] = gain_b[...]
    gains = rows_g[...].T
    rows_g_ref = rows_g
    core = place[0]
    hw = keep_a.shape[0]
    rope = dot_nt(lT[...], rows_s[...]) + gains
    lT_rows = [lT[:hw, :], lT[hw:, :]]
    first = core == 0
    for (a, b), side in (((send_a, send_b), 1), ((keep_a, keep_b), 0)):
        low = jnp.logical_xor(first, side == 1)
        rows = jnp.where(low, lT_rows[0], lT_rows[1])
        small = jnp.where(low, rope[:hw], rope[hw:]).astype(bf16)
        a[:, :kn] = dot_nt(rows, kv_ref[:kn, :]).astype(bf16)
        a[:, kn:] = small
        b[:, :kn] = dot_nt(rows, kv_ref[kn : 2 * kn, :]).astype(bf16)
        b[:, kn:] = small


def small_call(place, f, kv, gain_a, gain_b, kn, half):
    rows, width = f.shape
    full = lambda a: pl.BlockSpec(a, lambda i, p: (0, 0))
    part = jax.ShapeDtypeStruct((width // 2, kn + 128), bf16)
    return pl.pallas_call(
        functools.partial(small_kernel, kn, half),
        grid_spec=pltpu.PrefetchScalarGridSpec(
            num_scalar_prefetch=1,
            grid=(1,),
            in_specs=[full(f.shape), full(kv.shape), full((1, width)), full((1, width))],
            out_specs=[full(part.shape)] * 4 + [token_spec()],
            scratch_shapes=[pltpu.VMEM((width, rows), bf16), pltpu.VMEM((128, rows), bf16), pltpu.VMEM((128, width), f32)],
        ),
        out_shape=[part] * 4 + [TOKEN],
        compiler_params=vmem(48),
        cost_estimate=pl.CostEstimate(flops=2 * rows * width * 512, bytes_accessed=3 * rows * width, transcendentals=0),
        name="small_grads",
    )(place, f, kv, gain_a, gain_b)


def rms_parts(values):
    factor = lax.rsqrt(jnp.mean(values * values, axis=-1, keepdims=True) + eps_norm)
    return values * factor, factor


def norm_back(grad, normed, factor, gain):
    inner = grad * gain
    return factor * (inner - normed * jnp.mean(inner * normed, axis=-1, keepdims=True))


def mm(a, b, ca, cb):
    return lax.dot_general(a, b, (((ca,), (cb,)), ((), ())), preferred_element_type=f32)


def swap(x, axis, bit):
    n = lax.axis_size(axis)
    return lax.ppermute(x, axis, [(i, i ^ bit) for i in range(n)])


def joined(mine, other, bit):
    first = bit == 0
    return jnp.concatenate([jnp.where(first, mine, other), jnp.where(first, other, mine)], axis=0)


class Order:
    def __init__(self, first):
        self.last = first

    def after(self, out):
        *out, self.last = out
        return out if len(out) > 1 else out[0]

    def fold(self, groups, bit=None, deps=()):
        return self.after(fold(groups, bit, (self.last, *deps)))


def spread(piece, steps):
    pieces = [piece]
    for step in steps:
        pieces = pieces + [swap(p, "dp", step) for p in pieces]
    return pieces


def piece_order(bits):
    order = [jnp.int32(0)]
    for bit in bits:
        order = [2 * o + b for o in order for b in (bit, 1 - bit)]
    return jnp.stack(order).astype(jnp.int32)


class Sum:
    def __init__(self, run, bits):
        self.run, self.bits, self.steps = run, bits, [1]

    def x(self, groups):
        self.keep, send = self.run.fold(groups, self.bits[1])
        self.got = swap(send, "dp", 2)
        self.steps = [2, 1]

    def z(self):
        self.start([[self.keep, self.got]])

    def start(self, groups):
        self.keep, send = self.run.fold(groups, self.bits[2])
        self.got = swap(send, "dp", 4)
        self.steps = [4, 2, 1]

    def line(self, step=8):
        self.keep = self.run.fold([[self.keep, self.got]])
        self.got = swap(self.keep, "dp", step)

    def end(self, deps=()):
        step = 16
        while step < lax.axis_size("dp"):
            self.line(step)
            step *= 2
        self.keep = self.run.fold([[self.keep, self.got]], None, deps)
        self.pieces = spread(self.keep, self.steps)
        self.order = piece_order(self.bits[: len(self.steps)])


def body(tokens, lengths, attn_gain, w_query, w_kv, w_rope, w_out, mlp_gain, w_gate, w_up, w_down, out_grad):
    rows, width = tokens.shape
    shards = lax.axis_size("tensor")
    t = lax.axis_index("tensor")
    index = lax.axis_index("dp")
    bits = (index & 1, (index >> 1) & 1, (index >> 2) & 1)
    core = bits[0]
    half = w_rope.shape[1]
    hd = 2 * half
    kv_own = w_kv.shape[1]
    q_own = w_query.shape[1]
    groups = kv_own // hd
    per = q_own // kv_own
    ff = w_gate.shape[1]
    own0 = rows
    bq_f, bk_f, bq_b, bk_b = 256, 256, 512, 256
    place = jnp.stack([core, core, 1 - core]).astype(jnp.int32)

    kv_piece, taken = take(w_kv, core, 0, 2)
    kv_got = swap(kv_piece, "tensor", 1)
    q_piece, taken = take(w_query, core, 0, 2, (taken,))
    q_got = swap(q_piece, "tensor", 1)
    out_piece, taken = take(w_out, core, 0, 2, (taken,))
    out_got = swap(out_piece, "tensor", 1)

    slot, position, valid, start, bounds_f = local_layout(lengths[0], t, rows, bq_f, bk_f, own0)
    bounds_b = local_layout(lengths[0], t, rows, bq_b, bk_b, own0)[4]
    quarter = half // 2
    freq = 10000.0 ** (-jnp.arange(quarter, dtype=f32) / quarter)
    angle = freq[:, None] * position[None, :]
    cosT, sinT = jnp.cos(angle), jnp.sin(angle)

    first_in, tied_a, shared, q_a = pre_call(tokens, attn_gain, w_kv, w_rope, w_query, cosT, sinT, hd, per)
    sent, w_kv_o = kv_call(place, first_in, kv_got, swap(kv_got, "dp", 1), tied_a, shared)
    got = lax.ppermute(sent, "tensor", [(i, i + 1) for i in range(shards - 1)])
    q_b, w_query_o, q_done = query_call(place, first_in, q_got, swap(q_got, "dp", 1), cosT, sinT, hd, groups, per)
    gate_piece, taken = take(w_gate, core, 0, 2, (got, q_done))
    gate_got = swap(gate_piece, "tensor", 1)
    up_piece, taken = take(w_up, core, 0, 2, (taken,))
    up_got = swap(up_piece, "tensor", 1)
    down_piece, taken = take(w_down, core, 1, 2, (taken,))
    down_got = swap(down_piece, "tensor", 1)

    def both(p):
        return p, swap(p, "dp", 1)

    w_out_o = joined(out_got, swap(out_got, "dp", 1), core)
    mixed_a, mixed_b, lse_a, lse_b = attn_fwd(
        bounds_f, start, q_a, q_b, sent, got, hd, bq_f, bk_f, (taken, w_out_o)
    )
    mix_a, mix_b = mixed_a.reshape(-1, rows), mixed_b.reshape(-1, rows)
    inputs = tokens.astype(f32)
    middle = inputs + mm(mix_a, w_out, 0, 0) + mm(mix_b, w_out_o, 0, 0)
    normed_two, factor_two = rms_parts(middle)
    second_in = (normed_two * mlp_gain).astype(bf16)

    hid_a, gg_a, ug_a, keep_a, *send_a, in_T, back_T, done_a = mlp_call(
        place, second_in, out_grad, None, (w_gate, w_up, w_down), 0, ff
    )
    core_a = [swap(s, "dp", 1) for s in send_a]
    gates, ups, downs = both(hold(gate_got, done_a)), both(hold(up_got, done_a)), both(hold(down_got, done_a))
    second_a = mm(gg_a, w_gate, 1, 1) + mm(ug_a, w_up, 1, 1)
    hid_b, gg_b, ug_b, keep_b, *send_b, w_gate_o, w_up_o, w_down_o, done_b = mlp_call(
        place, second_in, out_grad, (in_T, back_T), (*gates, *ups, *downs), 0, ff, deps=(second_a,)
    )
    core_b = [swap(s, "dp", 1) for s in send_b]
    run = Order(done_b)
    gate_y = swap(run.fold([[(keep_b, 0), core_b[0]]]), "tensor", 1)
    gg_b, ug_b = hold(gg_b, run.last), hold(ug_b, run.last)
    second_grad = second_a + mm(gg_b, w_gate_o, 1, 1) + mm(ug_b, w_up_o, 1, 1)
    mlp_gain_part = jnp.sum(second_grad * normed_two, axis=0, keepdims=True)
    middle_grad = out_grad.astype(f32) + norm_back(second_grad, normed_two, factor_two, mlp_gain)
    attn_back = middle_grad.astype(bf16)
    live = valid[None, :].astype(bf16)
    mixed_grad_b = (mm(w_out_o, attn_back, 1, 1).astype(bf16) * live).reshape(mixed_b.shape)
    mixed_grad_a = (mm(w_out, attn_back, 1, 1).astype(bf16) * live).reshape(mixed_a.shape)

    def parts(x):
        return [(x, k) for k in range(groups)]

    def back(q, mixed, lse, grad, side, deps=()):
        return run.after(
            attn_bwd(
                bounds_b, start, q, sent, got, mixed, lse, grad, cosT, sinT, hd, side, 0, groups, bq_b, bk_b,
                (run.last, *deps),
            )
        )

    wo_keep_b, wo_send_b = run.after(wgrad(place, attn_back, parts(mixed_b), (run.last,)))
    wo_core_b = swap(wo_send_b, "dp", 1)
    wo_keep_a, wo_send_a = run.after(wgrad(place, attn_back, parts(mixed_a), (run.last,)))
    wo_core_a = swap(wo_send_a, "dp", 1)
    up_y = swap(run.fold([[(keep_b, 1), core_b[1]]]), "tensor", 1)
    down_kb, down_sb = run.fold([[(keep_b, 2), core_b[2]]], bits[1])
    down_xb = swap(down_sb, "dp", 2)
    down_ka, down_sa = run.fold([[(keep_a, 2), core_a[2]]], bits[1])
    down_xa = swap(down_sa, "dp", 2)
    gate_s, up_s, down_s, rest_s = (Sum(run, bits) for _ in range(4))
    dq_b, tg_b, sg_b = back(q_b, mixed_b, lse_b, mixed_grad_b, 1, (mixed_grad_a,))
    wq_keep_b, wq_send_b = run.after(wgrad(place, first_in, parts(dq_b), (run.last,)))
    wq_core_b = swap(wq_send_b, "dp", 1)
    key_b = run.after(back_call((tg_b,), (sg_b,), (run.last,)))
    to_lower = [(i + 1, i) for i in range(shards - 1)]
    key_got_a = lax.ppermute(key_b, "tensor", to_lower)
    gate_s.x([[(keep_a, 0), core_a[0], gate_y]])
    up_s.x([[(keep_a, 1), core_a[1], up_y]])
    down_y = swap(run.fold([[down_kb, down_xb]]), "tensor", 1)
    wo_y = swap(run.fold([[wo_keep_b, wo_core_b]]), "tensor", 1)
    wq_y = swap(run.fold([[wq_keep_b, wq_core_b]]), "tensor", 1)
    dq_a, tg_a, sg_a = back(q_a, mixed_a, lse_a, mixed_grad_a, 0)
    key_a = run.after(back_call((tg_a,), (sg_a,), (run.last,)))
    key_got_b = lax.ppermute(key_a, "tensor", to_lower)
    gate_s.z()
    up_s.z()
    down_s.start([[down_ka, down_xa, down_y]])
    wq_keep_a, wq_send_a = run.after(wgrad(place, first_in, parts(dq_a), (run.last,)))
    wq_core_a = swap(wq_send_a, "dp", 1)
    kv_grad = run.after(own_call((tg_a, tg_b), (sg_a, sg_b), (key_got_a, key_got_b), cosT, sinT, (run.last,)))
    tokens_grad, attn_gain_part = post_call(
        tokens, middle_grad, attn_gain, kv_grad, (w_query, w_query_o, w_kv, w_kv_o, w_rope), (dq_a, dq_b), (run.last,)
    )
    run.last = attn_gain_part
    sm_keep_a, sm_send_a, sm_keep_b, sm_send_b = run.after(
        small_call(place, first_in, kv_grad, attn_gain_part, mlp_gain_part, kv_own, half)
    )
    sm_core_b = swap(sm_send_b, "dp", 1)
    sm_core_a = swap(sm_send_a, "dp", 1)
    gate_s.line()
    sm_y = swap(run.fold([[sm_keep_b, sm_core_b]]), "tensor", 1)
    up_s.line()
    rest_s.x([[wo_keep_a, wo_core_a, wo_y], [wq_keep_a, wq_core_a, wq_y], [sm_keep_a, sm_core_a, sm_y]])
    hid_a, hid_b = hold(hid_a, run.last), hold(hid_b, run.last)
    layer_out = (middle + mm(hid_a, w_down, 1, 0) + mm(hid_b, w_down_o, 1, 0)).astype(bf16)

    gate_s.end((layer_out,))
    rest_s.z()
    up_s.end()
    down_s.line()
    rest_s.line()
    gate_sum = run.after(gathered(gate_s.pieces, gate_s.order, False, (run.last,)))
    down_s.end()
    rest_s.end()
    up_sum = run.after(gathered(up_s.pieces, up_s.order, False, (run.last,)))
    down_sum = run.after(gathered(down_s.pieces, down_s.order, True, (run.last,)))
    kv_sum, rope_sum, gains = gathered_small(rest_s.pieces, rest_s.order, kv_own, half, (run.last,), 2 * q_own)
    out_sum = gathered_tiles(rest_s.pieces, rest_s.order, True, (run.last,), 0, q_own)
    query_sum = gathered_tiles(rest_s.pieces, rest_s.order, False, (run.last,), q_own, q_own)
    return (
        layer_out,
        tokens_grad,
        gains[0],
        query_sum,
        kv_sum,
        rope_sum,
        out_sum,
        gains[1],
        gate_sum,
        up_sum,
        down_sum,
    )


def solution(mesh):
    rows = P(("dp", "tensor"), None)
    columns = P(None, "tensor")
    down = P("tensor", None)
    return jax.shard_map(
        body,
        mesh=mesh,
        in_specs=(rows, P("dp", None), P(), columns, columns, P(), down, P(), columns, columns, down, rows),
        out_specs=(rows, rows, P(), columns, columns, P(), down, P(), columns, columns, down),
        check_vma=False,
    )
```

```python
import functools

import jax
import jax.numpy as jnp
from jax import lax
from jax.experimental import pallas as pl
from jax.experimental.pallas import tpu as pltpu
from jax.sharding import PartitionSpec as P

eps_norm = 1e-05
masked_score = -1e30
f32 = jnp.float32
bf16 = jnp.bfloat16


def dot(a, b):
    return lax.dot_general(a, b, (((1,), (0,)), ((), ())), preferred_element_type=f32)


def dot_nt(a, b):
    return lax.dot_general(a, b, (((1,), (1,)), ((), ())), preferred_element_type=f32)


ANY = pl.BlockSpec(memory_space=pl.ANY)


TOKEN = jax.ShapeDtypeStruct((8, 128), f32)


def token_spec():
    return pl.BlockSpec((8, 128), lambda *a: (0, 0))


def mark(token):
    token[...] = jnp.zeros_like(token)


def vmem(mib):
    return pltpu.CompilerParams(vmem_limit_bytes=mib << 20)


def block_loops(bounds, i, step):
    k0, k1, k2, k3 = (bounds[i, n] for n in range(4))
    lax.fori_loop(k0, k1, lambda kb, c: step(kb, True), None)
    lax.fori_loop(k1, k2, lambda kb, c: step(kb, False), None)
    lax.fori_loop(k2, k3, lambda kb, c: step(kb, True), None)


def allowed_tile(start, kb, bk, qpos):
    kk = lax.broadcasted_iota(jnp.int32, (bk, start.shape[1]), 0) + kb * bk
    return (kk >= start) & (kk <= qpos)


def load_keys(own, partner, sent_ref, got_ref, k, kT, vT):
    hd = kT.shape[1]
    half = hd // 2
    rows = sent_ref.shape[1]
    shared = sent_ref.shape[0] - half
    for side, (at, ref) in enumerate(((partner, got_ref), (own, sent_ref))):
        to = slice(side * rows, (side + 1) * rows)
        vT[k, :, to] = ref[at * hd : (at + 1) * hd, :]
        kT[k, :half, to] = ref[at * hd : at * hd + half, :]
        kT[k, half:, to] = ref[shared:, :]


def fwd_kernel(n, heads, bk, deps, bounds, start_ref, qa_ref, qb_ref, sent_ref, got_ref, *refs):
    oa_ref, ob_ref, lsea_ref, lseb_ref, kT, vT, ks, acc, ms, ls = refs[deps:]
    i = pl.program_id(0)
    hd = kT.shape[1]
    bq = qa_ref.shape[2]
    own0 = kT.shape[2] // 2
    width = heads * hd

    @pl.when(i == 0)
    def _():
        for k in range(2 * n):
            load_keys(k, (k + n) % (2 * n), sent_ref, got_ref, k, kT, vT)
            ks[k] = kT[k].T

    acc[...] = jnp.zeros_like(acc)
    ms[...] = jnp.full_like(ms, masked_score)
    ls[...] = jnp.zeros_like(ls)
    start = start_ref[...]
    qpos = own0 + i * bq + lax.broadcasted_iota(jnp.int32, (1, bq), 1)

    def step(kb, masked):
        rows = pl.ds(pl.multiple_of(kb * bk, bk), bk)
        if masked:
            ok = allowed_tile(start, kb, bk, qpos)
        for k in range(2 * n):
            q_ref = qa_ref if k < n else qb_ref
            kblk = ks[k, rows, :]
            vblk = vT[k, :, rows]
            h0 = k * heads
            mold = [ms[h : h + 1, :] for h in range(h0, h0 + heads)]
            lold = [ls[h : h + 1, :] for h in range(h0, h0 + heads)]
            aold = [acc[h * hd : (h + 1) * hd, :] for h in range(h0, h0 + heads)]
            ss = [dot(kblk, q_ref[k % n, j * hd : (j + 1) * hd, :]) for j in range(heads)]
            if masked:
                ss = [jnp.where(ok, s, masked_score) for s in ss]
            mnew = [jnp.maximum(m, jnp.max(s, axis=0, keepdims=True)) for m, s in zip(mold, ss)]
            ps = [jnp.exp(s - m) for s, m in zip(ss, mnew)]
            als = [jnp.exp(a - b) for a, b in zip(mold, mnew)]
            lnew = [l * al + jnp.sum(p, axis=0, keepdims=True) for l, al, p in zip(lold, als, ps)]
            anew = [a * al + dot(vblk, p.astype(bf16)) for a, al, p in zip(aold, als, ps)]
            for j in range(heads):
                h = h0 + j
                ms[h : h + 1, :] = mnew[j]
                ls[h : h + 1, :] = lnew[j]
                acc[h * hd : (h + 1) * hd, :] = anew[j]

    block_loops(bounds, i, step)
    live = start < (1 << 29)
    for h in range(2 * n * heads):
        l = ls[h : h + 1, :]
        safe = jnp.where(l > 0, l, 1.0)
        side, g, j = h // (n * heads), h // heads % n, h % heads
        o_ref, lse_ref = ((oa_ref, lsea_ref), (ob_ref, lseb_ref))[side]
        out = jnp.where(live, acc[h * hd : (h + 1) * hd, :] / safe, 0.0)
        o_ref[g, j * hd : (j + 1) * hd, :] = out.astype(bf16)
        lse_ref[g, j : j + 1, :] = ms[h : h + 1, :] + jnp.log(safe)


def attn_fwd(bounds, start, qa, qb, sent, got, hd, bq, bk, deps=()):
    n, width, rows = qa.shape
    heads = width // hd
    tile = pl.BlockSpec((n, width, bq), lambda i, b: (0, 0, i))
    logs = pl.BlockSpec((n, heads, bq), lambda i, b: (0, 0, i))
    kv = pl.BlockSpec(sent.shape, lambda i, b: (0, 0), pipeline_mode=pl.Buffered(1))
    return pl.pallas_call(
        functools.partial(fwd_kernel, n, heads, bk, len(deps)),
        grid_spec=pltpu.PrefetchScalarGridSpec(
            num_scalar_prefetch=1,
            grid=(rows // bq,),
            in_specs=[pl.BlockSpec((1, bq), lambda i, b: (0, i)), tile, tile, kv, kv] + [ANY] * len(deps),
            out_specs=[tile, tile, logs, logs],
            scratch_shapes=[
                pltpu.VMEM((2 * n, hd, 2 * rows), bf16),
                pltpu.VMEM((2 * n, hd, 2 * rows), bf16),
                pltpu.VMEM((2 * n, 2 * rows, hd), bf16),
                pltpu.VMEM((2 * n * width, bq), f32),
                pltpu.VMEM((2 * n * heads, bq), f32),
                pltpu.VMEM((2 * n * heads, bq), f32),
            ],
        ),
        out_shape=[jax.ShapeDtypeStruct((n, width, rows), bf16)] * 2
        + [jax.ShapeDtypeStruct((n, heads, rows), f32)] * 2,
        compiler_params=vmem(60),
        cost_estimate=pl.CostEstimate(
            flops=96 * n * width * rows * rows, bytes_accessed=8 * n * width * rows, transcendentals=0
        ),
        name="attn_fwd",
    )(bounds, start, qa, qb, sent, got, *deps)


def bwd_kernel(
    n, first, partner, heads, bk, scale, deps, bounds, start_ref, q_ref, o_ref, lse_ref, do_ref, cos_ref, sin_ref,
    sent_ref, got_ref, *refs
):
    dq_ref, tg_ref, sg_ref, token, kT, vT, ks, vs, dk, dv, dqa, dl = refs[deps:]
    mark(token)
    i = pl.program_id(0)
    hd = kT.shape[1]
    half = hd // 2
    quarter = hd // 4
    bq = q_ref.shape[2]
    own0 = kT.shape[2] // 2

    @pl.when(i == 0)
    def _():
        for g in range(n):
            load_keys(first + g, partner + g, sent_ref, got_ref, g, kT, vT)
            ks[g] = kT[g].T
            vs[g] = vT[g].T
        dk[...] = jnp.zeros_like(dk)
        dv[...] = jnp.zeros_like(dv)

    dqa[...] = jnp.zeros_like(dqa)
    sls = [slice(j * hd, (j + 1) * hd) for j in range(heads)]
    for g in range(n):
        for j, sl in enumerate(sls):
            prod = do_ref[g, sl, :].astype(f32) * o_ref[g, sl, :].astype(f32)
            dl[g * heads + j : g * heads + j + 1, :] = jnp.sum(prod, axis=0, keepdims=True)
    start = start_ref[...]
    qpos = own0 + i * bq + lax.broadcasted_iota(jnp.int32, (1, bq), 1)

    def step(kb, masked):
        rows = pl.ds(pl.multiple_of(kb * bk, bk), bk)
        if masked:
            ok = allowed_tile(start, kb, bk, qpos)
        for g in range(n):
            kblk = ks[g, rows, :]
            vblk = vs[g, rows, :]
            kTb = kT[g, :, rows]
            dvt = dv[g, :, rows]
            dkt = dk[g, :, rows]
            qs = [q_ref[g, sl, :] for sl in sls]
            dos = [do_ref[g, sl, :] for sl in sls]
            lses = [lse_ref[g, j : j + 1, :] for j in range(heads)]
            dls = [dl[g * heads + j : g * heads + j + 1, :] for j in range(heads)]
            dqs = [dqa[g, sl, :] for sl in sls]
            new = []
            for j in range(heads):
                s = dot(kblk, qs[j])
                if masked:
                    s = jnp.where(ok, s, masked_score)
                p = jnp.exp(s - lses[j])
                dp = dot(vblk, dos[j])
                ds = (p * (dp - dls[j])).astype(bf16)
                dvt = dvt + dot_nt(dos[j], p.astype(bf16))
                dkt = dkt + dot_nt(qs[j], ds)
                new.append(dqs[j] + dot(kTb, ds))
            for sl, x in zip(sls, new):
                dqa[g, sl, :] = x
            dv[g, :, rows] = dvt
            dk[g, :, rows] = dkt

    block_loops(bounds, i, step)
    cosv = cos_ref[...]
    sinv = sin_ref[...]
    for g in range(n):
        for sl in sls:
            x = dqa[g, sl, :] * scale
            a, b = x[half : half + quarter], x[half + quarter :]
            turned = jnp.concatenate([x[:half], a * cosv + b * sinv, b * cosv - a * sinv], axis=0)
            dq_ref[g, sl, :] = turned.astype(bf16)

    @pl.when(i == pl.num_programs(0) - 1)
    def _():
        for g in range(n):
            tg_ref[g, :half, :] = dv[g, :half, :] + dk[g, :half, :]
            tg_ref[g, half:, :] = dv[g, half:, :]
        total = dk[0, half:, :]
        for g in range(1, n):
            total = total + dk[g, half:, :]
        sg_ref[...] = total


def attn_bwd(bounds, start, q, sent, got, o, lse, do, cosT, sinT, hd, side, g0, n, bq, bk, deps=()):
    groups, width, rows = q.shape
    first, partner = side * groups + g0, (1 - side) * groups + g0
    heads = width // hd
    tile = pl.BlockSpec((n, width, bq), lambda i, b: (g0 // n, 0, i))
    out = pl.BlockSpec((n, width, bq), lambda i, b: (0, 0, i))
    angle = pl.BlockSpec((hd // 4, bq), lambda i, b: (0, i))
    kv = pl.BlockSpec(sent.shape, lambda i, b: (0, 0), pipeline_mode=pl.Buffered(1))
    return pl.pallas_call(
        functools.partial(bwd_kernel, n, first, partner, heads, bk, hd**-0.5, len(deps)),
        grid_spec=pltpu.PrefetchScalarGridSpec(
            num_scalar_prefetch=1,
            grid=(rows // bq,),
            in_specs=[
                pl.BlockSpec((1, bq), lambda i, b: (0, i)),
                tile,
                tile,
                pl.BlockSpec((n, heads, bq), lambda i, b: (g0 // n, 0, i)),
                tile,
                angle,
                angle,
                kv,
                kv,
            ]
            + [ANY] * len(deps),
            out_specs=[
                out,
                pl.BlockSpec((n, hd, 2 * rows), lambda i, b: (0, 0, 0)),
                pl.BlockSpec((hd // 2, 2 * rows), lambda i, b: (0, 0)),
                token_spec(),
            ],
            scratch_shapes=[
                pltpu.VMEM((n, hd, 2 * rows), bf16),
                pltpu.VMEM((n, hd, 2 * rows), bf16),
                pltpu.VMEM((n, 2 * rows, hd), bf16),
                pltpu.VMEM((n, 2 * rows, hd), bf16),
                pltpu.VMEM((n, hd, 2 * rows), f32),
                pltpu.VMEM((n, hd, 2 * rows), f32),
                pltpu.VMEM((n, width, bq), f32),
                pltpu.VMEM((n * heads, bq), f32),
            ],
        ),
        out_shape=[
            jax.ShapeDtypeStruct((n, width, rows), bf16),
            jax.ShapeDtypeStruct((n, hd, 2 * rows), f32),
            jax.ShapeDtypeStruct((hd // 2, 2 * rows), f32),
            TOKEN,
        ],
        compiler_params=vmem(60),
        cost_estimate=pl.CostEstimate(
            flops=90 * n * width * rows * rows, bytes_accessed=8 * n * width * rows, transcendentals=0
        ),
        name="attn_bwd",
    )(bounds, start, q, o, lse, do, cosT, sinT, sent, got, *deps)


def local_layout(lengths_row, t, rows, bq, bk, own0):
    slot = t * rows + jnp.arange(rows, dtype=jnp.int32)
    ends = jnp.cumsum(lengths_row)
    passed = (slot[:, None] >= ends[None, :]).astype(jnp.int32)
    begin = jnp.sum(passed * lengths_row[None, :], axis=1)
    valid = slot < ends[-1]
    shift = own0 - t * rows
    start = jnp.where(valid, begin + shift, 1 << 30)
    nqb = rows // bq
    first = begin.reshape(nqb, bq)[:, 0] + shift
    last_start = jnp.max(jnp.where(valid, begin + shift, 0).reshape(nqb, bq), axis=1)
    any_valid = valid.reshape(nqb, bq)[:, 0]
    all_valid = valid.reshape(nqb, bq)[:, -1]
    q0 = own0 + jnp.arange(nqb, dtype=jnp.int32) * bq
    k0 = first // bk
    last = jnp.minimum(q0 + bq - 1, ends[-1] + shift - 1)
    k3 = last // bk + 1
    k1 = jnp.minimum((last_start + bk - 1) // bk, k3)
    k2 = jnp.minimum(jnp.maximum((q0 + 1) // bk, k1), k3)
    k1 = jnp.where(all_valid, k1, k3)
    k2 = jnp.where(all_valid, k2, k3)
    bounds = jnp.where(any_valid[:, None], jnp.stack([k0, k1, k2, k3], axis=1), 0).astype(jnp.int32)
    return slot, (slot - begin).astype(f32), valid, start[None, :], bounds


def turned_rows(x, cosv, sinv, n):
    a, b = x[:n], x[n:]
    return jnp.concatenate([a * cosv - b * sinv, a * sinv + b * cosv], axis=0)


def put_queries(raw, cosv, sinv, hd, out):
    half, quarter = hd // 2, hd // 4
    scale = hd**-0.5
    width = out.shape[1]
    for h in range(raw.shape[0] // hd):
        x = raw[h * hd : (h + 1) * hd]
        y = jnp.concatenate([x[:half], turned_rows(x[half:], cosv, sinv, quarter)], axis=0).astype(bf16)
        at = h * hd
        out[at // width, at % width : at % width + hd, :] = (y.astype(f32) * scale).astype(bf16)


def pre_kernel(hd, x_ref, gain_ref, wkv_ref, wr_ref, wq_ref, cos_ref, sin_ref, fin, tied, shared, q, wkvT, wrT, wqT):
    @pl.when(pl.program_id(0) == 0)
    def _():
        wkvT[...] = wkv_ref[...].T
        wrT[...] = wr_ref[...].T
        wqT[...] = wq_ref[...].T

    x = x_ref[...].astype(f32)
    normed = x * lax.rsqrt(jnp.mean(x * x, axis=-1, keepdims=True) + eps_norm)
    f = (normed * gain_ref[...]).astype(bf16)
    fin[...] = f
    cosv, sinv = cos_ref[...], sin_ref[...]
    tied[...] = dot_nt(wkvT[...], f).astype(bf16)
    shared[...] = turned_rows(dot_nt(wrT[...], f), cosv, sinv, hd // 4).astype(bf16)
    put_queries(dot_nt(wqT[...], f), cosv, sinv, hd, q)


def pre_call(x, gain, w_kv, w_rope, w_query, cosT, sinT, hd, per, bt=256):
    rows, width = x.shape
    kv, half, qn = w_kv.shape[1], w_rope.shape[1], w_query.shape[1]
    groups = kv // hd
    full = lambda a: pl.BlockSpec(a.shape, lambda i: (0, 0), pipeline_mode=pl.Buffered(1))
    return pl.pallas_call(
        functools.partial(pre_kernel, hd),
        grid=(rows // bt,),
        in_specs=[
            pl.BlockSpec((bt, width), lambda i: (i, 0)),
            pl.BlockSpec((1, width), lambda i: (0, 0)),
            full(w_kv),
            full(w_rope),
            full(w_query),
            pl.BlockSpec((hd // 4, bt), lambda i: (0, i)),
            pl.BlockSpec((hd // 4, bt), lambda i: (0, i)),
        ],
        out_specs=[
            pl.BlockSpec((bt, width), lambda i: (i, 0)),
            pl.BlockSpec((kv, bt), lambda i: (0, i)),
            pl.BlockSpec((half, bt), lambda i: (0, i)),
            pl.BlockSpec((groups, per * hd, bt), lambda i: (0, 0, i)),
        ],
        out_shape=[
            jax.ShapeDtypeStruct((rows, width), bf16),
            jax.ShapeDtypeStruct((kv, rows), bf16),
            jax.ShapeDtypeStruct((half, rows), bf16),
            jax.ShapeDtypeStruct((groups, per * hd, rows), bf16),
        ],
        scratch_shapes=[pltpu.VMEM((kv, width), bf16), pltpu.VMEM((half, width), bf16), pltpu.VMEM((qn, width), bf16)],
        compiler_params=vmem(32),
        cost_estimate=pl.CostEstimate(flops=4 * rows * width * (qn + kv + half), bytes_accessed=8 * rows * width, transcendentals=0),
        name="first_projections",
    )(x, gain[None, :], w_kv, w_rope, w_query, cosT, sinT)


def kv_kernel(place, f_ref, mine, other, tied_a, shared, sent, w_ref):
    n = mine.shape[0]
    core = place[0]
    w_ref[pl.ds(pl.multiple_of(core * n, n), n), :] = mine[...]
    w_ref[pl.ds(pl.multiple_of((1 - core) * n, n), n), :] = other[...]
    kv = tied_a.shape[0]
    sent[:kv, :] = tied_a[...]
    sent[kv : 2 * kv, :] = dot_nt(w_ref[...].T, f_ref[...]).astype(bf16)
    sent[2 * kv :, :] = shared[...]


def kv_call(place, f, mine, other, tied_a, shared):
    kv, rows = tied_a.shape
    total = 2 * kv + shared.shape[0]
    width = f.shape[1]
    full = lambda a: pl.BlockSpec(a, lambda i, p: (0, 0))
    return pl.pallas_call(
        kv_kernel,
        grid_spec=pltpu.PrefetchScalarGridSpec(
            num_scalar_prefetch=1,
            grid=(1,),
            in_specs=[full(f.shape), full(mine.shape), full(other.shape), full(tied_a.shape), full(shared.shape)],
            out_specs=[full((total, rows)), full((width, kv))],
        ),
        out_shape=[jax.ShapeDtypeStruct((total, rows), bf16), jax.ShapeDtypeStruct((width, kv), bf16)],
        compiler_params=vmem(32),
        cost_estimate=pl.CostEstimate(flops=4 * rows * width * kv, bytes_accessed=2 * rows * width, transcendentals=0),
        name="other_keys",
    )(place, f, mine, other, tied_a, shared)


def query_kernel(hd, place, f_ref, mine, other, cos_ref, sin_ref, q, w_ref, token, wT):
    mark(token)

    @pl.when(pl.program_id(0) == 0)
    def _():
        n = mine.shape[0]
        core = place[0]
        w_ref[pl.ds(pl.multiple_of(core * n, n), n), :] = mine[...]
        w_ref[pl.ds(pl.multiple_of((1 - core) * n, n), n), :] = other[...]
        wT[...] = w_ref[...].T

    put_queries(dot_nt(wT[...], f_ref[...]), cos_ref[...], sin_ref[...], hd, q)


def query_call(place, f, mine, other, cosT, sinT, hd, groups, per, bt=256):
    rows, width = f.shape
    qn = mine.shape[1]
    full = lambda a: pl.BlockSpec(a, lambda i, p: (0, 0))
    return pl.pallas_call(
        functools.partial(query_kernel, hd),
        grid_spec=pltpu.PrefetchScalarGridSpec(
            num_scalar_prefetch=1,
            grid=(rows // bt,),
            in_specs=[
                pl.BlockSpec((bt, width), lambda i, p: (i, 0)),
                full(mine.shape),
                full(other.shape),
                pl.BlockSpec((hd // 4, bt), lambda i, p: (0, i)),
                pl.BlockSpec((hd // 4, bt), lambda i, p: (0, i)),
            ],
            out_specs=[pl.BlockSpec((groups, per * hd, bt), lambda i, p: (0, 0, i)), full((width, qn)), token_spec()],
            scratch_shapes=[pltpu.VMEM((qn, width), bf16)],
        ),
        out_shape=[jax.ShapeDtypeStruct((groups, per * hd, rows), bf16), jax.ShapeDtypeStruct((width, qn), bf16), TOKEN],
        compiler_params=vmem(32),
        cost_estimate=pl.CostEstimate(flops=4 * rows * width * qn, bytes_accessed=4 * rows * width, transcendentals=0),
        name="other_queries",
    )(place, f, mine, other, cosT, sinT)


def mlp_kernel(first, pieces, edge, deps, place, *refs):
    s_ref, c_ref = refs[:2]
    refs = refs[2:]
    if not first:
        sT, cT = refs[:2]; refs = refs[2:]
    if pieces:
        gs, us, dn, refs = refs[:2], refs[2:4], refs[4:6], refs[6:]
    else:
        wg_ref, wu_ref, wd_ref = refs[:3]; refs = refs[3:]
    refs = refs[deps:]
    hid, gg, ug, keep = refs[:4]
    sends, refs = refs[4:7], refs[7:]
    if first:
        sT, cT = refs[:2]; refs = refs[2:]
    if pieces:
        wg_ref, wu_ref, wd_ref = refs[:3]
    token = refs[-1]
    i = pl.program_id(0)
    mark(token)
    core = place[0]
    if first:
        @pl.when(i==0)
        def _():
            sT[...] = s_ref[...].T
            cT[...] = c_ref[...].T
    if pieces:
        n4 = gs[0].shape[0]
        for k in range(2):
            at = pl.multiple_of(place[1+k]*n4, n4)
            wg_ref[pl.ds(at,n4),:] = gs[k][...]
            wu_ref[pl.ds(at,n4),:] = us[k][...]
            wd_ref[:,pl.ds(at,n4)] = dn[k][...]
    rows = s_ref.shape[0]
    width = s_ref.shape[1]
    def tile(n):
        step = rows//4
        for r in range(4):
            rs = slice(r*step,(r+1)*step)
            gate = dot(s_ref[rs,:], wg_ref[:,:n]); up = dot(s_ref[rs,:], wu_ref[:,:n])
            hg = dot_nt(c_ref[rs,:], wd_ref[:n,:])
            sig = 1.0/(1.0+jnp.exp(-gate))
            act = gate*sig
            hid[rs,:n] = (act*up).astype(bf16)
            gg[rs,:n] = (hg*up*(sig+act*(1.0-sig))).astype(bf16)
            ug[rs,:n] = (hg*act).astype(bf16)
        h = hid[:,:n]; g_ = gg[:,:n]; u_ = ug[:,:n]
        hw = width//2
        lo = pl.ds(pl.multiple_of(core*hw,hw),hw)
        away = pl.ds(pl.multiple_of((1-core)*hw,hw),hw)
        for k,(left,right) in enumerate(((sT,g_),(sT,u_),(cT,h))):
            keep[k,:,:n] = dot(left[lo,:],right).astype(bf16)
            sends[k][:,:n] = dot(left[away,:],right).astype(bf16)
    bn = wg_ref.shape[1]
    if edge == bn:
        tile(bn)
    else:
        last = pl.num_programs(0)-1
        pl.when(i<last)(lambda: tile(bn))
        pl.when(i==last)(lambda: tile(edge))

def mlp_call(place, s, c, turned, weights, base, cols, bn=256, deps=()):
    rows, width = s.shape
    pieces = len(weights)==6
    first = turned is None
    tiles = -(-cols//bn)
    edge = cols-(tiles-1)*bn
    whole = pl.BlockSpec((rows,width),lambda i,p:(0,0),pipeline_mode=pl.Buffered(1))
    wholeT = pl.BlockSpec((width,rows),lambda i,p:(0,0),pipeline_mode=pl.Buffered(1))
    wholeTo = pl.BlockSpec((width,rows),lambda i,p:(0,0))
    in_specs=[whole,whole]+([] if first else [wholeT,wholeT])
    if pieces:
        n4 = weights[0].shape[0]
        in_specs += [pl.BlockSpec((n4,bn),lambda i,p:(0,base+i))]*4 + [pl.BlockSpec((bn,n4),lambda i,p:(base+i,0))]*2
    else:
        in_specs += [pl.BlockSpec((width,bn),lambda i,p:(0,base+i))]*2 + [pl.BlockSpec((bn,width),lambda i,p:(base+i,0))]
    in_specs += [ANY]*len(deps)
    act = pl.BlockSpec((rows,bn),lambda i,p:(0,i))
    part = pl.BlockSpec((3,width//2,bn),lambda i,p:(0,0,i))
    one = pl.BlockSpec((width//2,bn),lambda i,p:(0,i))
    ones = jax.ShapeDtypeStruct((width//2,cols),bf16)
    acts = jax.ShapeDtypeStruct((rows,cols),bf16)
    parts = jax.ShapeDtypeStruct((3,width//2,cols),bf16)
    tsh = jax.ShapeDtypeStruct((width,rows),bf16)
    w_specs = [pl.BlockSpec((width,bn),lambda i,p:(0,i))]*2+[pl.BlockSpec((bn,width),lambda i,p:(i,0))] if pieces else []
    w_shapes = [jax.ShapeDtypeStruct((width,cols),bf16)]*2+[jax.ShapeDtypeStruct((cols,width),bf16)] if pieces else []
    out = pl.pallas_call(
        functools.partial(mlp_kernel,first,pieces,edge,len(deps)),
        grid_spec=pltpu.PrefetchScalarGridSpec(
            num_scalar_prefetch=1, grid=(tiles,), in_specs=in_specs,
            out_specs=[act]*3+[part]+[one]*3+([wholeTo]*2 if first else [])+w_specs+[token_spec()],
        ),
        out_shape=[acts]*3+[parts]+[ones]*3+([tsh]*2 if first else [])+w_shapes+[TOKEN],
        compiler_params=pltpu.CompilerParams(vmem_limit_bytes=56<<20),
        cost_estimate=pl.CostEstimate(flops=22*rows*width*cols,bytes_accessed=2*(4*rows*width+9*width*cols),transcendentals=rows*cols),
        name="mlp_grads",
    )(place, s, c, *(() if first else turned), *weights, *deps)
    return out


def fold_kernel(counts, sides, deps, bits, *refs):
    n = sum(counts)
    outs, token = refs[n * sides + deps : -1], refs[-1]
    mark(token)
    for side, out in enumerate(outs):
        at, col = side * n, 0
        for count in counts:
            total = None
            for ref in refs[at : at + count]:
                part = ref[0].astype(f32)
                total = part if total is None else total + part
            width = total.shape[1]
            out[:, col : col + width] = total.astype(out.dtype)
            at, col = at + count, col + width


def fold(groups, bit=None, deps=()):
    groups = [[a if isinstance(a, tuple) else (a[None], 0) for a in g] for g in groups]
    flat = [a for g in groups for a in g]
    rows = flat[0][0].shape[1]
    cols = sum(g[0][0].shape[2] for g in groups)
    sides = 1 if bit is None else 2
    rows_out = rows // sides
    step = rows_out
    while step % 32 == 0 and step * cols > 128 * 1408:
        step //= 2
    blocks = rows_out // step

    def spec(a, k, side):
        shape = (1, step, a.shape[2])
        if sides == 1:
            return pl.BlockSpec(shape, lambda i, b: (k, i, 0))
        if side == 0:
            return pl.BlockSpec(shape, lambda i, b: (k, b[0] * blocks + i, 0))
        return pl.BlockSpec(shape, lambda i, b: (k, (1 - b[0]) * blocks + i, 0))

    out = jax.ShapeDtypeStruct((rows_out, cols), bf16)
    scalars = jnp.reshape(jnp.int32(0) if bit is None else bit, (1,)).astype(jnp.int32)
    result = pl.pallas_call(
        functools.partial(fold_kernel, [len(g) for g in groups], sides, len(deps)),
        grid_spec=pltpu.PrefetchScalarGridSpec(
            num_scalar_prefetch=1,
            grid=(blocks,),
            in_specs=[spec(a, k, side) for side in range(sides) for a, k in flat] + [ANY] * len(deps),
            out_specs=[pl.BlockSpec((step, cols), lambda i, b: (i, 0))] * sides + [token_spec()],
        ),
        out_shape=[out] * sides + [TOKEN],
        compiler_params=vmem(32),
        cost_estimate=pl.CostEstimate(
            flops=3 * rows * cols, bytes_accessed=8 * rows * cols, transcendentals=0
        ),
        name="fold",
    )(scalars, *[a for _ in range(sides) for a, _ in flat], *deps)
    return result


def take_kernel(deps, place, *refs):
    refs[-2][...] = refs[0][...]
    mark(refs[-1])


def take(w, at, axis, parts, deps=()):
    shape = list(w.shape)
    shape[axis] //= parts
    block = tuple(shape)
    where = (lambda i, p: (p[0], 0)) if axis == 0 else (lambda i, p: (0, p[0]))
    return pl.pallas_call(
        functools.partial(take_kernel, len(deps)),
        grid_spec=pltpu.PrefetchScalarGridSpec(
            num_scalar_prefetch=1,
            grid=(1,),
            in_specs=[pl.BlockSpec(block, where)] + [pl.BlockSpec(memory_space=pl.ANY)] * len(deps),
            out_specs=[pl.BlockSpec(block, lambda i, p: (0, 0)), token_spec()],
        ),
        out_shape=[jax.ShapeDtypeStruct(block, w.dtype), TOKEN],
        compiler_params=vmem(32),
        cost_estimate=pl.CostEstimate(flops=0, bytes_accessed=4 * block[0] * block[1], transcendentals=0),
        name="take",
    )(jnp.reshape(at, (1,)).astype(jnp.int32), w, *deps)


def hold(x, dep):
    return pl.pallas_call(
        lambda a, b, c: None,
        in_specs=[ANY, ANY],
        out_specs=ANY,
        out_shape=jax.ShapeDtypeStruct(x.shape, x.dtype),
        input_output_aliases={0: 0},
        name="hold",
    )(x, dep)


def gather_kernel(turn, n, order, *refs):
    out, token = refs[-2:]
    mark(token)
    rows = refs[0].shape[0]
    for k in range(0, n, 2):

        @pl.when(pl.program_id(0) == k // 2)
        def _():
            for j in (k, k + 1):
                at = pl.ds(pl.multiple_of(order[j] % 2 * rows, rows), rows)
                if turn:
                    out[:, at] = refs[j][...].T.astype(f32)
                else:
                    out[at, :] = refs[j][...].astype(f32)


def gathered(pieces, order, turn, deps=()):
    n = len(pieces)
    rows, cols = pieces[0].shape
    total = n * rows
    two = 2 * rows
    return pl.pallas_call(
        functools.partial(gather_kernel, turn, n),
        grid_spec=pltpu.PrefetchScalarGridSpec(
            num_scalar_prefetch=1,
            grid=(n // 2,),
            in_specs=[pl.BlockSpec((rows, cols), lambda i, o: (0, 0), pipeline_mode=pl.Buffered(1))] * n
            + [ANY] * len(deps),
            out_specs=[
                pl.BlockSpec((cols, two), lambda i, o: (0, o[2 * i] // 2))
                if turn
                else pl.BlockSpec((two, cols), lambda i, o: (o[2 * i] // 2, 0)),
                token_spec(),
            ],
        ),
        out_shape=[jax.ShapeDtypeStruct((cols, total) if turn else (total, cols), f32), TOKEN],
        compiler_params=vmem(60),
        cost_estimate=pl.CostEstimate(flops=0, bytes_accessed=6 * total * cols, transcendentals=0),
        name="gathered",
    )(order, *pieces, *deps)


def gather_tiles_kernel(turn, n, order, *refs):
    out = refs[-1] if not turn else refs[-2]
    held = refs[-1]
    rows = refs[0].shape[0]
    for k in range(n):
        at = pl.ds(pl.multiple_of(order[k] * rows, rows), rows)
        held[at, :] = refs[k][...].astype(held.dtype)
    if turn:
        out[...] = held[...].T.astype(f32)


def gathered_tiles(pieces, order, turn, deps, start, cols, wide=256):
    n = len(pieces)
    rows = pieces[0].shape[0]
    base = start // wide
    total = n * rows
    return pl.pallas_call(
        functools.partial(gather_tiles_kernel, turn, n),
        grid_spec=pltpu.PrefetchScalarGridSpec(
            num_scalar_prefetch=1,
            grid=(cols // wide,),
            in_specs=[pl.BlockSpec((rows, wide), lambda i, o: (0, base + i))] * n + [ANY] * len(deps),
            out_specs=pl.BlockSpec((wide, total), lambda i, o: (i, 0))
            if turn
            else pl.BlockSpec((total, wide), lambda i, o: (0, i)),
            scratch_shapes=[pltpu.VMEM((total, wide), bf16)] if turn else [],
        ),
        out_shape=jax.ShapeDtypeStruct((cols, total) if turn else (total, cols), f32),
        compiler_params=vmem(32),
        cost_estimate=pl.CostEstimate(flops=0, bytes_accessed=6 * total * cols, transcendentals=0),
        name="gathered",
    )(order, *pieces, *deps)


def gather_small_kernel(n, kn, half, deps, order, *refs):
    pieces, refs = refs[:n], refs[n + deps :]
    kv, rope, gains, held = refs
    rows = pieces[0].shape[0]
    for k, piece in enumerate(pieces):
        at = pl.ds(pl.multiple_of(order[k] * rows, rows), rows)
        kv[at, :] = piece[:, :kn].astype(f32)
        held[at, :] = piece[:, kn:].astype(f32)
    rope[...] = held[:, :half]
    gains[...] = held[...].T[half : half + 8, :]


def gathered_small(pieces, order, kn, half, deps=(), start=0):
    n = len(pieces)
    rows, cols = pieces[0].shape[0], kn + 128
    base = start // cols
    total = n * rows
    full = lambda a: pl.BlockSpec(a, lambda i, o: (0, 0))
    shapes = [(total, kn), (total, half), (8, total)]
    return pl.pallas_call(
        functools.partial(gather_small_kernel, n, kn, half, len(deps)),
        grid_spec=pltpu.PrefetchScalarGridSpec(
            num_scalar_prefetch=1,
            grid=(1,),
            in_specs=[pl.BlockSpec((rows, cols), lambda i, o: (0, base))] * n + [ANY] * len(deps),
            out_specs=[full(a) for a in shapes],
            scratch_shapes=[pltpu.VMEM((total, 128), f32)],
        ),
        out_shape=[jax.ShapeDtypeStruct(a, f32) for a in shapes],
        compiler_params=vmem(32),
        cost_estimate=pl.CostEstimate(flops=0, bytes_accessed=6 * total * cols, transcendentals=0),
        name="gathered_small",
    )(order, *pieces, *deps)


def wgrad_kernel(n, deps, place, l_ref, *refs):
    right, refs = refs[:n], refs[n + deps :]
    keep, send, token, lT = refs
    mark(token)
    lT[...] = l_ref[...].T
    core = place[0]
    hw = keep.shape[0]
    for out, side in ((send, 1 - core), (keep, core)):
        rows = lT[pl.ds(pl.multiple_of(side * hw, hw), hw), :]
        at = 0
        for r in right:
            k = r.shape[-2]
            out[:, at : at + k] = dot_nt(rows, r[...].reshape(r.shape[-2:])).astype(bf16)
            at += k


def wgrad(place, left, right, deps=()):
    rows, width = left.shape
    right = [r if isinstance(r, tuple) else (r[None], 0) for r in right]
    cols = sum(r.shape[1] for r, _ in right)
    full = lambda a: pl.BlockSpec(a, lambda i, p: (0, 0))
    part = jax.ShapeDtypeStruct((width // 2, cols), bf16)

    def spec(r, k):
        return pl.BlockSpec((1, *r.shape[1:]), lambda i, p: (k, 0, 0))

    return pl.pallas_call(
        functools.partial(wgrad_kernel, len(right), len(deps)),
        grid_spec=pltpu.PrefetchScalarGridSpec(
            num_scalar_prefetch=1,
            grid=(1,),
            in_specs=[full(left.shape)] + [spec(r, k) for r, k in right] + [ANY] * len(deps),
            out_specs=[full(part.shape)] * 2 + [token_spec()],
            scratch_shapes=[pltpu.VMEM((width, rows), bf16)],
        ),
        out_shape=[part] * 2 + [TOKEN],
        compiler_params=vmem(48),
        cost_estimate=pl.CostEstimate(flops=4 * rows * width * cols, bytes_accessed=4 * rows * width, transcendentals=0),
        name="weight_grads",
    )(place, left, *[r for r, _ in right], *deps)


def back_kernel(n, *refs):
    tgs, sgs = refs[:n], refs[n : 2 * n]
    out, token = refs[-2:]
    mark(token)
    per, hd, _ = tgs[0].shape
    for g in range(n * per):
        out[g * hd : (g + 1) * hd, :] = tgs[g // per][g % per].astype(bf16)
    total = sgs[0][...]
    for s in sgs[1:]:
        total = total + s[...]
    out[n * per * hd :, :] = total.astype(bf16)


def back_call(tgs, sgs, deps=()):
    n = len(tgs)
    per, hd, two = tgs[0].shape
    rows = two // 2
    total = n * per * hd + hd // 2
    return pl.pallas_call(
        functools.partial(back_kernel, n),
        grid=(1,),
        in_specs=[pl.BlockSpec((per, hd, rows), lambda i: (0, 0, 0))] * n
        + [pl.BlockSpec((hd // 2, rows), lambda i: (0, 0))] * n
        + [ANY] * len(deps),
        out_specs=[pl.BlockSpec((total, rows), lambda i: (0, 0)), token_spec()],
        out_shape=[jax.ShapeDtypeStruct((total, rows), bf16), TOKEN],
        compiler_params=vmem(32),
        cost_estimate=pl.CostEstimate(flops=0, bytes_accessed=6 * total * rows, transcendentals=0),
        name="partner_key_grads",
    )(*tgs, *sgs, *deps)


def own_kernel(n, *refs):
    tgs, sgs = refs[: 2 * n], refs[2 * n : 4 * n]
    back_a, back_b, cos_ref, sin_ref = refs[4 * n : 4 * n + 4]
    out, token = refs[-2:]
    mark(token)
    per, hd, _ = tgs[0].shape
    kv = n * per * hd
    for k in range(2 * n * per):
        back = (back_a, back_b)[k // (n * per)]
        at = k % (n * per) * hd
        mine = tgs[k // per][k % per]
        out[k * hd : (k + 1) * hd, :] = (mine + back[at : at + hd, :].astype(f32)).astype(bf16)
    total = back_a[kv:, :].astype(f32) + back_b[kv:, :].astype(f32)
    for s in sgs:
        total = total + s[...]
    out[2 * kv :, :] = turned_rows(total, cos_ref[...], -sin_ref[...], hd // 4).astype(bf16)


def own_call(tgs, sgs, backs, cosT, sinT, deps=()):
    n = len(tgs)
    per, hd, two = tgs[0].shape
    rows = two // 2
    total = n * per * hd + hd // 2
    full = lambda a: pl.BlockSpec(a.shape, lambda i: (0, 0))
    return pl.pallas_call(
        functools.partial(own_kernel, n // 2),
        grid=(1,),
        in_specs=[pl.BlockSpec((per, hd, rows), lambda i: (0, 0, 1))] * n
        + [pl.BlockSpec((hd // 2, rows), lambda i: (0, 1))] * n
        + [full(backs[0]), full(backs[1]), full(cosT), full(sinT)]
        + [ANY] * len(deps),
        out_specs=[pl.BlockSpec((total, rows), lambda i: (0, 0)), token_spec()],
        out_shape=[jax.ShapeDtypeStruct((total, rows), bf16), TOKEN],
        compiler_params=vmem(32),
        cost_estimate=pl.CostEstimate(flops=0, bytes_accessed=8 * total * rows, transcendentals=0),
        name="own_key_grads",
    )(*tgs, *sgs, *backs, cosT, sinT, *deps)


def post_kernel(deps, x_ref, mg_ref, gain_ref, kv_ref, wqa, wqb, wka, wkb, wr, *refs):
    dqs = refs[:2]
    out, gain_out = refs[2 + deps :]
    kn = wka.shape[1]
    hn = wqa.shape[1]
    qa = dqs[0][...].reshape(hn, -1).T
    qb = dqs[1][...].reshape(hn, -1).T
    kv = kv_ref[...]
    first = dot_nt(qa, wqa[...]) + dot_nt(qb, wqb[...])
    first = first + dot_nt(kv[:kn].T, wka[...]) + dot_nt(kv[kn : 2 * kn].T, wkb[...])
    first = first + dot_nt(kv[2 * kn :].T, wr[...])
    x = x_ref[...].astype(f32)
    factor = lax.rsqrt(jnp.mean(x * x, axis=-1, keepdims=True) + eps_norm)
    normed = x * factor
    inner = first * gain_ref[...]
    back = factor * (inner - normed * jnp.mean(inner * normed, axis=-1, keepdims=True))
    out[...] = (mg_ref[...] + back).astype(bf16)

    @pl.when(pl.program_id(0) == 0)
    def _():
        gain_out[...] = jnp.zeros_like(gain_out)

    gain_out[...] += jnp.sum(first * normed, axis=0, keepdims=True)


def post_call(x, middle_grad, gain, kv, weights, dqs, deps=(), bt=256):
    rows, width = x.shape
    full = lambda a: pl.BlockSpec(a.shape, lambda i: (0, 0), pipeline_mode=pl.Buffered(1))
    row = pl.BlockSpec((bt, width), lambda i: (i, 0))
    one = pl.BlockSpec((1, width), lambda i: (0, 0))
    return pl.pallas_call(
        functools.partial(post_kernel, len(deps)),
        grid=(rows // bt,),
        in_specs=[row, row, one, pl.BlockSpec((kv.shape[0], bt), lambda i: (0, i))]
        + [full(w) for w in weights]
        + [pl.BlockSpec((*d.shape[:2], bt), lambda i: (0, 0, i)) for d in dqs]
        + [ANY] * len(deps),
        out_specs=[row, one],
        out_shape=[jax.ShapeDtypeStruct((rows, width), bf16), jax.ShapeDtypeStruct((1, width), f32)],
        compiler_params=vmem(40),
        cost_estimate=pl.CostEstimate(flops=5 * rows * width * width, bytes_accessed=16 * rows * width, transcendentals=0),
        name="token_grads",
    )(x, middle_grad, gain[None, :], kv, *weights, *dqs, *deps)


def small_kernel(kn, half, place, f_ref, kv_ref, gain_a, gain_b, keep_a, send_a, keep_b, send_b, token, lT, rows_s, rows_g):
    mark(token)
    lT[...] = f_ref[...].T
    rows_s[...] = jnp.zeros_like(rows_s)
    rows_s[:half, :] = kv_ref[2 * kn :, :]
    rows_g[...] = jnp.zeros_like(rows_g)
    rows_g[half : half + 1, :] = gain_a[...]
    rows_g[half + 1 : half + 2, :] = gain_b[...]
    gains = rows_g[...].T
    rows_g_ref = rows_g
    core = place[0]
    hw = keep_a.shape[0]
    rope = dot_nt(lT[...], rows_s[...]) + gains
    lT_rows = [lT[:hw, :], lT[hw:, :]]
    first = core == 0
    for (a, b), side in (((send_a, send_b), 1), ((keep_a, keep_b), 0)):
        low = jnp.logical_xor(first, side == 1)
        rows = jnp.where(low, lT_rows[0], lT_rows[1])
        small = jnp.where(low, rope[:hw], rope[hw:]).astype(bf16)
        a[:, :kn] = dot_nt(rows, kv_ref[:kn, :]).astype(bf16)
        a[:, kn:] = small
        b[:, :kn] = dot_nt(rows, kv_ref[kn : 2 * kn, :]).astype(bf16)
        b[:, kn:] = small


def small_call(place, f, kv, gain_a, gain_b, kn, half):
    rows, width = f.shape
    full = lambda a: pl.BlockSpec(a, lambda i, p: (0, 0))
    part = jax.ShapeDtypeStruct((width // 2, kn + 128), bf16)
    return pl.pallas_call(
        functools.partial(small_kernel, kn, half),
        grid_spec=pltpu.PrefetchScalarGridSpec(
            num_scalar_prefetch=1,
            grid=(1,),
            in_specs=[full(f.shape), full(kv.shape), full((1, width)), full((1, width))],
            out_specs=[full(part.shape)] * 4 + [token_spec()],
            scratch_shapes=[pltpu.VMEM((width, rows), bf16), pltpu.VMEM((128, rows), bf16), pltpu.VMEM((128, width), f32)],
        ),
        out_shape=[part] * 4 + [TOKEN],
        compiler_params=vmem(48),
        cost_estimate=pl.CostEstimate(flops=2 * rows * width * 512, bytes_accessed=3 * rows * width, transcendentals=0),
        name="small_grads",
    )(place, f, kv, gain_a, gain_b)


def rms_parts(values):
    factor = lax.rsqrt(jnp.mean(values * values, axis=-1, keepdims=True) + eps_norm)
    return values * factor, factor


def norm_back(grad, normed, factor, gain):
    inner = grad * gain
    return factor * (inner - normed * jnp.mean(inner * normed, axis=-1, keepdims=True))


def mm(a, b, ca, cb):
    return lax.dot_general(a, b, (((ca,), (cb,)), ((), ())), preferred_element_type=f32)


def swap(x, axis, bit):
    n = lax.axis_size(axis)
    return lax.ppermute(x, axis, [(i, i ^ bit) for i in range(n)])


def joined(mine, other, bit):
    first = bit == 0
    return jnp.concatenate([jnp.where(first, mine, other), jnp.where(first, other, mine)], axis=0)


class Order:
    def __init__(self, first):
        self.last = first

    def after(self, out):
        *out, self.last = out
        return out if len(out) > 1 else out[0]

    def fold(self, groups, bit=None, deps=()):
        return self.after(fold(groups, bit, (self.last, *deps)))


def spread(piece, steps):
    pieces = [piece]
    for step in steps:
        pieces = pieces + [swap(p, "dp", step) for p in pieces]
    return pieces


def piece_order(bits):
    order = [jnp.int32(0)]
    for bit in bits:
        order = [2 * o + b for o in order for b in (bit, 1 - bit)]
    return jnp.stack(order).astype(jnp.int32)


class Sum:
    def __init__(self, run, bits):
        self.run, self.bits, self.steps = run, bits, [1]

    def x(self, groups):
        self.keep, send = self.run.fold(groups, self.bits[1])
        self.got = swap(send, "dp", 2)
        self.steps = [2, 1]

    def z(self):
        self.start([[self.keep, self.got]])

    def start(self, groups):
        self.keep, send = self.run.fold(groups, self.bits[2])
        self.got = swap(send, "dp", 4)
        self.steps = [4, 2, 1]

    def line(self, step=8):
        self.keep = self.run.fold([[self.keep, self.got]])
        self.got = swap(self.keep, "dp", step)

    def end(self, deps=()):
        step = 16
        while step < lax.axis_size("dp"):
            self.line(step)
            step *= 2
        self.keep = self.run.fold([[self.keep, self.got]], None, deps)
        self.pieces = spread(self.keep, self.steps)
        self.order = piece_order(self.bits[: len(self.steps)])


def body(tokens, lengths, attn_gain, w_query, w_kv, w_rope, w_out, mlp_gain, w_gate, w_up, w_down, out_grad):
    rows, width = tokens.shape
    shards = lax.axis_size("tensor")
    t = lax.axis_index("tensor")
    index = lax.axis_index("dp")
    bits = (index & 1, (index >> 1) & 1, (index >> 2) & 1)
    core = bits[0]
    half = w_rope.shape[1]
    hd = 2 * half
    kv_own = w_kv.shape[1]
    q_own = w_query.shape[1]
    groups = kv_own // hd
    per = q_own // kv_own
    ff = w_gate.shape[1]
    own0 = rows
    bq_f, bk_f, bq_b, bk_b = 256, 256, 512, 256
    place = jnp.stack([core, core, 1 - core]).astype(jnp.int32)

    kv_piece, taken = take(w_kv, core, 0, 2)
    kv_got = swap(kv_piece, "tensor", 1)
    q_piece, taken = take(w_query, core, 0, 2, (taken,))
    q_got = swap(q_piece, "tensor", 1)
    out_piece, taken = take(w_out, core, 0, 2, (taken,))
    out_got = swap(out_piece, "tensor", 1)

    slot, position, valid, start, bounds_f = local_layout(lengths[0], t, rows, bq_f, bk_f, own0)
    bounds_b = local_layout(lengths[0], t, rows, bq_b, bk_b, own0)[4]
    quarter = half // 2
    freq = 10000.0 ** (-jnp.arange(quarter, dtype=f32) / quarter)
    angle = freq[:, None] * position[None, :]
    cosT, sinT = jnp.cos(angle), jnp.sin(angle)

    first_in, tied_a, shared, q_a = pre_call(tokens, attn_gain, w_kv, w_rope, w_query, cosT, sinT, hd, per)
    sent, w_kv_o = kv_call(place, first_in, kv_got, swap(kv_got, "dp", 1), tied_a, shared)
    got = lax.ppermute(sent, "tensor", [(i, i + 1) for i in range(shards - 1)])
    q_b, w_query_o, q_done = query_call(place, first_in, q_got, swap(q_got, "dp", 1), cosT, sinT, hd, groups, per)
    gate_piece, taken = take(w_gate, core, 0, 2, (q_done,))
    gate_got = swap(hold(gate_piece, got), "tensor", 1)
    up_piece, taken = take(w_up, core, 0, 2, (taken,))
    up_got = swap(hold(up_piece, got), "tensor", 1)
    down_piece, taken = take(w_down, core, 1, 2, (taken,))
    down_got = swap(hold(down_piece, got), "tensor", 1)

    def both(p):
        return p, swap(p, "dp", 1)

    w_out_o = joined(out_got, swap(out_got, "dp", 1), core)
    mixed_a, mixed_b, lse_a, lse_b = attn_fwd(
        bounds_f, start, q_a, q_b, sent, got, hd, bq_f, bk_f, (taken, w_out_o)
    )
    mix_a, mix_b = mixed_a.reshape(-1, rows), mixed_b.reshape(-1, rows)
    inputs = tokens.astype(f32)
    middle = inputs + mm(mix_a, w_out, 0, 0) + mm(mix_b, w_out_o, 0, 0)
    normed_two, factor_two = rms_parts(middle)
    second_in = (normed_two * mlp_gain).astype(bf16)

    hid_a, gg_a, ug_a, keep_a, *send_a, in_T, back_T, done_a = mlp_call(
        place, second_in, out_grad, None, (w_gate, w_up, w_down), 0, ff
    )
    core_a = [swap(s, "dp", 1) for s in send_a]
    gates, ups, downs = both(hold(gate_got, done_a)), both(hold(up_got, done_a)), both(hold(down_got, done_a))
    second_a = mm(gg_a, w_gate, 1, 1) + mm(ug_a, w_up, 1, 1)
    hid_b, gg_b, ug_b, keep_b, *send_b, w_gate_o, w_up_o, w_down_o, done_b = mlp_call(
        place, second_in, out_grad, (in_T, back_T), (*gates, *ups, *downs), 0, ff, deps=(second_a,)
    )
    core_b = [swap(s, "dp", 1) for s in send_b]
    run = Order(done_b)
    gate_y = swap(run.fold([[(keep_b, 0), core_b[0]]]), "tensor", 1)
    gg_b, ug_b = hold(gg_b, run.last), hold(ug_b, run.last)
    second_grad = second_a + mm(gg_b, w_gate_o, 1, 1) + mm(ug_b, w_up_o, 1, 1)
    mlp_gain_part = jnp.sum(second_grad * normed_two, axis=0, keepdims=True)
    middle_grad = out_grad.astype(f32) + norm_back(second_grad, normed_two, factor_two, mlp_gain)
    attn_back = middle_grad.astype(bf16)
    live = valid[None, :].astype(bf16)
    mixed_grad_b = (mm(w_out_o, attn_back, 1, 1).astype(bf16) * live).reshape(mixed_b.shape)
    mixed_grad_a = (mm(w_out, attn_back, 1, 1).astype(bf16) * live).reshape(mixed_a.shape)

    def parts(x):
        return [(x, k) for k in range(groups)]

    def back(q, mixed, lse, grad, side, deps=()):
        return run.after(
            attn_bwd(
                bounds_b, start, q, sent, got, mixed, lse, grad, cosT, sinT, hd, side, 0, groups, bq_b, bk_b,
                (run.last, *deps),
            )
        )

    wo_keep_b, wo_send_b = run.after(wgrad(place, attn_back, parts(mixed_b), (run.last,)))
    wo_core_b = swap(wo_send_b, "dp", 1)
    up_y = swap(run.fold([[(keep_b, 1), core_b[1]]]), "tensor", 1)
    down_kb, down_sb = run.fold([[(keep_b, 2), core_b[2]]], bits[1])
    down_xb = swap(down_sb, "dp", 2)
    down_ka, down_sa = run.fold([[(keep_a, 2), core_a[2]]], bits[1])
    down_xa = swap(down_sa, "dp", 2)
    gate_s, up_s, down_s, rest_s = (Sum(run, bits) for _ in range(4))
    dq_b, tg_b, sg_b = back(q_b, mixed_b, lse_b, mixed_grad_b, 1, (mixed_grad_a,))
    wq_keep_b, wq_send_b = run.after(wgrad(place, first_in, parts(dq_b), (run.last,)))
    wq_core_b = swap(wq_send_b, "dp", 1)
    key_b = run.after(back_call((tg_b,), (sg_b,), (run.last,)))
    to_lower = [(i + 1, i) for i in range(shards - 1)]
    key_got_a = lax.ppermute(key_b, "tensor", to_lower)
    gate_s.x([[(keep_a, 0), core_a[0], gate_y]])
    up_s.x([[(keep_a, 1), core_a[1], up_y]])
    down_y = swap(run.fold([[down_kb, down_xb]]), "tensor", 1)
    wo_y = swap(run.fold([[wo_keep_b, wo_core_b]]), "tensor", 1)
    wq_y = swap(run.fold([[wq_keep_b, wq_core_b]]), "tensor", 1)
    dq_a, tg_a, sg_a = back(q_a, mixed_a, lse_a, mixed_grad_a, 0)
    key_a = run.after(back_call((tg_a,), (sg_a,), (run.last,)))
    key_got_b = lax.ppermute(key_a, "tensor", to_lower)
    gate_s.z()
    up_s.z()
    down_s.start([[down_ka, down_xa, down_y]])
    wq_keep_a, wq_send_a = run.after(wgrad(place, first_in, parts(dq_a), (run.last,)))
    wq_core_a = swap(wq_send_a, "dp", 1)
    kv_grad = run.after(own_call((tg_a, tg_b), (sg_a, sg_b), (key_got_a, key_got_b), cosT, sinT, (run.last,)))
    tokens_grad, attn_gain_part = post_call(
        tokens, middle_grad, attn_gain, kv_grad, (w_query, w_query_o, w_kv, w_kv_o, w_rope), (dq_a, dq_b), (run.last,)
    )
    run.last = attn_gain_part
    sm_keep_a, sm_send_a, sm_keep_b, sm_send_b = run.after(
        small_call(place, first_in, kv_grad, attn_gain_part, mlp_gain_part, kv_own, half)
    )
    sm_core_b = swap(sm_send_b, "dp", 1)
    sm_core_a = swap(sm_send_a, "dp", 1)
    wo_keep_a, wo_send_a = run.after(wgrad(place, attn_back, parts(mixed_a), (run.last,)))
    wo_core_a = swap(wo_send_a, "dp", 1)
    gate_s.line()
    sm_y = swap(run.fold([[sm_keep_b, sm_core_b]]), "tensor", 1)
    up_s.line()
    rest_s.x([[wo_keep_a, wo_core_a, wo_y], [wq_keep_a, wq_core_a, wq_y], [sm_keep_a, sm_core_a, sm_y]])
    hid_a, hid_b = hold(hid_a, run.last), hold(hid_b, run.last)
    layer_out = (middle + mm(hid_a, w_down, 1, 0) + mm(hid_b, w_down_o, 1, 0)).astype(bf16)

    gate_s.end((layer_out,))
    rest_s.z()
    up_s.end()
    down_s.line()
    rest_s.line()
    gate_sum = run.after(gathered(gate_s.pieces, gate_s.order, False, (run.last,)))
    down_s.end()
    rest_s.end()
    up_sum = run.after(gathered(up_s.pieces, up_s.order, False, (run.last,)))
    down_sum = run.after(gathered(down_s.pieces, down_s.order, True, (run.last,)))
    kv_sum, rope_sum, gains = gathered_small(rest_s.pieces, rest_s.order, kv_own, half, (run.last,), 2 * q_own)
    out_sum = gathered_tiles(rest_s.pieces, rest_s.order, True, (run.last,), 0, q_own)
    query_sum = gathered_tiles(rest_s.pieces, rest_s.order, False, (run.last,), q_own, q_own)
    return (
        layer_out,
        tokens_grad,
        gains[0],
        query_sum,
        kv_sum,
        rope_sum,
        out_sum,
        gains[1],
        gate_sum,
        up_sum,
        down_sum,
    )


def solution(mesh):
    rows = P(("dp", "tensor"), None)
    columns = P(None, "tensor")
    down = P("tensor", None)
    return jax.shard_map(
        body,
        mesh=mesh,
        in_specs=(rows, P("dp", None), P(), columns, columns, P(), down, P(), columns, columns, down, rows),
        out_specs=(rows, rows, P(), columns, columns, P(), down, P(), columns, columns, down),
        check_vma=False,
    )
```
